32 devices in a mesh: dp: 16 (over z, x, core), seq: 2 (over y).
Axes of the slice: x: 2, y: 2, z: 4, core: 2. Of those that a mesh axis runs over, the one named last changes fastest.
Arguments:
- inputs: bfloat16 [64, 512, 768], P('dp', 'seq'), may hold values from -6 to 6
- cotangent: bfloat16 [64, 512, 768], P('dp', 'seq'), may hold values from -6 to 6
- w_query: bfloat16 [768, 768], replicated, may hold values from -0.21875 to 0.21875
- b_query: bfloat16 [768], replicated, may hold values from -3 to 3
- w_key: bfloat16 [768, 768], replicated, may hold values from -0.21875 to 0.21875
- w_value: bfloat16 [768, 768], replicated, may hold values from -0.21875 to 0.21875
- b_value: bfloat16 [768], replicated, may hold values from -3 to 3
- w_out: bfloat16 [768, 768], replicated, may hold values from -0.875 to 0.875
- b_out: bfloat16 [768], replicated, may hold values from -3 to 3
- gain_one: bfloat16 [768], replicated, may hold values from 0.5 to 1.5
- shift_one: bfloat16 [768], replicated, may hold values from -3 to 3
- w_up: bfloat16 [768, 3072], replicated, may hold values from -0.21875 to 0.21875
- b_up: bfloat16 [3072], replicated, may hold values from -3 to 3
- w_down: bfloat16 [3072, 768], replicated, may hold values from -0.109375 to 0.109375
- b_down: bfloat16 [768], replicated, may hold values from -3 to 3
- gain_two: bfloat16 [768], replicated, may hold values from 0.5 to 1.5
- shift_two: bfloat16 [768], replicated, may hold values from -3 to 3
- live_counts: int32 [16], P('dp'), may hold values from 1 to 4, as said below
- valid_mask: int32 [64, 512], P('dp', 'seq'), may hold values from 0 to 1, as said below
- segments: int32 [64, 512], P('dp', 'seq'), may hold values from 0 to 8, as said below
Outputs:
- result_out: bfloat16 [64, 512, 768], P('dp', 'seq')
- grad_inputs: float32 [64, 512, 768], P('dp', 'seq')
- grad_w_query: float32 [768, 768], replicated
- grad_b_query: float32 [768], replicated
- grad_w_key: float32 [768, 768], replicated
- grad_w_value: float32 [768, 768], replicated
- grad_b_value: float32 [768], replicated
- grad_w_out: float32 [768, 768], replicated
- grad_b_out: float32 [768], replicated
- grad_gain_one: float32 [768], replicated
- grad_shift_one: float32 [768], replicated
- grad_w_up: float32 [768, 3072], replicated
- grad_b_up: float32 [3072], replicated
- grad_w_down: float32 [3072, 768], replicated
- grad_b_down: float32 [768], replicated
- grad_gain_two: float32 [768], replicated
- grad_shift_two: float32 [768], replicated
- rms_values: float32 [4], replicated
The draws below stay inside these ranges and needn't reach their ends.
Inputs may be any that keep to these rules, and one draw needn't show every extreme that they name: `live_counts`: the live micro-batches of a data group are the first of its 4 sequences; in every draw some data group has all 4 live. `valid_mask`: padding lies only at the end of a sequence; in each data group one live sequence, drawn from the seed, has no padding and a single segment. `segments`: segment numbers never fall along a sequence and start at 0; every sequence other than the single-segment ones reaches the largest number.
All inputs are finite; a program needn't handle non-finite values.
Results may differ from the reference program's by a relative error of at most 0.019.
Values may be sent and summed in bfloat16 or wider, within the bound.
No kernel may reach another device: no remote copies, remote signals or barrier semaphores. Data moves between devices by JAX's collectives and lax.ppermute only.
A program may use at most 256 MiB of HBM per device.

```python
import jax
import jax.numpy as jnp
from jax import lax

D = 768
HEADS = 12
HEAD_DIM = 64
FF = 3072
LEN = 512
SEQS_G = 4
SEQS = 64


def packing(key):
    key_count, key_full, key_slot, key_bound, key_pad = jax.random.split(key, 5)
    group_count = SEQS // SEQS_G
    half_most = max(SEQS_G // 2, 1)
    counts = jax.random.randint(key_count, (group_count,), 1, half_most + 1)
    full_group = jax.random.randint(key_full, (), 0, group_count)
    counts = jnp.where(jnp.arange(group_count) == full_group, SEQS_G, counts).astype(jnp.int32)
    chosen = jax.random.randint(key_slot, (group_count,), 0, counts)
    whole_seq = jnp.arange(group_count) * SEQS_G + chosen
    is_whole = jnp.any(jnp.arange(SEQS)[:, None] == whole_seq[None, :], axis=1)
    top_segment = max(LEN // 64, 1)
    stride = LEN // (top_segment + 1)
    place = jnp.arange(LEN)
    forced = (place % stride == 0) & (place > 0)
    bounds = (jax.random.randint(key_bound, (SEQS, LEN), 0, 48) == 0) | forced[None, :]
    bounds = bounds & (place > 0)[None, :]
    segment_ids = jnp.cumsum(bounds.astype(jnp.int32), axis=1)
    segment_ids = jnp.minimum(segment_ids, top_segment)
    padding = jax.random.randint(key_pad, (SEQS, 1), 0, LEN // 4 + 1)
    valid_rows = place[None, :] < LEN - padding
    segment_ids = jnp.where(is_whole[:, None], 0, segment_ids)
    valid_rows = jnp.where(is_whole[:, None], True, valid_rows)
    return (counts, valid_rows.astype(jnp.int32), segment_ids.astype(jnp.int32))


def draw_live_counts(key, part):
    return packing(key)[0]


def draw_valid_mask(key, part):
    return packing(key)[1]


def draw_segments(key, part):
    return packing(key)[2]


def level_of(rng, shape, cuts, least, high):
    def one(dim, shards_of):
        draws = jax.random.uniform(jax.random.fold_in(jax.random.fold_in(rng, 6), dim), (shards_of,), jnp.float32, least / len(cuts), high / len(cuts))
        return jnp.repeat(jnp.exp(draws), shape[dim] // shards_of).reshape((-1,) + (1,) * (len(shape) - dim - 1))

    loudness = one(*cuts[0])
    for cut in cuts[1:]:
        loudness = loudness * one(*cut)
    return loudness


def scatter_about(key, shape, scale, reach, shards=(), kind=jnp.bfloat16):
    entries = scale * jax.random.normal(key, shape, jnp.float32)
    if shards:
        entries = entries * level_of(key, shape, shards, -0.22, 0.18)
    return jnp.clip(entries, -reach, reach).astype(kind)


def setup_inputs(seed: int = 0) -> dict:
    keys = jax.random.split(jax.random.key(seed), 21)
    inputs = scatter_about(keys[0], (SEQS, LEN, D), 1.0, 6.0, ((0, 16), (1, 2)))
    cotangent = scatter_about(keys[1], (SEQS, LEN, D), 1.0, 6.0, ((0, 16), (1, 2)))
    w_query = scatter_about(keys[2], (D, D), D ** -0.5, 0.21875)
    b_query = scatter_about(keys[3], (D,), 0.5, 3.0)
    w_key = scatter_about(keys[4], (D, D), D ** -0.5, 0.21875)
    w_value = scatter_about(keys[5], (D, D), D ** -0.5, 0.21875)
    b_value = scatter_about(keys[6], (D,), 0.5, 3.0)
    w_out = scatter_about(keys[7], (D, D), (D // 16) ** -0.5, 0.875)
    b_out = scatter_about(keys[8], (D,), 0.5, 3.0)
    gain_one = jnp.clip(1.0 + 0.1 * jax.random.normal(keys[9], (D,), jnp.float32), 0.5, 1.5).astype(jnp.bfloat16)
    shift_one = scatter_about(keys[10], (D,), 0.5, 3.0)
    w_up = scatter_about(keys[11], (D, FF), D ** -0.5, 0.21875)
    b_up = scatter_about(keys[12], (FF,), 0.5, 3.0)
    w_down = scatter_about(keys[13], (FF, D), FF ** -0.5, 0.109375)
    b_down = scatter_about(keys[14], (D,), 0.5, 3.0)
    gain_two = jnp.clip(1.0 + 0.1 * jax.random.normal(keys[15], (D,), jnp.float32), 0.5, 1.5).astype(jnp.bfloat16)
    shift_two = scatter_about(keys[16], (D,), 0.5, 3.0)
    live_counts = draw_live_counts(jax.random.fold_in(keys[20], 71), 0)
    valid_mask = draw_valid_mask(jax.random.fold_in(keys[20], 71), 0)
    segments = draw_segments(jax.random.fold_in(keys[20], 71), 0)
    return {"inputs": inputs, "cotangent": cotangent, "w_query": w_query, "b_query": b_query, "w_key": w_key, "w_value": w_value, "b_value": b_value, "w_out": w_out, "b_out": b_out, "gain_one": gain_one, "shift_one": shift_one, "w_up": w_up, "b_up": b_up, "w_down": w_down, "b_down": b_down, "gain_two": gain_two, "shift_two": shift_two, "live_counts": live_counts, "valid_mask": valid_mask, "segments": segments}


@jax.custom_vjp
def low(v):
    return lax.optimization_barrier(v.astype(jnp.bfloat16)).astype(jnp.float32)

@jax.custom_vjp
def low_back(v):
    return v

def low_keep(v):
    return (low(v), None)

def low_pass(kept, grad):
    return (grad,)

def back_keep(v):
    return (v, None)

def back_low(kept, grad):
    return (low(grad),)
low.defvjp(low_keep, low_pass)
low_back.defvjp(back_keep, back_low)
EPSILON = 1e-05
NEGATIVE = -1e+30
SCORE_SCALE = 0.125
HIGHEST = lax.Precision.HIGHEST

def product(left, right):
    return jnp.dot(left, right, precision=HIGHEST)

def layer_norm(values, scale_gain, shift_bias):
    center = values - lax.optimization_barrier(jnp.mean(values, axis=-1, keepdims=True))
    spread = lax.optimization_barrier(jnp.mean(center * center, axis=-1, keepdims=True))
    return center * lax.rsqrt(spread + EPSILON) * scale_gain + shift_bias

def forward(token_in, params, seg_rows, mark_rows):
    w_query, b_query, w_key, w_value, b_value, w_out, b_out, gain_one, shift_one, w_up, b_up, w_down, b_down, gain_two, shift_two = params
    batch_seqs, seq_len, model_width = token_in.shape
    token_rows = token_in.reshape(batch_seqs * seq_len, model_width)

    def headwise(flat):
        return flat.reshape(batch_seqs, seq_len, HEADS, HEAD_DIM)
    queries = low(low_back((product(token_rows, w_query) + b_query) * SCORE_SCALE))
    key_proj = low(low_back(product(token_rows, w_key)))
    value_proj = low(low_back(product(token_rows, w_value) + b_value))
    scores = low_back(jnp.einsum('bqhd,bkhd->bhqk', headwise(queries), headwise(key_proj), precision=HIGHEST))
    position = jnp.arange(seq_len)
    visible = (seg_rows[:, :, None] == mark_rows[:, None, :]) | (position[:, None] == position[None, :])[None]
    chances = jax.nn.softmax(jnp.where(visible[:, None], scores, NEGATIVE), axis=-1)
    context = jnp.einsum('bhqk,bkhd->bqhd', low(chances), headwise(value_proj), precision=HIGHEST)
    context = low(low_back(context.reshape(batch_seqs * seq_len, model_width)))
    attention = low_back(product(context, w_out) + b_out)
    middle = layer_norm(token_rows + attention, gain_one, shift_one)
    hidden = low_back(product(low(middle), w_up) + b_up)
    activated = low(jax.nn.gelu(hidden, approximate=False))
    feed_out = low_back(product(activated, w_down) + b_down)
    result = layer_norm(middle + feed_out, gain_two, shift_two)
    return (result, attention, feed_out)

def reference(inputs, cotangent, w_query, b_query, w_key, w_value, b_value, w_out, b_out, gain_one, shift_one, w_up, b_up, w_down, b_down, gain_two, shift_two, live_counts, valid_mask, segments):
    slot_index = jnp.arange(SEQS) % SEQS_G
    owner_group = (jnp.arange(SEQS) // SEQS_G).astype(jnp.int32)
    live_rows = (slot_index < live_counts[owner_group]).astype(jnp.float32)
    token_weight = valid_mask.astype(jnp.float32) * live_rows[:, None]
    key_mark = jnp.where(token_weight > 0, segments, -1).astype(jnp.int32)
    params = tuple((param.astype(jnp.float32) for param in (w_query, b_query, w_key, w_value, b_value, w_out, b_out, gain_one, shift_one, w_up, b_up, w_down, b_down, gain_two, shift_two)))
    block_count = SEQS // 8

    def regroup(array):
        return array.reshape((block_count, 8) + array.shape[1:])

    def scan_block(carried, pieces):
        gradients, totals = carried
        block_in, block_cot, block_weight, block_segs, block_marks = pieces
        rows_in = block_in.astype(jnp.float32)

        def forward_all(token_in, *weights):
            return forward(token_in, weights, block_segs, block_marks)
        primal, pull_back = jax.vjp(forward_all, rows_in, *params)
        result, attention, feed_out = primal
        weight_rows = block_weight.reshape(-1)
        grad_result = (block_cot.astype(jnp.float32) * block_weight[..., None]).reshape(result.shape)
        pulled = pull_back((grad_result, jnp.zeros_like(attention), jnp.zeros_like(feed_out)))
        gradients = tuple((first + second for first, second in zip(gradients, pulled[1:])))
        flat_in = rows_in.reshape(-1, D)
        sums = [jnp.sum(weight_rows * lax.optimization_barrier(jnp.sum(entry * entry, axis=-1))) for entry in (flat_in, attention, feed_out, result)]
        new_totals = jnp.stack(sums + [jnp.sum(weight_rows)])
        outputs = (result.astype(jnp.bfloat16).reshape(block_in.shape), pulled[0])
        return ((gradients, totals + new_totals), outputs)
    start = (tuple((jnp.zeros_like(param) for param in params)), jnp.zeros((5,), jnp.float32))
    (gradients, totals), (outs_all, grads_all) = lax.scan(scan_block, start, (regroup(inputs), regroup(cotangent), regroup(token_weight), regroup(segments), regroup(key_mark)))
    result_out = outs_all.reshape(SEQS, LEN, D)
    grad_inputs = grads_all.reshape(SEQS, LEN, D)
    rms_values = jnp.sqrt(totals[:4] / (D * totals[4]))
    return (result_out, grad_inputs) + tuple(gradients) + (rms_values,)
```

```python
import functools

import jax
import jax.numpy as jnp
from jax import lax
from jax.experimental import pallas as pl
from jax.experimental.pallas import tpu as pltpu
from jax.sharding import PartitionSpec as P

HEAD_DIM = 64
EPSILON = 1e-05
NEGATIVE = -1e30
SCORE_SCALE = 0.125
LOW = jnp.bfloat16
WIDE = jnp.float32
VMEM_LIMIT = 56 * 1024 * 1024
HIDDEN_STEP = 512

ERF_P = 0.3275911
ERF_C = (0.254829592, -0.284496736, 1.421413741, -1.453152027, 1.061405429)
ROOT_HALF = 0.7071067811865476
DENSITY = 0.3989422804014327


def nn(left, right):
    return jnp.dot(left, right, preferred_element_type=WIDE)


def nt(left, right):
    return lax.dot_general(
        left, right, (((1,), (1,)), ((), ())), preferred_element_type=WIDE
    )


def tn(left, right):
    return lax.dot_general(
        left, right, (((0,), (0,)), ((), ())), preferred_element_type=WIDE
    )


def gelu_pair(hidden):
    tail_exp = jnp.exp(hidden * hidden * -0.5)
    t = 1.0 / (1.0 + (ERF_P * ROOT_HALF) * jnp.abs(hidden))
    c1, c2, c3, c4, c5 = (0.5 * c for c in ERF_C)
    tail = ((((c5 * t + c4) * t + c3) * t + c2) * t + c1) * t * tail_exp
    below = jnp.where(hidden >= 0.0, 1.0 - tail, tail)
    return hidden * below, below + hidden * (DENSITY * tail_exp)


def lane_half(half):
    lane = lax.broadcasted_iota(jnp.int32, (1, 2 * HEAD_DIM), 1)
    inside = (lane < HEAD_DIM) if half == 0 else (lane >= HEAD_DIM)
    return inside.astype(WIDE).astype(LOW)


def fill_bias(bias_ref, seg_row, mark_col):
    length = bias_ref.shape[0]
    key_place = lax.broadcasted_iota(jnp.int32, (length, length), 0)
    query_place = lax.broadcasted_iota(jnp.int32, (length, length), 1)
    visible = (mark_col == seg_row) | (key_place == query_place)
    bias_ref[...] = jnp.where(visible, 0.0, NEGATIVE)


def total(rows_weight, values):
    per_row = jnp.sum(values * values, axis=1, keepdims=True) * rows_weight
    return jnp.sum(per_row, axis=0, keepdims=True)


def attend_kernel(
    x_ref, seg_ref, mark_ref, wq_ref, bq_ref, wk_ref, wv_ref, bv_ref, wo_ref, bo_ref, gain_ref,
    shift_ref, q_ref, k_ref, v_ref, ctx_ref, lse_ref, mid_ref, norm_ref, rstd_ref, stat_ref,
    bias_ref,
):
    x = x_ref[...]
    q_ref[...] = ((nn(x, wq_ref[...]) + bq_ref[...]) * SCORE_SCALE).astype(LOW)
    k_ref[...] = nn(x, wk_ref[...]).astype(LOW)
    v_ref[...] = (nn(x, wv_ref[...]) + bv_ref[...]).astype(LOW)
    fill_bias(bias_ref, seg_ref[...], mark_ref[...])
    width = 2 * HEAD_DIM
    pairs = x.shape[1] // width

    def pair_step(pair, carried):
        lanes = pl.ds(pl.multiple_of(pair * width, width), width)
        q, k, v = q_ref[:, lanes], k_ref[:, lanes], v_ref[:, lanes]
        v_turned = v.T
        outs = []
        for half in range(2):
            scores = nt(k * lane_half(half), q) + bias_ref[...]
            top = jnp.max(scores, axis=0, keepdims=True)
            weights = jnp.exp(scores - top)
            amount = jnp.sum(weights, axis=0, keepdims=True)
            summed = nn(v_turned[half * HEAD_DIM : (half + 1) * HEAD_DIM], weights.astype(LOW))
            outs.append(summed * (1.0 / amount))
            lse_ref[pl.ds(pair * 2 + half, 1), :] = top + jnp.log(amount)
        ctx_ref[:, lanes] = jnp.concatenate(outs, axis=0).T.astype(LOW)
        return carried

    lax.fori_loop(0, pairs, pair_step, 0)
    attention = nn(ctx_ref[...], wo_ref[...]) + bo_ref[...]
    rows = x.astype(WIDE)
    total_in = rows + attention
    center = total_in - jnp.mean(total_in, axis=1, keepdims=True)
    rstd = lax.rsqrt(jnp.mean(center * center, axis=1, keepdims=True) + EPSILON)
    normal = center * rstd
    mid_ref[...] = normal * gain_ref[...] + shift_ref[...]
    norm_ref[...] = normal.astype(LOW)
    rstd_ref[...] = rstd
    row_weight = (mark_ref[...] >= 0).astype(WIDE)
    stat_ref[...] = jnp.concatenate(
        [
            jnp.broadcast_to(total(row_weight, rows), (1, 128)),
            jnp.broadcast_to(total(row_weight, attention), (1, 128)),
            jnp.zeros((6, 128), WIDE),
        ],
        axis=0,
    )


def whole(shape):
    return pl.BlockSpec(shape, lambda *_: (0,) * len(shape), pipeline_mode=pl.Buffered(1))


def attend(x, seg_row, mark_col, wq, bq, wk, wv, bv, wo, bo, gain, shift):
    length, width = x.shape
    heads = width // HEAD_DIM
    lse_rows = heads + (-heads) % 8
    shapes = (
        jax.ShapeDtypeStruct((length, width), LOW),
        jax.ShapeDtypeStruct((length, width), LOW),
        jax.ShapeDtypeStruct((length, width), LOW),
        jax.ShapeDtypeStruct((length, width), LOW),
        jax.ShapeDtypeStruct((lse_rows, length), WIDE),
        jax.ShapeDtypeStruct((length, width), WIDE),
        jax.ShapeDtypeStruct((length, width), LOW),
        jax.ShapeDtypeStruct((length, 1), WIDE),
        jax.ShapeDtypeStruct((8, 128), WIDE),
    )
    args = (x, seg_row, mark_col, wq, bq, wk, wv, bv, wo, bo, gain, shift)
    return pl.pallas_call(
        attend_kernel,
        out_shape=shapes,
        in_specs=[pl.BlockSpec(memory_space=pltpu.VMEM)] * len(args),
        out_specs=tuple([pl.BlockSpec(memory_space=pltpu.VMEM)] * len(shapes)),
        scratch_shapes=[pltpu.VMEM((length, length), WIDE)],
        compiler_params=pltpu.CompilerParams(vmem_limit_bytes=VMEM_LIMIT),
        cost_estimate=pl.CostEstimate(
            flops=2 * length * width * (4 * width + 2 * length),
            transcendentals=heads * length * length,
            bytes_accessed=12 * length * width + 8 * width * width,
        ),
        name="attend",
    )(*args)


def feed_kernel(
    place_ref, mid0_ref, mid1_ref, cot_ref, weight_ref, wu_ref, bu_ref, wd_ref, bd_ref, gain_ref,
    shift_ref, act_s_ref, act_k_ref, slope_s_ref, slope_k_ref, low_ref, result_ref, grad_ref,
    grad_low_ref, sums_ref, stat_ref, *, half_tiles,
):
    step = pl.program_id(0)
    half = act_s_ref.shape[1]
    core = place_ref[0]
    middle = jnp.where(step < half_tiles, mid0_ref[...], mid1_ref[...])
    middle_low = middle.astype(LOW)
    low_ref[...] = middle_low
    feed = jnp.zeros_like(middle) + bd_ref[...]
    for part, (act_ref, slope_ref) in enumerate(((act_s_ref, slope_s_ref), (act_k_ref, slope_k_ref))):
        base = (1 - core if part == 0 else core) * half
        for start in range(0, half, HIDDEN_STEP):
            place = pl.ds(pl.multiple_of(base + start, HIDDEN_STEP), HIDDEN_STEP)
            here = pl.ds(start, HIDDEN_STEP)
            hidden = nn(middle_low, wu_ref[:, place]) + bu_ref[:, place]
            active, slope = gelu_pair(hidden)
            active = active.astype(LOW)
            act_ref[:, here] = active
            slope_ref[:, here] = slope.astype(LOW)
            feed = feed + nn(active, wd_ref[place, :])
    total_in = middle + feed
    center = total_in - jnp.mean(total_in, axis=1, keepdims=True)
    rstd = lax.rsqrt(jnp.mean(center * center, axis=1, keepdims=True) + EPSILON)
    normal = center * rstd
    gain = gain_ref[...]
    result = normal * gain + shift_ref[...]
    result_ref[...] = result.astype(LOW)
    weight = weight_ref[...]
    grad_result = cot_ref[...].astype(WIDE) * weight
    pulled = grad_result * gain
    grad = rstd * (
        pulled
        - jnp.mean(pulled, axis=1, keepdims=True)
        - normal * jnp.mean(pulled * normal, axis=1, keepdims=True)
    )
    grad_ref[...] = grad
    grad_low = grad.astype(LOW)
    grad_low_ref[...] = grad_low

    @pl.when(step == 0)
    def _():
        sums_ref[...] = jnp.zeros_like(sums_ref)
        stat_ref[...] = jnp.zeros_like(stat_ref)

    sums_ref[0:1, :] += jnp.sum(grad_result * normal, axis=0, keepdims=True)
    sums_ref[1:2, :] += jnp.sum(grad_result, axis=0, keepdims=True)
    sums_ref[2:3, :] += jnp.sum(grad_low.astype(WIDE), axis=0, keepdims=True)
    stat_ref[0:1, :] += jnp.broadcast_to(total(weight, feed), (1, 128))
    stat_ref[1:2, :] += jnp.broadcast_to(total(weight, result), (1, 128))


def feed_forward(place, mids, cot, weight_col, wu, bu, wd, bd, gain, shift):
    length, width = mids[0].shape
    rows = length * len(mids)
    tile = 256
    steps = rows // tile
    half_tiles = steps // 2
    hidden = wu.shape[1]
    half = hidden // 2

    def tiled(columns):
        return pl.BlockSpec((tile, columns), lambda i, *_: (i, 0))

    args = (mids[0], mids[1], cot, weight_col, wu, bu, wd, bd, gain, shift)
    in_specs = [
        pl.BlockSpec((tile, width), lambda i, *_: (jnp.minimum(i, half_tiles - 1), 0)),
        pl.BlockSpec((tile, width), lambda i, *_: (jnp.maximum(i - half_tiles, 0), 0)),
        tiled(width),
        tiled(1),
    ] + [whole(arg.shape) for arg in args[4:]]
    shapes = (
        jax.ShapeDtypeStruct((rows, half), LOW),
        jax.ShapeDtypeStruct((rows, half), LOW),
        jax.ShapeDtypeStruct((rows, half), LOW),
        jax.ShapeDtypeStruct((rows, half), LOW),
        jax.ShapeDtypeStruct((rows, width), LOW),
        jax.ShapeDtypeStruct((rows, width), LOW),
        jax.ShapeDtypeStruct((rows, width), WIDE),
        jax.ShapeDtypeStruct((rows, width), LOW),
        jax.ShapeDtypeStruct((8, width), WIDE),
        jax.ShapeDtypeStruct((8, 128), WIDE),
    )
    out_specs = tuple(
        tiled(shape.shape[1]) if shape.shape[0] == rows else whole(shape.shape) for shape in shapes
    )
    return pl.pallas_call(
        functools.partial(feed_kernel, half_tiles=half_tiles),
        out_shape=shapes,
        grid_spec=pltpu.PrefetchScalarGridSpec(
            num_scalar_prefetch=1, grid=(steps,), in_specs=in_specs, out_specs=out_specs
        ),
        compiler_params=pltpu.CompilerParams(
            vmem_limit_bytes=VMEM_LIMIT, dimension_semantics=("arbitrary",)
        ),
        cost_estimate=pl.CostEstimate(
            flops=4 * rows * width * hidden,
            transcendentals=2 * rows * hidden,
            bytes_accessed=rows * (4 * hidden + 16 * width) + 4 * width * hidden,
        ),
        name="feed_forward",
    )(place, *args)


def feed_back_kernel(
    place_ref, grad_low_ref, grad_ref, slope_s_ref, slope_k_ref, norm0_ref, norm1_ref, rstd0_ref,
    rstd1_ref, wu_ref, wd_ref, wo_ref, gain_ref, hid_s_ref, hid_k_ref, grad_one_ref, attn_ref,
    ctx_ref, up_sums_ref, sums_ref, *, half_tiles,
):
    step = pl.program_id(0)
    half = hid_s_ref.shape[1]
    core = place_ref[0]

    @pl.when(step == 0)
    def _():
        up_sums_ref[...] = jnp.zeros_like(up_sums_ref)
        sums_ref[...] = jnp.zeros_like(sums_ref)

    grad_low = grad_low_ref[...]
    grad_middle = grad_ref[...]
    for part, (hid_ref, slope_ref) in enumerate(((hid_s_ref, slope_s_ref), (hid_k_ref, slope_k_ref))):
        base = (1 - core if part == 0 else core) * half
        for start in range(0, half, HIDDEN_STEP):
            place = pl.ds(pl.multiple_of(base + start, HIDDEN_STEP), HIDDEN_STEP)
            here = pl.ds(start, HIDDEN_STEP)
            grad_act = nt(grad_low, wd_ref[place, :])
            grad_hidden = (grad_act * slope_ref[:, here].astype(WIDE)).astype(LOW)
            hid_ref[:, here] = grad_hidden
            up_sums_ref[0:1, place] += jnp.sum(grad_hidden.astype(WIDE), axis=0, keepdims=True)
            grad_middle = grad_middle + nt(grad_hidden, wu_ref[:, place])
    first = step < half_tiles
    normal = jnp.where(first, norm0_ref[...].astype(WIDE), norm1_ref[...].astype(WIDE))
    rstd = jnp.where(first, rstd0_ref[...], rstd1_ref[...])
    pulled = grad_middle * gain_ref[...]
    grad_one = rstd * (
        pulled
        - jnp.mean(pulled, axis=1, keepdims=True)
        - normal * jnp.mean(pulled * normal, axis=1, keepdims=True)
    )
    grad_one_ref[...] = grad_one
    attn = grad_one.astype(LOW)
    attn_ref[...] = attn
    ctx_ref[...] = nt(attn, wo_ref[...]).astype(LOW)
    sums_ref[0:1, :] += jnp.sum(grad_middle * normal, axis=0, keepdims=True)
    sums_ref[1:2, :] += jnp.sum(grad_middle, axis=0, keepdims=True)
    sums_ref[2:3, :] += jnp.sum(attn.astype(WIDE), axis=0, keepdims=True)


def feed_back(place, grad_low, grad, slope_s, slope_k, norms, rstds, wu, wd, wo, gain):
    rows, width = grad.shape
    tile = 256
    steps = rows // tile
    half_tiles = steps // 2
    hidden = wu.shape[1]
    half = hidden // 2

    def tiled(columns):
        return pl.BlockSpec((tile, columns), lambda i, *_: (i, 0))

    def first(columns):
        return pl.BlockSpec((tile, columns), lambda i, *_: (jnp.minimum(i, half_tiles - 1), 0))

    def second(columns):
        return pl.BlockSpec((tile, columns), lambda i, *_: (jnp.maximum(i - half_tiles, 0), 0))

    args = (
        grad_low, grad, slope_s, slope_k, norms[0], norms[1], rstds[0], rstds[1], wu, wd, wo, gain,
    )
    in_specs = [
        tiled(width), tiled(width), tiled(half), tiled(half), first(width), second(width),
        first(1), second(1),
    ] + [whole(arg.shape) for arg in args[8:]]
    shapes = (
        jax.ShapeDtypeStruct((rows, half), LOW),
        jax.ShapeDtypeStruct((rows, half), LOW),
        jax.ShapeDtypeStruct((rows, width), WIDE),
        jax.ShapeDtypeStruct((rows, width), LOW),
        jax.ShapeDtypeStruct((rows, width), LOW),
        jax.ShapeDtypeStruct((8, hidden), WIDE),
        jax.ShapeDtypeStruct((8, width), WIDE),
    )
    out_specs = tuple(
        tiled(shape.shape[1]) if shape.shape[0] == rows else whole(shape.shape) for shape in shapes
    )
    return pl.pallas_call(
        functools.partial(feed_back_kernel, half_tiles=half_tiles),
        out_shape=shapes,
        grid_spec=pltpu.PrefetchScalarGridSpec(
            num_scalar_prefetch=1, grid=(steps,), in_specs=in_specs, out_specs=out_specs
        ),
        compiler_params=pltpu.CompilerParams(
            vmem_limit_bytes=VMEM_LIMIT, dimension_semantics=("arbitrary",)
        ),
        cost_estimate=pl.CostEstimate(
            flops=4 * rows * width * hidden + 2 * rows * width * width,
            transcendentals=0,
            bytes_accessed=rows * (4 * hidden + 16 * width) + 4 * width * hidden,
        ),
        name="feed_back",
    )(place, *args)


def attend_back_kernel(
    q_ref, k_ref, v_ref, ctx_ref, grad_ctx_ref, lse_ref, seg_ref, mark_ref, grad_one_ref, wq_ref,
    wk_ref, wv_ref, dq_ref, dk_ref, dv_ref, grad_in_ref, sums_ref, bias_ref,
):
    fill_bias(bias_ref, seg_ref[...], mark_ref[...])
    width = 2 * HEAD_DIM
    pairs = q_ref.shape[1] // width

    def pair_step(pair, carried):
        lanes = pl.ds(pl.multiple_of(pair * width, width), width)
        q, k, v, grad = q_ref[:, lanes], k_ref[:, lanes], v_ref[:, lanes], grad_ctx_ref[:, lanes]
        k_turned = k.T
        shared = (grad.astype(WIDE) * ctx_ref[:, lanes].astype(WIDE)).T
        part_q, part_k, part_v = [], [], []
        for half in range(2):
            inside = slice(half * HEAD_DIM, (half + 1) * HEAD_DIM)
            delta = jnp.sum(shared[inside], axis=0, keepdims=True)
            scores = nt(k * lane_half(half), q) + bias_ref[...]
            chances = jnp.exp(scores - lse_ref[pl.ds(pair * 2 + half, 1), :])
            part_v.append(nn(chances.astype(LOW), grad))
            grad_chances = nt(v * lane_half(half), grad)
            grad_scores = (chances * (grad_chances - delta)).astype(LOW)
            part_k.append(nn(grad_scores, q))
            part_q.append(nn(k_turned[inside], grad_scores))
        first = lax.broadcasted_iota(jnp.int32, part_k[0].shape, 1) < HEAD_DIM
        dq_ref[:, lanes] = jnp.concatenate(part_q, axis=0).T.astype(LOW)
        dk_ref[:, lanes] = jnp.where(first, part_k[0], part_k[1]).astype(LOW)
        dv_ref[:, lanes] = jnp.where(first, part_v[0], part_v[1]).astype(LOW)
        return carried

    lax.fori_loop(0, pairs, pair_step, 0)
    dq, dk, dv = dq_ref[...], dk_ref[...], dv_ref[...]
    grad_in_ref[...] = (
        grad_one_ref[...]
        + nt(dq, wq_ref[...]) * SCORE_SCALE
        + nt(dk, wk_ref[...])
        + nt(dv, wv_ref[...])
    )
    sums_ref[...] = jnp.concatenate(
        [
            jnp.sum(dq.astype(WIDE), axis=0, keepdims=True) * SCORE_SCALE,
            jnp.sum(dv.astype(WIDE), axis=0, keepdims=True),
            jnp.zeros((6, dq.shape[1]), WIDE),
        ],
        axis=0,
    )


def attend_back(slot, q, k, v, ctx, grad_ctx, lse, seg_row, mark_col, grad_one, wq, wk, wv):
    length, width = q.shape
    heads = width // HEAD_DIM
    shapes = (
        jax.ShapeDtypeStruct((length, width), LOW),
        jax.ShapeDtypeStruct((length, width), LOW),
        jax.ShapeDtypeStruct((length, width), LOW),
        jax.ShapeDtypeStruct((length, width), WIDE),
        jax.ShapeDtypeStruct((8, width), WIDE),
    )
    args = (q, k, v, ctx, grad_ctx, lse, seg_row, mark_col, grad_one, wq, wk, wv)
    picked = pl.BlockSpec((length, width), lambda i: (slot, 0), pipeline_mode=pl.Buffered(1))
    in_specs = [
        picked if arg is grad_ctx or arg is grad_one else whole(arg.shape) for arg in args
    ]
    return pl.pallas_call(
        attend_back_kernel,
        grid=(1,),
        out_shape=shapes,
        in_specs=in_specs,
        out_specs=tuple(whole(shape.shape) for shape in shapes),
        scratch_shapes=[pltpu.VMEM((length, length), WIDE)],
        compiler_params=pltpu.CompilerParams(
            vmem_limit_bytes=VMEM_LIMIT, dimension_semantics=("arbitrary",)
        ),
        cost_estimate=pl.CostEstimate(
            flops=2 * length * width * (3 * width + 5 * length),
            transcendentals=heads * length * length,
            bytes_accessed=24 * length * width + 6 * width * width,
        ),
        name="attend_back",
    )(*args)


def swap_pieces(value, axis):
    count = lax.axis_size(axis)
    me = lax.axis_index(axis)
    slots = value.shape[0] // count
    pieces = [lax.dynamic_slice_in_dim(value, me * slots, slots, 0)]
    for shift in range(1, count):
        target = (me + shift) % count
        block = lax.dynamic_slice_in_dim(value, target * slots, slots, 0)
        pairs = [(source, (source + shift) % count) for source in range(count)]
        pieces.append(lax.ppermute(block, axis, pairs))
    return pieces


def return_pieces(pieces, axis):
    count = lax.axis_size(axis)
    me = lax.axis_index(axis)
    slots = pieces[0].shape[0]
    out = jnp.zeros((slots * count,) + pieces[0].shape[1:], pieces[0].dtype)
    out = lax.dynamic_update_slice_in_dim(out, pieces[0], me * slots, 0)
    for shift in range(1, count):
        pairs = [(source, (source - shift) % count) for source in range(count)]
        got = lax.ppermute(pieces[shift], axis, pairs)
        out = lax.dynamic_update_slice_in_dim(out, got, ((me + shift) % count) * slots, 0)
    return out


def sum_everywhere(value):
    part = lax.psum_scatter(value, ("dp", "seq"), scatter_dimension=0, tiled=True)
    return lax.all_gather(part, ("dp", "seq"), axis=0, tiled=True)


def on_device(
    inputs, cotangent, w_query, b_query, w_key, w_value, b_value, w_out, b_out, gain_one,
    shift_one, w_up, b_up, w_down, b_down, gain_two, shift_two, live_counts, valid_mask, segments,
):
    seqs, piece, width = inputs.shape
    count = lax.axis_size("seq")
    slots = seqs // count
    length = piece * count
    rows = slots * length
    place = (lax.axis_index("dp") % 2).astype(jnp.int32).reshape(1)

    def row_of(vector):
        return vector.astype(WIDE).reshape(1, -1)

    live = (jnp.arange(seqs) < live_counts[0]).astype(jnp.int32)
    code = segments * 2 + valid_mask * live[:, None]
    codes = jnp.concatenate(swap_pieces(code, "seq"), axis=1)
    seg = codes // 2
    weight = codes % 2
    mark = jnp.where(weight > 0, seg, -1)
    x_parts = swap_pieces(inputs, "seq")
    x_all = jnp.concatenate(x_parts, axis=1)
    cot_all = jnp.concatenate(swap_pieces(cotangent, "seq"), axis=1).reshape(rows, width)
    weight_col = weight.astype(WIDE).reshape(rows, 1)

    bq, bv, bo = row_of(b_query), row_of(b_value), row_of(b_out)
    gain1, shift1 = row_of(gain_one), row_of(shift_one)
    gain2, shift2 = row_of(gain_two), row_of(shift_two)
    bu, bd = row_of(b_up), row_of(b_down)

    seg_rows = [seg[slot].reshape(1, length) for slot in range(slots)]
    mark_cols = [mark[slot].reshape(length, 1) for slot in range(slots)]
    forward = [
        attend(
            x_all[slot], seg_rows[slot], mark_cols[slot], w_query, bq, w_key, w_value, bv, w_out,
            bo, gain1, shift1,
        )
        for slot in range(slots)
    ]
    (act_s, act_k, slope_s, slope_k, mid_low, result, grad_h2, grad_feed, sums_two, stat_two) = (
        feed_forward(
            place, [each[5] for each in forward], cot_all, weight_col, w_up, bu, w_down, bd,
            gain2, shift2,
        )
    )
    core = place[0]

    def halves(sent, kept, axis):
        low = jnp.where(core == 0, kept, sent)
        high = jnp.where(core == 0, sent, kept)
        return jnp.concatenate([low, high], axis=axis)

    grad_w_down = halves(tn(act_s, grad_feed).astype(LOW), tn(act_k, grad_feed).astype(LOW), 0)
    grad_w_down = sum_everywhere(grad_w_down)
    hid_s, hid_k, grad_h1, grad_attn, grad_ctx, up_sums, sums_one = feed_back(
        place, grad_feed, grad_h2, slope_s, slope_k, [each[6] for each in forward],
        [each[7] for each in forward], w_up, w_down, w_out, gain1,
    )
    grad_w_up = halves(tn(mid_low, hid_s).astype(LOW), tn(mid_low, hid_k).astype(LOW), 1)
    grad_w_up = sum_everywhere(grad_w_up)
    ctx_all = jnp.concatenate([each[3] for each in forward], axis=0)
    grad_w_out = tn(ctx_all, grad_attn).astype(LOW)
    backward = [
        attend_back(
            slot, *forward[slot][:4], grad_ctx, forward[slot][4], seg_rows[slot],
            mark_cols[slot], grad_h1, w_query, w_key, w_value,
        )
        for slot in range(slots)
    ]
    x_rows = x_all.reshape(rows, width)
    dq, dk, dv = (jnp.concatenate([each[i] for each in backward], axis=0) for i in range(3))
    grads = jnp.concatenate(
        [
            (tn(x_rows, dq) * SCORE_SCALE).astype(LOW),
            tn(x_rows, dk).astype(LOW),
            tn(x_rows, dv).astype(LOW),
            grad_w_out,
        ],
        axis=1,
    )
    grads = sum_everywhere(grads)

    stats = [
        sum(each[8][0, 0] for each in forward),
        sum(each[8][1, 0] for each in forward),
        stat_two[0, 0],
        stat_two[1, 0],
        jnp.sum(weight).astype(WIDE),
    ]
    stats = jnp.concatenate([jnp.stack(stats), jnp.zeros((width - 5,), WIDE)]).reshape(1, width)
    small = jnp.concatenate(
        [
            sum(each[4][0:2] for each in backward),
            sums_one[0:3],
            sums_two[0:3],
            stats,
            up_sums[0:1].reshape(-1, width),
        ],
        axis=0,
    )
    small = lax.psum(small, ("dp", "seq"))
    rms_values = jnp.sqrt(small[8, :4] / (width * small[8, 4]))

    result = result.reshape(slots, length, width)
    grad_inputs = jnp.stack([each[3] for each in backward])
    result_out = return_pieces(
        [result[:, i * piece : (i + 1) * piece] for i in range(count)], "seq"
    )
    sent = [
        grad_inputs[:, i * piece : (i + 1) * piece].astype(LOW if i else WIDE)
        for i in range(count)
    ]
    me = lax.axis_index("seq")
    grad_out = jnp.zeros((seqs, piece, width), WIDE)
    grad_out = lax.dynamic_update_slice_in_dim(grad_out, sent[0], me * slots, 0)
    for shift in range(1, count):
        pairs = [(source, (source - shift) % count) for source in range(count)]
        got = lax.ppermute(sent[shift], "seq", pairs).astype(WIDE)
        grad_out = lax.dynamic_update_slice_in_dim(
            grad_out, got, ((me + shift) % count) * slots, 0
        )

    grads = grads.astype(WIDE)
    return (
        result_out,
        grad_out,
        grads[:, 0 * width : 1 * width],
        small[0],
        grads[:, 1 * width : 2 * width],
        grads[:, 2 * width : 3 * width],
        small[1],
        grads[:, 3 * width : 4 * width],
        small[4],
        small[2],
        small[3],
        grad_w_up.astype(WIDE),
        small[9:].reshape(-1),
        grad_w_down.astype(WIDE),
        small[7],
        small[5],
        small[6],
        rms_values,
    )


def solution(mesh):
    split = P("dp", "seq", None)
    pair = P("dp", "seq")
    return jax.shard_map(
        on_device,
        mesh=mesh,
        in_specs=(split, split) + (P(),) * 15 + (P("dp"), pair, pair),
        out_specs=(split, split) + (P(),) * 16,
        check_vma=False,
    )
```

```python
import functools

import jax
import jax.numpy as jnp
from jax import lax
from jax.experimental import pallas as pl
from jax.experimental.pallas import tpu as pltpu
from jax.sharding import PartitionSpec as P

HEAD_DIM = 64
EPSILON = 1e-05
NEGATIVE = -1e30
SCORE_SCALE = 0.125
LOW = jnp.bfloat16
WIDE = jnp.float32
VMEM_LIMIT = 56 * 1024 * 1024
HIDDEN_STEP = 512

ERF_P = 0.3275911
ERF_C = (0.254829592, -0.284496736, 1.421413741, -1.453152027, 1.061405429)
ROOT_HALF = 0.7071067811865476
DENSITY = 0.3989422804014327


def nn(left, right):
    return jnp.dot(left, right, preferred_element_type=WIDE)


def nt(left, right):
    return lax.dot_general(
        left, right, (((1,), (1,)), ((), ())), preferred_element_type=WIDE
    )


def tn(left, right):
    return lax.dot_general(
        left, right, (((0,), (0,)), ((), ())), preferred_element_type=WIDE
    )


def gelu_pair(hidden):
    tail_exp = jnp.exp(hidden * hidden * -0.5)
    t = 1.0 / (1.0 + (ERF_P * ROOT_HALF) * jnp.abs(hidden))
    c1, c2, c3, c4, c5 = (0.5 * c for c in ERF_C)
    tail = ((((c5 * t + c4) * t + c3) * t + c2) * t + c1) * t * tail_exp
    below = jnp.where(hidden >= 0.0, 1.0 - tail, tail)
    return hidden * below, below + hidden * (DENSITY * tail_exp)


def lane_half(half):
    lane = lax.broadcasted_iota(jnp.int32, (1, 2 * HEAD_DIM), 1)
    inside = (lane < HEAD_DIM) if half == 0 else (lane >= HEAD_DIM)
    return inside.astype(WIDE).astype(LOW)


def fill_bias(bias_ref, seg_row, mark_col):
    length = bias_ref.shape[0]
    key_place = lax.broadcasted_iota(jnp.int32, (length, length), 0)
    query_place = lax.broadcasted_iota(jnp.int32, (length, length), 1)
    visible = (mark_col == seg_row) | (key_place == query_place)
    bias_ref[...] = jnp.where(visible, 0.0, NEGATIVE)


def total(rows_weight, values):
    per_row = jnp.sum(values * values, axis=1, keepdims=True) * rows_weight
    return jnp.sum(per_row, axis=0, keepdims=True)


def attend_kernel(
    x_ref, seg_ref, mark_ref, wq_ref, bq_ref, wk_ref, wv_ref, bv_ref, wo_ref, bo_ref, gain_ref,
    shift_ref, q_ref, k_ref, v_ref, ctx_ref, lse_ref, mid_ref, norm_ref, rstd_ref, stat_ref,
    bias_ref,
):
    x = x_ref[...]
    q_ref[...] = ((nn(x, wq_ref[...]) + bq_ref[...]) * SCORE_SCALE).astype(LOW)
    k_ref[...] = nn(x, wk_ref[...]).astype(LOW)
    v_ref[...] = (nn(x, wv_ref[...]) + bv_ref[...]).astype(LOW)
    fill_bias(bias_ref, seg_ref[...], mark_ref[...])
    width = 2 * HEAD_DIM
    pairs = x.shape[1] // width

    def pair_step(pair, carried):
        lanes = pl.ds(pl.multiple_of(pair * width, width), width)
        q, k, v = q_ref[:, lanes], k_ref[:, lanes], v_ref[:, lanes]
        v_turned = v.T
        outs = []
        for half in range(2):
            scores = nt(k * lane_half(half), q) + bias_ref[...]
            top = jnp.max(scores, axis=0, keepdims=True)
            weights = jnp.exp(scores - top)
            amount = jnp.sum(weights, axis=0, keepdims=True)
            summed = nn(v_turned[half * HEAD_DIM : (half + 1) * HEAD_DIM], weights.astype(LOW))
            outs.append(summed * (1.0 / amount))
            lse_ref[pl.ds(pair * 2 + half, 1), :] = top + jnp.log(amount)
        ctx_ref[:, lanes] = jnp.concatenate(outs, axis=0).T.astype(LOW)
        return carried

    lax.fori_loop(0, pairs, pair_step, 0)
    attention = nn(ctx_ref[...], wo_ref[...]) + bo_ref[...]
    rows = x.astype(WIDE)
    total_in = rows + attention
    center = total_in - jnp.mean(total_in, axis=1, keepdims=True)
    rstd = lax.rsqrt(jnp.mean(center * center, axis=1, keepdims=True) + EPSILON)
    normal = center * rstd
    mid_ref[...] = normal * gain_ref[...] + shift_ref[...]
    norm_ref[...] = normal.astype(LOW)
    rstd_ref[...] = rstd
    row_weight = (mark_ref[...] >= 0).astype(WIDE)
    stat_ref[...] = jnp.concatenate(
        [
            jnp.broadcast_to(total(row_weight, rows), (1, 128)),
            jnp.broadcast_to(total(row_weight, attention), (1, 128)),
            jnp.zeros((6, 128), WIDE),
        ],
        axis=0,
    )


def whole(shape):
    return pl.BlockSpec(shape, lambda *_: (0,) * len(shape), pipeline_mode=pl.Buffered(1))


def attend(x, seg_row, mark_col, wq, bq, wk, wv, bv, wo, bo, gain, shift):
    length, width = x.shape
    heads = width // HEAD_DIM
    lse_rows = heads + (-heads) % 8
    shapes = (
        jax.ShapeDtypeStruct((length, width), LOW),
        jax.ShapeDtypeStruct((length, width), LOW),
        jax.ShapeDtypeStruct((length, width), LOW),
        jax.ShapeDtypeStruct((length, width), LOW),
        jax.ShapeDtypeStruct((lse_rows, length), WIDE),
        jax.ShapeDtypeStruct((length, width), WIDE),
        jax.ShapeDtypeStruct((length, width), LOW),
        jax.ShapeDtypeStruct((length, 1), WIDE),
        jax.ShapeDtypeStruct((8, 128), WIDE),
    )
    args = (x, seg_row, mark_col, wq, bq, wk, wv, bv, wo, bo, gain, shift)
    return pl.pallas_call(
        attend_kernel,
        out_shape=shapes,
        in_specs=[pl.BlockSpec(memory_space=pltpu.VMEM)] * len(args),
        out_specs=tuple([pl.BlockSpec(memory_space=pltpu.VMEM)] * len(shapes)),
        scratch_shapes=[pltpu.VMEM((length, length), WIDE)],
        compiler_params=pltpu.CompilerParams(vmem_limit_bytes=VMEM_LIMIT),
        cost_estimate=pl.CostEstimate(
            flops=2 * length * width * (4 * width + 2 * length),
            transcendentals=heads * length * length,
            bytes_accessed=12 * length * width + 8 * width * width,
        ),
        name="attend",
    )(*args)


def feed_kernel(
    place_ref, mid0_ref, mid1_ref, cot_ref, weight_ref, wu_ref, bu_ref, wd_ref, bd_ref, gain_ref,
    shift_ref, act_s_ref, act_k_ref, slope_s_ref, slope_k_ref, low_ref, result_ref, grad_ref,
    grad_low_ref, sums_ref, stat_ref, *, half_tiles,
):
    step = pl.program_id(0)
    half = act_s_ref.shape[1]
    core = place_ref[0]
    middle = jnp.where(step < half_tiles, mid0_ref[...], mid1_ref[...])
    middle_low = middle.astype(LOW)
    low_ref[...] = middle_low
    feed = jnp.zeros_like(middle) + bd_ref[...]
    for part, (act_ref, slope_ref) in enumerate(((act_s_ref, slope_s_ref), (act_k_ref, slope_k_ref))):
        base = (1 - core if part == 0 else core) * half
        for start in range(0, half, HIDDEN_STEP):
            place = pl.ds(pl.multiple_of(base + start, HIDDEN_STEP), HIDDEN_STEP)
            here = pl.ds(start, HIDDEN_STEP)
            hidden = nn(middle_low, wu_ref[:, place]) + bu_ref[:, place]
            active, slope = gelu_pair(hidden)
            active = active.astype(LOW)
            act_ref[:, here] = active
            slope_ref[:, here] = slope.astype(LOW)
            feed = feed + nn(active, wd_ref[place, :])
    total_in = middle + feed
    center = total_in - jnp.mean(total_in, axis=1, keepdims=True)
    rstd = lax.rsqrt(jnp.mean(center * center, axis=1, keepdims=True) + EPSILON)
    normal = center * rstd
    gain = gain_ref[...]
    result = normal * gain + shift_ref[...]
    result_ref[...] = result.astype(LOW)
    weight = weight_ref[...]
    grad_result = cot_ref[...].astype(WIDE) * weight
    pulled = grad_result * gain
    grad = rstd * (
        pulled
        - jnp.mean(pulled, axis=1, keepdims=True)
        - normal * jnp.mean(pulled * normal, axis=1, keepdims=True)
    )
    grad_ref[...] = grad
    grad_low = grad.astype(LOW)
    grad_low_ref[...] = grad_low

    @pl.when(step == 0)
    def _():
        sums_ref[...] = jnp.zeros_like(sums_ref)
        stat_ref[...] = jnp.zeros_like(stat_ref)

    sums_ref[0:1, :] += jnp.sum(grad_result * normal, axis=0, keepdims=True)
    sums_ref[1:2, :] += jnp.sum(grad_result, axis=0, keepdims=True)
    sums_ref[2:3, :] += jnp.sum(grad_low.astype(WIDE), axis=0, keepdims=True)
    stat_ref[0:1, :] += jnp.broadcast_to(total(weight, feed), (1, 128))
    stat_ref[1:2, :] += jnp.broadcast_to(total(weight, result), (1, 128))


def feed_forward(place, mids, cot, weight_col, wu, bu, wd, bd, gain, shift):
    length, width = mids[0].shape
    rows = length * len(mids)
    tile = 256
    steps = rows // tile
    half_tiles = steps // 2
    hidden = wu.shape[1]
    half = hidden // 2

    def tiled(columns):
        return pl.BlockSpec((tile, columns), lambda i, *_: (i, 0))

    args = (mids[0], mids[1], cot, weight_col, wu, bu, wd, bd, gain, shift)
    in_specs = [
        pl.BlockSpec((tile, width), lambda i, *_: (jnp.minimum(i, half_tiles - 1), 0)),
        pl.BlockSpec((tile, width), lambda i, *_: (jnp.maximum(i - half_tiles, 0), 0)),
        tiled(width),
        tiled(1),
    ] + [whole(arg.shape) for arg in args[4:]]
    shapes = (
        jax.ShapeDtypeStruct((rows, half), LOW),
        jax.ShapeDtypeStruct((rows, half), LOW),
        jax.ShapeDtypeStruct((rows, half), LOW),
        jax.ShapeDtypeStruct((rows, half), LOW),
        jax.ShapeDtypeStruct((rows, width), LOW),
        jax.ShapeDtypeStruct((rows, width), LOW),
        jax.ShapeDtypeStruct((rows, width), WIDE),
        jax.ShapeDtypeStruct((rows, width), LOW),
        jax.ShapeDtypeStruct((8, width), WIDE),
        jax.ShapeDtypeStruct((8, 128), WIDE),
    )
    out_specs = tuple(
        tiled(shape.shape[1]) if shape.shape[0] == rows else whole(shape.shape) for shape in shapes
    )
    return pl.pallas_call(
        functools.partial(feed_kernel, half_tiles=half_tiles),
        out_shape=shapes,
        grid_spec=pltpu.PrefetchScalarGridSpec(
            num_scalar_prefetch=1, grid=(steps,), in_specs=in_specs, out_specs=out_specs
        ),
        compiler_params=pltpu.CompilerParams(
            vmem_limit_bytes=VMEM_LIMIT, dimension_semantics=("arbitrary",)
        ),
        cost_estimate=pl.CostEstimate(
            flops=4 * rows * width * hidden,
            transcendentals=2 * rows * hidden,
            bytes_accessed=rows * (4 * hidden + 16 * width) + 4 * width * hidden,
        ),
        name="feed_forward",
    )(place, *args)


def feed_back_kernel(
    place_ref, grad_low_ref, grad_ref, slope_s_ref, slope_k_ref, norm0_ref, norm1_ref, rstd0_ref,
    rstd1_ref, wu_ref, wd_ref, wo_ref, gain_ref, hid_s_ref, hid_k_ref, grad_one_ref, attn_ref,
    ctx_ref, up_sums_ref, sums_ref, *, half_tiles,
):
    step = pl.program_id(0)
    half = hid_s_ref.shape[1]
    core = place_ref[0]

    @pl.when(step == 0)
    def _():
        up_sums_ref[...] = jnp.zeros_like(up_sums_ref)
        sums_ref[...] = jnp.zeros_like(sums_ref)

    grad_low = grad_low_ref[...]
    grad_middle = grad_ref[...]
    for part, (hid_ref, slope_ref) in enumerate(((hid_s_ref, slope_s_ref), (hid_k_ref, slope_k_ref))):
        base = (1 - core if part == 0 else core) * half
        for start in range(0, half, HIDDEN_STEP):
            place = pl.ds(pl.multiple_of(base + start, HIDDEN_STEP), HIDDEN_STEP)
            here = pl.ds(start, HIDDEN_STEP)
            grad_act = nt(grad_low, wd_ref[place, :])
            grad_hidden = (grad_act * slope_ref[:, here].astype(WIDE)).astype(LOW)
            hid_ref[:, here] = grad_hidden
            up_sums_ref[0:1, place] += jnp.sum(grad_hidden.astype(WIDE), axis=0, keepdims=True)
            grad_middle = grad_middle + nt(grad_hidden, wu_ref[:, place])
    first = step < half_tiles
    normal = jnp.where(first, norm0_ref[...].astype(WIDE), norm1_ref[...].astype(WIDE))
    rstd = jnp.where(first, rstd0_ref[...], rstd1_ref[...])
    pulled = grad_middle * gain_ref[...]
    grad_one = rstd * (
        pulled
        - jnp.mean(pulled, axis=1, keepdims=True)
        - normal * jnp.mean(pulled * normal, axis=1, keepdims=True)
    )
    grad_one_ref[...] = grad_one
    attn = grad_one.astype(LOW)
    attn_ref[...] = attn
    ctx_ref[...] = nt(attn, wo_ref[...]).astype(LOW)
    sums_ref[0:1, :] += jnp.sum(grad_middle * normal, axis=0, keepdims=True)
    sums_ref[1:2, :] += jnp.sum(grad_middle, axis=0, keepdims=True)
    sums_ref[2:3, :] += jnp.sum(attn.astype(WIDE), axis=0, keepdims=True)


def feed_back(place, grad_low, grad, slope_s, slope_k, norms, rstds, wu, wd, wo, gain):
    rows, width = grad.shape
    tile = 256
    steps = rows // tile
    half_tiles = steps // 2
    hidden = wu.shape[1]
    half = hidden // 2

    def tiled(columns):
        return pl.BlockSpec((tile, columns), lambda i, *_: (i, 0))

    def first(columns):
        return pl.BlockSpec((tile, columns), lambda i, *_: (jnp.minimum(i, half_tiles - 1), 0))

    def second(columns):
        return pl.BlockSpec((tile, columns), lambda i, *_: (jnp.maximum(i - half_tiles, 0), 0))

    args = (
        grad_low, grad, slope_s, slope_k, norms[0], norms[1], rstds[0], rstds[1], wu, wd, wo, gain,
    )
    in_specs = [
        tiled(width), tiled(width), tiled(half), tiled(half), first(width), second(width),
        first(1), second(1),
    ] + [whole(arg.shape) for arg in args[8:]]
    shapes = (
        jax.ShapeDtypeStruct((rows, half), LOW),
        jax.ShapeDtypeStruct((rows, half), LOW),
        jax.ShapeDtypeStruct((rows, width), WIDE),
        jax.ShapeDtypeStruct((rows, width), LOW),
        jax.ShapeDtypeStruct((rows, width), LOW),
        jax.ShapeDtypeStruct((8, hidden), WIDE),
        jax.ShapeDtypeStruct((8, width), WIDE),
    )
    out_specs = tuple(
        tiled(shape.shape[1]) if shape.shape[0] == rows else whole(shape.shape) for shape in shapes
    )
    return pl.pallas_call(
        functools.partial(feed_back_kernel, half_tiles=half_tiles),
        out_shape=shapes,
        grid_spec=pltpu.PrefetchScalarGridSpec(
            num_scalar_prefetch=1, grid=(steps,), in_specs=in_specs, out_specs=out_specs
        ),
        compiler_params=pltpu.CompilerParams(
            vmem_limit_bytes=VMEM_LIMIT, dimension_semantics=("arbitrary",)
        ),
        cost_estimate=pl.CostEstimate(
            flops=4 * rows * width * hidden + 2 * rows * width * width,
            transcendentals=0,
            bytes_accessed=rows * (4 * hidden + 16 * width) + 4 * width * hidden,
        ),
        name="feed_back",
    )(place, *args)


def attend_back_kernel(
    q_ref, k_ref, v_ref, ctx_ref, grad_ctx_ref, lse_ref, seg_ref, mark_ref, grad_one_ref, wq_ref,
    wk_ref, wv_ref, dq_ref, dk_ref, dv_ref, grad_in_ref, sums_ref, bias_ref,
):
    fill_bias(bias_ref, seg_ref[...], mark_ref[...])
    width = 2 * HEAD_DIM
    pairs = q_ref.shape[1] // width

    def pair_step(pair, carried):
        lanes = pl.ds(pl.multiple_of(pair * width, width), width)
        q, k, v, grad = q_ref[:, lanes], k_ref[:, lanes], v_ref[:, lanes], grad_ctx_ref[:, lanes]
        k_turned = k.T
        shared = (grad.astype(WIDE) * ctx_ref[:, lanes].astype(WIDE)).T
        part_q, part_k, part_v = [], [], []
        for half in range(2):
            inside = slice(half * HEAD_DIM, (half + 1) * HEAD_DIM)
            delta = jnp.sum(shared[inside], axis=0, keepdims=True)
            scores = nt(k * lane_half(half), q) + bias_ref[...]
            chances = jnp.exp(scores - lse_ref[pl.ds(pair * 2 + half, 1), :])
            part_v.append(nn(chances.astype(LOW), grad))
            grad_chances = nt(v * lane_half(half), grad)
            grad_scores = (chances * (grad_chances - delta)).astype(LOW)
            part_k.append(nn(grad_scores, q))
            part_q.append(nn(k_turned[inside], grad_scores))
        first = lax.broadcasted_iota(jnp.int32, part_k[0].shape, 1) < HEAD_DIM
        dq_ref[:, lanes] = jnp.concatenate(part_q, axis=0).T.astype(LOW)
        dk_ref[:, lanes] = jnp.where(first, part_k[0], part_k[1]).astype(LOW)
        dv_ref[:, lanes] = jnp.where(first, part_v[0], part_v[1]).astype(LOW)
        return carried

    lax.fori_loop(0, pairs, pair_step, 0)
    dq, dk, dv = dq_ref[...], dk_ref[...], dv_ref[...]
    grad_in_ref[...] = (
        grad_one_ref[...]
        + nt(dq, wq_ref[...]) * SCORE_SCALE
        + nt(dk, wk_ref[...])
        + nt(dv, wv_ref[...])
    )
    sums_ref[...] = jnp.concatenate(
        [
            jnp.sum(dq.astype(WIDE), axis=0, keepdims=True) * SCORE_SCALE,
            jnp.sum(dv.astype(WIDE), axis=0, keepdims=True),
            jnp.zeros((6, dq.shape[1]), WIDE),
        ],
        axis=0,
    )


def attend_back(slot, q, k, v, ctx, grad_ctx, lse, seg_row, mark_col, grad_one, wq, wk, wv):
    length, width = q.shape
    heads = width // HEAD_DIM
    shapes = (
        jax.ShapeDtypeStruct((length, width), LOW),
        jax.ShapeDtypeStruct((length, width), LOW),
        jax.ShapeDtypeStruct((length, width), LOW),
        jax.ShapeDtypeStruct((length, width), WIDE),
        jax.ShapeDtypeStruct((8, width), WIDE),
    )
    args = (q, k, v, ctx, grad_ctx, lse, seg_row, mark_col, grad_one, wq, wk, wv)
    picked = pl.BlockSpec((length, width), lambda i: (slot, 0), pipeline_mode=pl.Buffered(1))
    in_specs = [
        picked if arg is grad_ctx or arg is grad_one else whole(arg.shape) for arg in args
    ]
    return pl.pallas_call(
        attend_back_kernel,
        grid=(1,),
        out_shape=shapes,
        in_specs=in_specs,
        out_specs=tuple(whole(shape.shape) for shape in shapes),
        scratch_shapes=[pltpu.VMEM((length, length), WIDE)],
        compiler_params=pltpu.CompilerParams(
            vmem_limit_bytes=VMEM_LIMIT, dimension_semantics=("arbitrary",)
        ),
        cost_estimate=pl.CostEstimate(
            flops=2 * length * width * (3 * width + 5 * length),
            transcendentals=heads * length * length,
            bytes_accessed=24 * length * width + 6 * width * width,
        ),
        name="attend_back",
    )(*args)


def after(value, *earlier):
    return lax.optimization_barrier((value,) + earlier)[0]


def own_pieces(value, slot, slots):
    count = lax.axis_size("seq")
    me = lax.axis_index("seq")
    pieces = [lax.dynamic_index_in_dim(value, me * slots + slot, 0, keepdims=False)]
    for shift in range(1, count):
        target = (me + shift) % count
        block = lax.dynamic_index_in_dim(value, target * slots + slot, 0, keepdims=False)
        pairs = [(source, (source + shift) % count) for source in range(count)]
        pieces.append(lax.ppermute(block, "seq", pairs))
    return pieces


def return_pieces(pieces, link_type):
    count = lax.axis_size("seq")
    me = lax.axis_index("seq")
    slots = pieces[0].shape[0]
    out = jnp.zeros((slots * count,) + pieces[0].shape[1:], pieces[0].dtype)
    out = lax.dynamic_update_slice_in_dim(out, pieces[0], me * slots, 0)
    for shift in range(1, count):
        pairs = [(source, (source - shift) % count) for source in range(count)]
        got = lax.ppermute(pieces[shift].astype(link_type), "seq", pairs).astype(out.dtype)
        out = lax.dynamic_update_slice_in_dim(out, got, ((me + shift) % count) * slots, 0)
    return out


def swap(value, axis, bit):
    count = lax.axis_size(axis)
    return lax.ppermute(value, axis, [(source, source ^ bit) for source in range(count)])


def bit_of(axis, bit):
    return (lax.axis_index(axis) // bit) % 2


def chip_orders():
    dp, seq = lax.axis_size("dp"), lax.axis_size("seq")
    along_dp = [("dp", 2**i) for i in range(1, dp.bit_length() - 1)]
    along_seq = [("seq", 2**i) for i in range(seq.bit_length() - 1)]
    x, z, y = along_dp[0], along_dp[1], along_seq[0]
    rest = along_dp[2:] + along_seq[1:]
    return [x, y, z] + rest, [y, z, x] + rest, [z, x, y] + rest


HALVINGS = 4


def scatter_sum(first, second, order):
    for axis, bit in order[:HALVINGS]:
        half = first.shape[0] // 2
        mine = bit_of(axis, bit)

        def part(which):
            a = lax.dynamic_slice_in_dim(first, which * half, half, 0).astype(WIDE)
            b = lax.dynamic_slice_in_dim(second, which * half, half, 0).astype(WIDE)
            return (a + b).astype(LOW)

        second_next = swap(part(1 - mine), axis, bit)
        first, second = part(mine), second_next
    share = (first.astype(WIDE) + second.astype(WIDE)).astype(LOW)
    for axis, bit in order[HALVINGS:]:
        share = (share.astype(WIDE) + swap(share, axis, bit).astype(WIDE)).astype(LOW)
    return share


def gather_shares(share, order):
    for axis, bit in reversed(order[:HALVINGS]):
        share = jnp.concatenate([share, swap(share, axis, bit)], axis=0)
    return share


def place_in(order):
    place = 0
    for axis, bit in order[:HALVINGS]:
        place = place * 2 + bit_of(axis, bit)
    return place


def finish_down_kernel(place_ref, own_ref, other_ref, out_ref):
    half, tile = pl.program_id(0), pl.program_id(1)
    block = own_ref.shape[0] >> HALVINGS
    for j in range(out_ref.shape[0] // block):
        inside = tile * (out_ref.shape[0] // block) + j
        spot = pl.multiple_of((inside ^ place_ref[1]) * block, block)
        own, other = own_ref[pl.ds(spot, block), :], other_ref[pl.ds(spot, block), :]
        out_ref[j * block : (j + 1) * block, :] = jnp.where(
            place_ref[0] == half, own.astype(WIDE), other.astype(WIDE)
        )


def finish_up_kernel(place_ref, own_ref, other_ref, out_ref):
    half, tile = pl.program_id(0), pl.program_id(1)
    block = own_ref.shape[0] >> HALVINGS
    found = []
    for j in range(out_ref.shape[1] // block):
        inside = tile * (out_ref.shape[1] // block) + j
        spot = pl.multiple_of((inside ^ place_ref[1]) * block, block)
        own, other = own_ref[pl.ds(spot, block), :], other_ref[pl.ds(spot, block), :]
        found.append(jnp.where(place_ref[0] == half, own.astype(WIDE), other.astype(WIDE)))
    out_ref[...] = jnp.concatenate(found, axis=0).T


def finish(place, own, other, turned):
    rows, width = own.shape
    tile = rows // 4
    if turned:
        shape = (width, 2 * rows)
        spec = pl.BlockSpec((width, tile), lambda h, t, *_: (0, h * 4 + t))
    else:
        shape = (2 * rows, width)
        spec = pl.BlockSpec((tile, width), lambda h, t, *_: (h * 4 + t, 0))
    return pl.pallas_call(
        finish_up_kernel if turned else finish_down_kernel,
        out_shape=jax.ShapeDtypeStruct(shape, WIDE),
        grid_spec=pltpu.PrefetchScalarGridSpec(
            num_scalar_prefetch=1,
            grid=(2, 4),
            in_specs=[whole(own.shape), whole(other.shape)],
            out_specs=spec,
        ),
        compiler_params=pltpu.CompilerParams(vmem_limit_bytes=VMEM_LIMIT),
        cost_estimate=pl.CostEstimate(
            flops=0, transcendentals=0, bytes_accessed=12 * rows * width
        ),
        name="finish",
    )(place, own, other)


def finish_square_kernel(place_ref, *refs):
    parts = (len(refs) - 4) // 2
    own_refs, other_refs, out_refs = refs[:parts], refs[parts : 2 * parts], refs[2 * parts :]
    rows_each, width = own_refs[0].shape
    block = rows_each >> HALVINGS
    core = place_ref[0]
    for half in range(2):
        for row in range(0, rows_each * parts, block):
            part = row // rows_each
            inside = (row - part * rows_each) // block
            spot = pl.multiple_of((inside ^ place_ref[1 + part]) * block, block)
            own = own_refs[part][pl.ds(spot, block), :].astype(WIDE)
            other = other_refs[part][pl.ds(spot, block), :].astype(WIDE)
            out = out_refs[half * 2 + row // width]
            out[row % width : row % width + block, :] = jnp.where(core == half, own, other)


def finish_square(place, owns, others):
    width = owns[0].shape[1]
    shape = jax.ShapeDtypeStruct((width, width), WIDE)
    args = (*owns, *others)
    return pl.pallas_call(
        finish_square_kernel,
        out_shape=(shape,) * 4,
        grid_spec=pltpu.PrefetchScalarGridSpec(
            num_scalar_prefetch=1,
            grid=(1,),
            in_specs=[whole(arg.shape) for arg in args],
            out_specs=(whole(shape.shape),) * 4,
        ),
        compiler_params=pltpu.CompilerParams(vmem_limit_bytes=VMEM_LIMIT),
        cost_estimate=pl.CostEstimate(
            flops=0, transcendentals=0, bytes_accessed=24 * width * width
        ),
        name="finish_square",
    )(place, *args)


def on_device(
    inputs, cotangent, w_query, b_query, w_key, w_value, b_value, w_out, b_out, gain_one,
    shift_one, w_up, b_up, w_down, b_down, gain_two, shift_two, live_counts, valid_mask, segments,
):
    seqs, piece, width = inputs.shape
    count = lax.axis_size("seq")
    slots = seqs // count
    length = piece * count
    rows = slots * length
    core = bit_of("dp", 1).astype(jnp.int32)
    orders = chip_orders()
    places = [place_in(order).astype(jnp.int32) for order in orders]
    core_place = core.reshape(1)

    def row_of(vector):
        return vector.astype(WIDE).reshape(1, -1)

    live = (jnp.arange(seqs) < live_counts[0]).astype(jnp.int32)
    code = segments * 2 + valid_mask * live[:, None]
    codes = jnp.stack([jnp.concatenate(own_pieces(code, slot, slots)) for slot in range(slots)])
    seg = codes // 2
    weight = codes % 2
    mark = jnp.where(weight > 0, seg, -1)
    x_slots = []
    for slot in range(slots):
        value = inputs if slot == 0 else after(inputs, x_slots[-1])
        x_slots.append(jnp.concatenate(own_pieces(value, slot, slots)))
    weight_col = weight.astype(WIDE).reshape(rows, 1)

    bq, bv, bo = row_of(b_query), row_of(b_value), row_of(b_out)
    gain1, shift1 = row_of(gain_one), row_of(shift_one)
    gain2, shift2 = row_of(gain_two), row_of(shift_two)
    bu, bd = row_of(b_up), row_of(b_down)

    seg_rows = [seg[slot].reshape(1, length) for slot in range(slots)]
    mark_cols = [mark[slot].reshape(length, 1) for slot in range(slots)]
    forward = [
        attend(
            x_slots[slot], seg_rows[slot], mark_cols[slot], w_query, bq, w_key, w_value, bv,
            w_out, bo, gain1, shift1,
        )
        for slot in range(slots)
    ]
    late_cot = after(cotangent, x_slots[-1])
    cot_all = jnp.concatenate(
        [piece_of for slot in range(slots) for piece_of in own_pieces(late_cot, slot, slots)]
    )
    (act_s, act_k, slope_s, slope_k, mid_low, result, grad_h2, grad_feed, sums_two, stat_two) = (
        feed_forward(
            core_place, [each[5] for each in forward], cot_all, weight_col, w_up, bu, w_down, bd,
            gain2, shift2,
        )
    )
    down_got = swap(tn(act_s, grad_feed).astype(LOW), "dp", 1)
    down_kept = tn(act_k, grad_feed).astype(LOW)
    down_share = scatter_sum(down_kept, down_got, orders[0])
    down_own = gather_shares(down_share, orders[0])
    down_other = swap(down_own, "dp", 1)
    grad_w_down = finish(jnp.stack([core, places[0]]), down_own, down_other, False)

    result = result.reshape(slots, length, width)
    result_out = return_pieces(
        [result[:, i * piece : (i + 1) * piece] for i in range(count)], LOW
    )

    hid_s, hid_k, grad_h1, grad_attn, grad_ctx, up_sums, sums_one = feed_back(
        core_place, grad_feed, grad_h2, slope_s, slope_k, [each[6] for each in forward],
        [each[7] for each in forward], w_up, w_down, w_out, gain1,
    )
    up_got = swap(tn(hid_s, mid_low).astype(LOW), "dp", 1)
    up_kept = tn(hid_k, mid_low).astype(LOW)
    up_share = scatter_sum(up_kept, up_got, orders[1])
    up_own = gather_shares(up_share, orders[1])
    up_other = swap(up_own, "dp", 1)
    grad_w_up = finish(jnp.stack([core, places[1]]), up_own, up_other, True)

    ctx_all = jnp.concatenate([each[3] for each in forward], axis=0)
    grad_w_out = tn(ctx_all, grad_attn).astype(LOW)
    backward = [
        attend_back(
            slot, *forward[slot][:4], grad_ctx, forward[slot][4], seg_rows[slot],
            mark_cols[slot], grad_h1, w_query, w_key, w_value,
        )
        for slot in range(slots)
    ]
    x_rows = jnp.concatenate(x_slots)
    dq, dk, dv = (jnp.concatenate([each[i] for each in backward], axis=0) for i in range(3))
    low_half = jnp.concatenate(
        [(tn(x_rows, dq) * SCORE_SCALE).astype(LOW), tn(x_rows, dk).astype(LOW)]
    )
    high_half = jnp.concatenate([tn(x_rows, dv).astype(LOW), grad_w_out])
    square_got = swap(jnp.where(core == 0, high_half, low_half), "dp", 1)
    square_kept = jnp.where(core == 0, low_half, high_half)
    parts = len(orders)
    each_rows = square_kept.shape[0] // parts
    square_own, square_other = [], []
    for part, order in enumerate(orders):
        inside = slice(part * each_rows, (part + 1) * each_rows)
        share = scatter_sum(square_kept[inside], square_got[inside], order)
        square_own.append(gather_shares(share, order))
        square_other.append(swap(square_own[-1], "dp", 1))
    squares = finish_square(jnp.stack([core] + places), square_own, square_other)

    stats = [
        sum(each[8][0, 0] for each in forward),
        sum(each[8][1, 0] for each in forward),
        stat_two[0, 0],
        stat_two[1, 0],
        jnp.sum(weight).astype(WIDE),
    ]
    stats = jnp.concatenate([jnp.stack(stats), jnp.zeros((width - 5,), WIDE)]).reshape(1, width)
    small = jnp.concatenate(
        [
            sum(each[4][0:2] for each in backward),
            sums_one[0:3],
            sums_two[0:3],
            stats,
            up_sums[0:1].reshape(-1, width),
        ],
        axis=0,
    )
    for axis, bit in [("dp", 1)] + orders[0]:
        small = small + swap(small, axis, bit)
    rms_values = jnp.sqrt(small[8, :4] / (width * small[8, 4]))

    grad_inputs = jnp.stack([each[3] for each in backward])
    grad_out = return_pieces(
        [grad_inputs[:, i * piece : (i + 1) * piece] for i in range(count)], LOW
    )
    return (
        result_out,
        grad_out,
        squares[0],
        small[0],
        squares[1],
        squares[2],
        small[1],
        squares[3],
        small[4],
        small[2],
        small[3],
        grad_w_up,
        small[9:].reshape(-1),
        grad_w_down,
        small[7],
        small[5],
        small[6],
        rms_values,
    )


def solution(mesh):
    split = P("dp", "seq", None)
    pair = P("dp", "seq")
    return jax.shard_map(
        on_device,
        mesh=mesh,
        in_specs=(split, split) + (P(),) * 15 + (P("dp"), pair, pair),
        out_specs=(split, split) + (P(),) * 16,
        check_vma=False,
    )
```

```python
import functools

import jax
import jax.numpy as jnp
from jax import lax
from jax.experimental import pallas as pl
from jax.experimental.pallas import tpu as pltpu
from jax.sharding import PartitionSpec as P

HEAD_DIM = 64
EPSILON = 1e-05
NEGATIVE = -1e30
SCORE_SCALE = 0.125
LOW = jnp.bfloat16
WIDE = jnp.float32
VMEM_LIMIT = 56 * 1024 * 1024
HIDDEN_STEP = 512
TILE = 256
ROWS = 32
ROWS_NORM = 16
ANY = pl.BlockSpec(memory_space=pl.ANY)
IN_VMEM = pl.BlockSpec(memory_space=pltpu.VMEM)
IN_SMEM = pl.BlockSpec(memory_space=pltpu.SMEM)

ERF_P = 0.3275911
ERF_C = (0.254829592, -0.284496736, 1.421413741, -1.453152027, 1.061405429)
ROOT_HALF = 0.7071067811865476
DENSITY = 0.3989422804014327


def nn(left, right):
    return jnp.dot(left, right, preferred_element_type=WIDE)


def nt(left, right):
    return lax.dot_general(
        left, right, (((1,), (1,)), ((), ())), preferred_element_type=WIDE
    )


def tn(left, right):
    return lax.dot_general(
        left, right, (((0,), (0,)), ((), ())), preferred_element_type=WIDE
    )


def gelu_pair(hidden):
    tail_exp = jnp.exp(hidden * hidden * -0.5)
    slow = 1.0 + (ERF_P * ROOT_HALF) * jnp.abs(hidden)
    t = pl.reciprocal(slow, approx=True)
    t = t * (2.0 - slow * t)
    c1, c2, c3, c4, c5 = (0.5 * c for c in ERF_C)
    tail = ((((c5 * t + c4) * t + c3) * t + c2) * t + c1) * t * tail_exp
    below = jnp.where(hidden >= 0.0, 1.0 - tail, tail)
    return hidden * below, below + hidden * (DENSITY * tail_exp)


def lane_half(half):
    lane = lax.broadcasted_iota(jnp.int32, (1, 2 * HEAD_DIM), 1)
    inside = (lane < HEAD_DIM) if half == 0 else (lane >= HEAD_DIM)
    return inside.astype(WIDE).astype(LOW)


def fill_bias(bias_ref, seg_row, mark_col):
    length = bias_ref.shape[0]
    key_place = lax.broadcasted_iota(jnp.int32, (length, length), 0)
    query_place = lax.broadcasted_iota(jnp.int32, (length, length), 1)
    visible = (mark_col == seg_row) | (key_place == query_place)
    bias_ref[...] = jnp.where(visible, 0.0, NEGATIVE)


def total(rows_weight, values):
    per_row = jnp.sum(values * values, axis=1, keepdims=True) * rows_weight
    return jnp.sum(per_row, axis=0, keepdims=True)


def column(row):
    return jnp.broadcast_to(row.astype(WIDE), (8, row.shape[1])).T[:, 0:1]


VECTORS = ("b_query", "b_value", "b_out", "gain_one", "shift_one", "b_down", "gain_two", "shift_two")


def vector(ref, name):
    place = VECTORS.index(name)
    return ref[place : place + 1, :]


def attend_kernel(
    x_ref, seg_ref, mark_ref, vectors_ref, wq_ref, wk_ref, wv_ref, wo_ref,
    q_ref, k_ref, v_ref, ctx_ref, lse_ref, mid_ref, norm_ref, rstd_ref, stat_ref,
    wq_s, wk_s, wv_s, wo_s, q_s, k_s, v_s, bias_s, score_s, chance_s, weight_s, in_sems, out_sems,
    *, slot,
):
    loads = [
        pltpu.make_async_copy(a, b, in_sems.at[n])
        for n, (a, b) in enumerate(
            ((wk_ref, wk_s), (wq_ref, wq_s), (wv_ref, wv_s), (wo_ref, wo_s))
        )
    ]
    for load in loads:
        load.start()
    stores = [
        pltpu.make_async_copy(a, b, out_sems.at[n])
        for n, (a, b) in enumerate(((k_s, k_ref), (q_s, q_ref), (v_s, v_ref)))
    ]
    mark_col = column(mark_ref[slot : slot + 1, :])
    weight_s[...] = (mark_col >= 0).astype(WIDE)
    fill_bias(bias_s, seg_ref[slot : slot + 1, :].astype(WIDE), mark_col)
    length, model = x_ref.shape
    heads = model // HEAD_DIM
    width = 2 * HEAD_DIM
    loads[0].wait()
    k_s[...] = nn(x_ref[...], wk_s[...]).astype(LOW)
    stores[0].start()
    loads[1].wait()
    q_s[...] = ((nn(x_ref[...], wq_s[...]) + vector(vectors_ref, "b_query")) * SCORE_SCALE).astype(LOW)
    stores[1].start()
    loads[2].wait()
    v_s[...] = (nn(x_ref[...], wv_s[...]) + vector(vectors_ref, "b_value")).astype(LOW)
    stores[2].start()

    def lanes(head):
        return pl.ds(head // 2 * width, width)

    def scores(head):
        keys = k_s[:, lanes(head)] * lane_half(head % 2)
        score_s[head % 2] = nt(keys, q_s[:, lanes(head)])

    def soften(head):
        here, chance = score_s.at[head % 2], chance_s.at[head % 2]
        top = jnp.full((8, length), NEGATIVE, WIDE)
        for row in range(0, length, ROWS):
            block = here[row : row + ROWS, :] + bias_s[row : row + ROWS, :]
            here[row : row + ROWS, :] = block
            top = jnp.maximum(top, jnp.max(block.reshape(-1, 8, length), axis=0))
        top = jnp.max(top, axis=0, keepdims=True)
        amount = jnp.zeros((8, length), WIDE)
        for row in range(0, length, ROWS):
            block = jnp.exp(here[row : row + ROWS, :] - top)
            chance[row : row + ROWS, :] = block.astype(LOW)
            amount = amount + jnp.sum(block.reshape(-1, 8, length), axis=0)
        amount = jnp.sum(amount, axis=0, keepdims=True)
        lse_ref[head : head + 1, :] = top + jnp.log(amount)
        return 1.0 / amount

    def combine(head, share, turned):
        part = turned[head % 2 * HEAD_DIM : (head % 2 + 1) * HEAD_DIM]
        summed = nn(part, chance_s[head % 2]) * share
        ctx_ref[head * HEAD_DIM : (head + 1) * HEAD_DIM, :] = summed.astype(LOW)

    scores(0)
    waiting = None
    for head in range(heads):
        share = soften(head)
        if head % 2 == 0:
            turned = v_s[:, lanes(head)].T
        if head + 1 < heads:
            scores(head + 1)
        if waiting is not None:
            combine(*waiting)
        waiting = (head, share, turned)
    combine(*waiting)
    loads[3].wait()
    attention_all = tn(ctx_ref[...], wo_s[...])
    bias, gain, shift = (vector(vectors_ref, n) for n in ("b_out", "gain_one", "shift_one"))
    stats = [jnp.zeros((1, 1), WIDE) for _ in range(2)]
    for row in range(0, length, ROWS_NORM):
        at = pl.ds(row, ROWS_NORM)
        attention = attention_all[row : row + ROWS_NORM] + bias
        rows = x_ref[at, :].astype(WIDE)
        total_in = rows + attention
        center = total_in - jnp.mean(total_in, axis=1, keepdims=True)
        rstd = lax.rsqrt(jnp.mean(center * center, axis=1, keepdims=True) + EPSILON)
        normal = center * rstd
        mid_ref[at, :] = normal * gain + shift
        norm_ref[at, :] = normal.astype(LOW)
        rstd_ref[at, :] = rstd
        row_weight = weight_s[at, :]
        stats[0] = stats[0] + total(row_weight, rows)
        stats[1] = stats[1] + total(row_weight, attention)
    stat_ref[...] = jnp.concatenate(
        [jnp.broadcast_to(stat, (1, 128)) for stat in stats] + [jnp.zeros((6, 128), WIDE)], axis=0
    )
    for store in stores:
        store.wait()


def cost(flops):
    return pl.CostEstimate(flops=flops, transcendentals=0, bytes_accessed=0)


def ignoring(kernel, inputs, extra):
    def wrapped(*refs):
        return kernel(*refs[:inputs], *refs[inputs + extra :])

    return wrapped


def whole(shape):
    return pl.BlockSpec(shape, lambda *_: (0,) * len(shape), pipeline_mode=pl.Buffered(1))


def attend(slot, x, segs, marks, vectors, wq, wk, wv, wo):
    length, width = x.shape
    heads = width // HEAD_DIM
    lse_rows = heads + (-heads) % 8
    shapes = (
        jax.ShapeDtypeStruct((length, width), LOW),
        jax.ShapeDtypeStruct((length, width), LOW),
        jax.ShapeDtypeStruct((length, width), LOW),
        jax.ShapeDtypeStruct((width, length), LOW),
        jax.ShapeDtypeStruct((lse_rows, length), WIDE),
        jax.ShapeDtypeStruct((length, width), WIDE),
        jax.ShapeDtypeStruct((length, width), LOW),
        jax.ShapeDtypeStruct((length, 1), WIDE),
        jax.ShapeDtypeStruct((8, 128), WIDE),
    )
    args = (x, segs, marks, vectors, wq, wk, wv, wo)
    weight = pltpu.VMEM((width, width), LOW)
    tokens = pltpu.VMEM((length, width), LOW)
    return pl.pallas_call(
        functools.partial(attend_kernel, slot=slot),
        out_shape=shapes,
        in_specs=[IN_VMEM] * 4 + [ANY] * 4,
        out_specs=(ANY,) * 3 + (IN_VMEM,) * 6,
        scratch_shapes=[weight] * 4 + [tokens] * 3 + [
            pltpu.VMEM((length, length), WIDE),
            pltpu.VMEM((2, length, length), WIDE),
            pltpu.VMEM((2, length, length), LOW),
            pltpu.VMEM((length, 1), WIDE),
            pltpu.SemaphoreType.DMA((4,)),
            pltpu.SemaphoreType.DMA((3,)),
        ],
        compiler_params=pltpu.CompilerParams(vmem_limit_bytes=VMEM_LIMIT),
        cost_estimate=cost(0),
        name="attend",
    )(*args)


def lane_split(core, half, length):
    return [
        pl.multiple_of(start * half, length) for start in (1 - core, core)
    ]


def norm_back(grad, normal, rstd, gain):
    pulled = grad * gain
    return rstd * (
        pulled
        - jnp.mean(pulled, axis=1, keepdims=True)
        - normal * jnp.mean(pulled * normal, axis=1, keepdims=True)
    )


def row_total(values):
    return jnp.sum(values, axis=0, keepdims=True)


def feed_kernel(
    place_ref, mid0_ref, mid1_ref, cot_ref, mark_ref, bu_ref, vectors_ref, wu_ref, wd_ref,
    slope_ref, low_ref, result_ref, grad_ref, grad_low_ref, send_ref, keep_ref, sums_ref, stat_ref,
    mid_s, cot_s, wu_s, wd_s, act_s, slope_s, low_s, result_s, grad_s, grad_low_s, out_s,
    feed_s, weight_s, in_sems, up_sems, down_sems, tile_sems, out_sems,
):
    length, width = mid0_ref.shape
    rows = cot_ref.shape[0]
    hidden = wu_ref.shape[1]
    half = hidden // 2
    chunks = hidden // HIDDEN_STEP
    tile = TILE
    core = place_ref[0]
    bases = lane_split(core, half, HIDDEN_STEP)

    def place_of(chunk):
        part, inside = divmod(chunk * HIDDEN_STEP, half)
        return pl.ds(pl.multiple_of(bases[part] + inside, HIDDEN_STEP), HIDDEN_STEP)

    def own(chunk):
        return pl.ds(chunk * HIDDEN_STEP, HIDDEN_STEP)

    first_in = pltpu.make_async_copy(mid0_ref, mid_s.at[pl.ds(0, length)], in_sems.at[0])
    second_in = pltpu.make_async_copy(mid1_ref, mid_s.at[pl.ds(length, length)], in_sems.at[1])
    cot_in = pltpu.make_async_copy(cot_ref, cot_s, in_sems.at[2])
    ups = [
        pltpu.make_async_copy(wu_ref.at[:, place_of(c)], wu_s.at[:, own(c)], up_sems.at[c])
        for c in range(chunks)
    ]
    downs = [
        pltpu.make_async_copy(wd_ref.at[place_of(c), :], wd_s.at[own(c), :], down_sems.at[c])
        for c in range(chunks)
    ]
    first_in.start()
    for chunk in range(chunks):
        ups[chunk].start()
        downs[chunk].start()
    cot_in.start()
    second_in.start()
    sums_ref[...] = jnp.zeros_like(sums_ref)
    stat_ref[...] = jnp.zeros_like(stat_ref)
    for slot in range(mark_ref.shape[0]):
        mark_col = column(mark_ref[slot : slot + 1, :])
        weight_s[pl.ds(slot * length, length), :] = (mark_col >= 0).astype(WIDE)

    def tile_copies(index):
        spot = pl.ds(pl.multiple_of(index * tile, tile), tile)
        pairs = (
            (slope_s, slope_ref), (low_s, low_ref), (result_s, result_ref), (grad_s, grad_ref),
            (grad_low_s, grad_low_ref),
        )
        return [
            pltpu.make_async_copy(a.at[spot, :], b.at[spot, :], tile_sems.at[n, index])
            for n, (a, b) in enumerate(pairs)
        ]

    def inside(index, row, count=ROWS):
        return pl.ds(pl.multiple_of(index * tile + row, count), count)

    def work(index, opening):
        spot = pl.ds(pl.multiple_of(index * tile, tile), tile)
        for row in range(0, tile, ROWS):
            low_s[inside(index, row), :] = mid_s[inside(index, row), :].astype(LOW)
        middle_low = low_s[spot, :]

        def up(chunk):
            if opening:
                ups[chunk].wait()
            return nn(middle_low, wu_s[:, own(chunk)])

        def down(chunk, feed):
            if opening:
                downs[chunk].wait()
            more = nn(act_s[spot, own(chunk)], wd_s[own(chunk), :])
            return more if feed is None else feed + more

        feed = None
        ahead = up(0)
        for chunk in range(chunks):
            bias = bu_ref[:, place_of(chunk)]
            for row in range(0, tile, ROWS):
                active, slope = gelu_pair(ahead[row : row + ROWS] + bias)
                act_s[inside(index, row), own(chunk)] = active.astype(LOW)
                slope_s[inside(index, row), own(chunk)] = slope.astype(LOW)
            if chunk + 1 < chunks:
                ahead = up(chunk + 1)
            if chunk > 0:
                feed = down(chunk - 1, feed)
        feed_s[...] = down(chunks - 1, feed)

    def norm(index):
        gain, shift, bias = (vector(vectors_ref, n) for n in ("gain_two", "shift_two", "b_down"))
        sums = [jnp.zeros((1, width), WIDE) for _ in range(3)]
        stats = [jnp.zeros((1, 1), WIDE) for _ in range(2)]
        for row in range(0, tile, ROWS_NORM):
            here = inside(index, row, ROWS_NORM)
            feed_here = feed_s[row : row + ROWS_NORM, :] + bias
            total_in = mid_s[here, :] + feed_here
            center = total_in - jnp.mean(total_in, axis=1, keepdims=True)
            rstd = lax.rsqrt(jnp.mean(center * center, axis=1, keepdims=True) + EPSILON)
            normal = center * rstd
            result = normal * gain + shift
            result_s[here, :] = result.astype(LOW)
            weight = weight_s[here, :]
            grad_result = cot_s[here, :].astype(WIDE) * weight
            grad = norm_back(grad_result, normal, rstd, gain)
            grad_s[here, :] = grad
            grad_low = grad.astype(LOW)
            grad_low_s[here, :] = grad_low
            sums[0] = sums[0] + row_total(grad_result * normal)
            sums[1] = sums[1] + row_total(grad_result)
            sums[2] = sums[2] + row_total(grad_low.astype(WIDE))
            stats[0] = stats[0] + total(weight, feed_here)
            stats[1] = stats[1] + total(weight, result)
        for copy in tile_copies(index):
            copy.start()
        for n in range(3):
            sums_ref[n : n + 1, :] += sums[n]
        for n in range(2):
            stat_ref[n : n + 1, :] += jnp.broadcast_to(stats[n], (1, 128))

    first_in.wait()
    work(0, True)
    second_in.wait()
    cot_in.wait()

    def turn(index, carried):
        norm(index - 1)
        work(index, False)
        return carried

    lax.fori_loop(1, rows // tile, turn, 0)
    norm(rows // tile - 1)
    outer(act_s, grad_low_s, out_s, send_ref, keep_ref, out_sems)
    for index in range(rows // tile):
        for copy in tile_copies(index):
            copy.wait()


def outer(left_s, right_s, out_s, send_ref, keep_ref, sems):
    half = left_s.shape[1] // 2
    steps = left_s.shape[1] // HIDDEN_STEP
    copies = []
    for step in range(steps):
        part, inside = divmod(step * HIDDEN_STEP, half)
        spot = pl.ds(step * HIDDEN_STEP, HIDDEN_STEP)
        out_s[spot, :] = tn(left_s[:, spot], right_s[...]).astype(LOW)
        target = (send_ref, keep_ref)[part].at[pl.ds(inside, HIDDEN_STEP), :]
        copies.append(pltpu.make_async_copy(out_s.at[spot, :], target, sems.at[step]))
        copies[-1].start()
    for copy in copies:
        copy.wait()


def feed_forward(place, mids, cot, marks, wu, bu, wd, vectors):
    length, width = mids[0].shape
    rows = cot.shape[0]
    hidden = wu.shape[1]
    half = hidden // 2
    chunks = hidden // HIDDEN_STEP
    shapes = (
        jax.ShapeDtypeStruct((rows, hidden), LOW),
        jax.ShapeDtypeStruct((rows, width), LOW),
        jax.ShapeDtypeStruct((rows, width), LOW),
        jax.ShapeDtypeStruct((rows, width), WIDE),
        jax.ShapeDtypeStruct((rows, width), LOW),
        jax.ShapeDtypeStruct((half, width), LOW),
        jax.ShapeDtypeStruct((half, width), LOW),
        jax.ShapeDtypeStruct((8, width), WIDE),
        jax.ShapeDtypeStruct((8, 128), WIDE),
    )
    return pl.pallas_call(
        feed_kernel,
        out_shape=shapes,
        in_specs=[IN_SMEM] + [ANY] * 3 + [IN_VMEM] * 3 + [ANY] * 2,
        out_specs=(ANY,) * 7 + (IN_VMEM,) * 2,
        scratch_shapes=[
            pltpu.VMEM((rows, width), WIDE),
            pltpu.VMEM((rows, width), LOW),
            pltpu.VMEM((width, hidden), LOW),
            pltpu.VMEM((hidden, width), LOW),
            pltpu.VMEM((rows, hidden), LOW),
            pltpu.VMEM((rows, hidden), LOW),
            pltpu.VMEM((rows, width), LOW),
            pltpu.VMEM((rows, width), LOW),
            pltpu.VMEM((rows, width), WIDE),
            pltpu.VMEM((rows, width), LOW),
            pltpu.VMEM((hidden, width), LOW),
            pltpu.VMEM((TILE, width), WIDE),
            pltpu.VMEM((rows, 1), WIDE),
            pltpu.SemaphoreType.DMA((3,)),
            pltpu.SemaphoreType.DMA((chunks,)),
            pltpu.SemaphoreType.DMA((chunks,)),
            pltpu.SemaphoreType.DMA((5, rows // TILE)),
            pltpu.SemaphoreType.DMA((chunks,)),
        ],
        compiler_params=pltpu.CompilerParams(vmem_limit_bytes=VMEM_LIMIT),
        cost_estimate=cost(0),
        name="feed_forward",
    )(place, mids[0], mids[1], cot, marks, bu, vectors, wu, wd)


def feed_back_kernel(
    place_ref, grad_low_ref, grad_ref, slope_ref, norm0_ref, norm1_ref, low_ref, wu_ref, wd_ref,
    wo_ref, rstd0_ref, rstd1_ref, vectors_ref,
    grad_one_ref, attn_ref, ctx_ref, send_ref, keep_ref, up_sums_ref, sums_ref,
    grad_low_s, grad_s, slope_s, norm_s, low_s, wu_s, wd_s, wo_s, rstd_s, grad_one_s, attn_s,
    ctx_s, out_s, middle_s,
    in_sems, slope_sems, up_sems, down_sems, tile_sems, out_sems, ctx_sems,
):
    length = norm0_ref.shape[0]
    rows, width = grad_low_ref.shape
    hidden = wu_ref.shape[1]
    half = hidden // 2
    chunks = hidden // HIDDEN_STEP
    tile = TILE
    core = place_ref[0]
    bases = lane_split(core, half, HIDDEN_STEP)

    def place_of(chunk):
        part, inside = divmod(chunk * HIDDEN_STEP, half)
        return pl.ds(pl.multiple_of(bases[part] + inside, HIDDEN_STEP), HIDDEN_STEP)

    def own(chunk):
        return pl.ds(chunk * HIDDEN_STEP, HIDDEN_STEP)

    def spot_of(index):
        return pl.ds(pl.multiple_of(index * tile, tile), tile)

    slopes = [
        pltpu.make_async_copy(
            slope_ref.at[spot_of(i), :], slope_s.at[spot_of(i), :], slope_sems.at[i]
        )
        for i in range(rows // tile)
    ]
    ups = [
        pltpu.make_async_copy(wu_ref.at[:, place_of(c)], wu_s.at[:, own(c)], up_sems.at[c])
        for c in range(chunks)
    ]
    downs = [
        pltpu.make_async_copy(wd_ref.at[place_of(c), :], wd_s.at[own(c), :], down_sems.at[c])
        for c in range(chunks)
    ]
    others = [
        pltpu.make_async_copy(a, b, in_sems.at[n])
        for n, (a, b) in enumerate(
            (
                (grad_low_ref, grad_low_s),
                (grad_ref, grad_s),
                (norm0_ref, norm_s.at[pl.ds(0, length)]),
                (norm1_ref, norm_s.at[pl.ds(length, length)]),
                (wo_ref, wo_s),
                (low_ref, low_s),
            )
        )
    ]
    others[0].start()
    downs[0].start()
    slopes[0].start()
    ups[0].start()
    for chunk in range(1, chunks):
        downs[chunk].start()
        ups[chunk].start()
    for copy in others[1:5] + slopes[1:] + others[5:]:
        copy.start()
    rstd_s[pl.ds(0, length), :] = rstd0_ref[...]
    rstd_s[pl.ds(length, length), :] = rstd1_ref[...]
    sums_ref[...] = jnp.zeros_like(sums_ref)
    up_sums_ref[...] = jnp.zeros_like(up_sums_ref)

    def tile_copies(index):
        spot = spot_of(index)
        pairs = ((grad_one_s, grad_one_ref), (attn_s, attn_ref))
        return [
            pltpu.make_async_copy(a.at[spot, :], b.at[spot, :], tile_sems.at[n, index])
            for n, (a, b) in enumerate(pairs)
        ]

    def inside(index, row, count=ROWS):
        return pl.ds(pl.multiple_of(index * tile + row, count), count)

    def work(index, opening):
        spot = spot_of(index)
        grad_low = grad_low_s[spot, :]

        def back(chunk):
            if opening:
                downs[chunk].wait()
            return nt(grad_low, wd_s[own(chunk), :])

        def forth(chunk, grad):
            if opening:
                ups[chunk].wait()
            more = nt(slope_s[spot, own(chunk)], wu_s[:, own(chunk)])
            return more if grad is None else grad + more

        ahead = back(0)
        if opening:
            slopes[0].wait()
        grad_middle = None
        for chunk in range(chunks):
            sums = jnp.zeros((8, HIDDEN_STEP), WIDE)
            for row in range(0, tile, ROWS):
                at = inside(index, row)
                slope = slope_s[at, own(chunk)].astype(WIDE)
                grad_hidden = (ahead[row : row + ROWS] * slope).astype(LOW)
                slope_s[at, own(chunk)] = grad_hidden
                sums = sums + jnp.sum(
                    grad_hidden.astype(WIDE).reshape(-1, 8, HIDDEN_STEP), axis=0
                )
            up_sums_ref[:, place_of(chunk)] += sums
            if chunk + 1 < chunks:
                ahead = back(chunk + 1)
            if chunk > 0:
                grad_middle = forth(chunk - 1, grad_middle)
        middle_s[...] = forth(chunks - 1, grad_middle)

    def norm(index):
        gain = vector(vectors_ref, "gain_one")
        sums = [jnp.zeros((1, width), WIDE) for _ in range(3)]
        for row in range(0, tile, ROWS_NORM):
            at = inside(index, row, ROWS_NORM)
            grad = middle_s[row : row + ROWS_NORM, :] + grad_s[at, :]
            normal = norm_s[at, :].astype(WIDE)
            grad_one = norm_back(grad, normal, rstd_s[at, :], gain)
            grad_one_s[at, :] = grad_one
            attn = grad_one.astype(LOW)
            attn_s[at, :] = attn
            sums[0] = sums[0] + row_total(grad * normal)
            sums[1] = sums[1] + row_total(grad)
            sums[2] = sums[2] + row_total(attn.astype(WIDE))
        for copy in tile_copies(index):
            copy.start()
        for n in range(3):
            sums_ref[n : n + 1, :] += sums[n]

    def project(index):
        spot = spot_of(index)
        turned = nt(wo_s[...], attn_s[spot, :]).astype(LOW)
        slot, inner = divmod(index * tile, length)
        ctx_s[slot, :, inner : inner + tile] = turned
        copy = pltpu.make_async_copy(
            ctx_s.at[slot, :, pl.ds(inner, tile)], ctx_ref.at[slot, :, pl.ds(inner, tile)],
            ctx_sems.at[index],
        )
        copy.start()
        return copy

    others[0].wait()
    work(0, True)
    for copy in slopes[1:] + others[1:5]:
        copy.wait()

    def turn(index, carried):
        norm(index - 1)
        work(index, False)
        return carried

    lax.fori_loop(1, rows // tile, turn, 0)
    norm(rows // tile - 1)
    copies = [project(index) for index in range(rows // tile)]
    others[5].wait()
    outer(slope_s, low_s, out_s, send_ref, keep_ref, out_sems)
    for copy in copies:
        copy.wait()
    for index in range(rows // tile):
        for copy in tile_copies(index):
            copy.wait()


def feed_back(place, grad_low, grad, slope, norms, rstds, mid_low, wu, wd, wo, vectors, *earlier):
    rows, width = grad.shape
    length = norms[0].shape[0]
    hidden = wu.shape[1]
    half = hidden // 2
    chunks = hidden // HIDDEN_STEP
    shapes = (
        jax.ShapeDtypeStruct((rows, width), WIDE),
        jax.ShapeDtypeStruct((rows, width), LOW),
        jax.ShapeDtypeStruct((rows // length, width, length), LOW),
        jax.ShapeDtypeStruct((half, width), LOW),
        jax.ShapeDtypeStruct((half, width), LOW),
        jax.ShapeDtypeStruct((8, hidden), WIDE),
        jax.ShapeDtypeStruct((8, width), WIDE),
    )
    return pl.pallas_call(
        ignoring(feed_back_kernel, 13, len(earlier)),
        out_shape=shapes,
        in_specs=[IN_SMEM] + [ANY] * 9 + [IN_VMEM] * 3 + [ANY] * len(earlier),
        out_specs=(ANY,) * 5 + (IN_VMEM,) * 2,
        scratch_shapes=[
            pltpu.VMEM((rows, width), LOW),
            pltpu.VMEM((rows, width), WIDE),
            pltpu.VMEM((rows, hidden), LOW),
            pltpu.VMEM((rows, width), LOW),
            pltpu.VMEM((rows, width), LOW),
            pltpu.VMEM((width, hidden), LOW),
            pltpu.VMEM((hidden, width), LOW),
            pltpu.VMEM((width, width), LOW),
            pltpu.VMEM((rows, 1), WIDE),
            pltpu.VMEM((rows, width), WIDE),
            pltpu.VMEM((rows, width), LOW),
            pltpu.VMEM((rows // length, width, length), LOW),
            pltpu.VMEM((hidden, width), LOW),
            pltpu.VMEM((TILE, width), WIDE),
            pltpu.SemaphoreType.DMA((6,)),
            pltpu.SemaphoreType.DMA((rows // TILE,)),
            pltpu.SemaphoreType.DMA((chunks,)),
            pltpu.SemaphoreType.DMA((chunks,)),
            pltpu.SemaphoreType.DMA((2, rows // TILE)),
            pltpu.SemaphoreType.DMA((chunks,)),
            pltpu.SemaphoreType.DMA((rows // TILE,)),
        ],
        compiler_params=pltpu.CompilerParams(vmem_limit_bytes=VMEM_LIMIT),
        cost_estimate=cost(0),
        name="feed_back",
    )(
        place, grad_low, grad, slope, norms[0], norms[1], mid_low, wu, wd, wo, rstds[0], rstds[1],
        vectors, *earlier,
    )


def attend_back_kernel(
    seg_ref, mark_ref, lse_ref, q_ref, k_ref, v_ref, ctx_ref, grad_ctx_ref, grad_one_ref, wq_ref,
    wk_ref, wv_ref,
    dq_ref, dk_ref, dv_ref, grad_in_ref, sums_ref,
    q_s, k_s, v_s, ctx_s, grad_ctx_s, grad_one_s, wq_s, wk_s, wv_s, bias_s, score_s, pull_s,
    chance_s, grad_s, in_sems, *, slot,
):
    length, model = q_ref.shape
    heads = model // HEAD_DIM
    width = 2 * HEAD_DIM
    loads = [
        pltpu.make_async_copy(a, b, in_sems.at[n])
        for n, (a, b) in enumerate(
            (
                (k_ref, k_s), (q_ref, q_s), (v_ref, v_s), (grad_ctx_ref.at[slot], grad_ctx_s),
                (ctx_ref, ctx_s), (wq_ref, wq_s), (wk_ref, wk_s), (wv_ref, wv_s),
                (grad_one_ref.at[pl.ds(slot * length, length), :], grad_one_s),
            )
        )
    ]
    for load in loads:
        load.start()
    mark_col = column(mark_ref[slot : slot + 1, :])
    fill_bias(bias_s, seg_ref[slot : slot + 1, :].astype(WIDE), mark_col)

    def lanes(head):
        return pl.ds(head // 2 * width, width)

    def rows_of(head):
        return pl.ds(head * HEAD_DIM, HEAD_DIM)

    def products(head):
        score_s[head % 2] = nt(k_s[:, lanes(head)] * lane_half(head % 2), q_s[:, lanes(head)])
        values = v_s[:, lanes(head)] * lane_half(head % 2)
        pull_s[head % 2] = nn(values, grad_ctx_s[lanes(head), :])

    def soften(head):
        score, pull = score_s.at[head % 2], pull_s.at[head % 2]
        chance, grad = chance_s.at[head % 2], grad_s.at[head % 2]
        shared = grad_ctx_s[rows_of(head), :].astype(WIDE) * ctx_s[rows_of(head), :].astype(WIDE)
        delta = jnp.sum(shared, axis=0, keepdims=True)
        lse = lse_ref[head : head + 1, :]
        for row in range(0, length, ROWS):
            at = slice(row, row + ROWS)
            block = jnp.exp(score[at, :] + bias_s[at, :] - lse)
            chance[at, :] = block.astype(LOW)
            grad[at, :] = (block * (pull[at, :] - delta)).astype(LOW)

    def combine(head, turned):
        part_v = nt(chance_s[head % 2], grad_ctx_s[lanes(head), :])
        part_k = nn(grad_s[head % 2], q_s[:, lanes(head)])
        part = turned[head % 2 * HEAD_DIM : (head % 2 + 1) * HEAD_DIM]
        return part_v, part_k, nn(part, grad_s[head % 2])

    def keep(head, one, two):
        first = lax.broadcasted_iota(jnp.int32, one[0].shape, 1) < HEAD_DIM
        dv_ref[:, lanes(head)] = jnp.where(first, one[0], two[0]).astype(LOW)
        dk_ref[:, lanes(head)] = jnp.where(first, one[1], two[1]).astype(LOW)
        dq_ref[:, lanes(head)] = jnp.concatenate([one[2], two[2]], axis=0).T.astype(LOW)

    for load in loads[:4]:
        load.wait()
    products(0)
    loads[4].wait()
    waiting = None
    found = []
    for head in range(heads):
        soften(head)
        if head % 2 == 0:
            turned = k_s[:, lanes(head)].T
        if len(found) == 2:
            keep(head - 2, *found)
            found = []
        if head + 1 < heads:
            products(head + 1)
        if waiting is not None:
            found.append(combine(*waiting))
        waiting = (head, turned)
    found.append(combine(*waiting))
    keep(heads - 1, *found)
    for load in loads[5:]:
        load.wait()
    grad_in_ref[...] = (
        grad_one_s[...]
        + nt(dq_ref[...], wq_s[...]) * SCORE_SCALE
        + nt(dk_ref[...], wk_s[...])
        + nt(dv_ref[...], wv_s[...])
    )
    sums_ref[...] = jnp.concatenate(
        [
            row_total(dq_ref[...].astype(WIDE)) * SCORE_SCALE,
            row_total(dv_ref[...].astype(WIDE)),
            jnp.zeros((6, model), WIDE),
        ],
        axis=0,
    )


def attend_back(slot, q, k, v, ctx, grad_ctx, lse, segs, marks, grad_one, wq, wk, wv, *earlier):
    length, width = q.shape
    heads = width // HEAD_DIM
    shapes = (
        jax.ShapeDtypeStruct((length, width), LOW),
        jax.ShapeDtypeStruct((length, width), LOW),
        jax.ShapeDtypeStruct((length, width), LOW),
        jax.ShapeDtypeStruct((length, width), WIDE),
        jax.ShapeDtypeStruct((8, width), WIDE),
    )
    tokens = pltpu.VMEM((length, width), LOW)
    turned = pltpu.VMEM((width, length), LOW)
    weight = pltpu.VMEM((width, width), LOW)
    return pl.pallas_call(
        ignoring(functools.partial(attend_back_kernel, slot=slot), 12, len(earlier)),
        out_shape=shapes,
        in_specs=[IN_VMEM] * 3 + [ANY] * (9 + len(earlier)),
        out_specs=(IN_VMEM,) * 5,
        scratch_shapes=[
            tokens, tokens, tokens, turned, turned, pltpu.VMEM((length, width), WIDE),
            weight, weight, weight,
            pltpu.VMEM((length, length), WIDE),
            pltpu.VMEM((2, length, length), WIDE),
            pltpu.VMEM((2, length, length), WIDE),
            pltpu.VMEM((2, length, length), LOW),
            pltpu.VMEM((2, length, length), LOW),
            pltpu.SemaphoreType.DMA((9,)),
        ],
        compiler_params=pltpu.CompilerParams(vmem_limit_bytes=VMEM_LIMIT),
        cost_estimate=cost(0),
        name="attend_back",
    )(segs, marks, lse, q, k, v, ctx, grad_ctx, grad_one, wq, wk, wv, *earlier)


def square_kernel(
    place_ref, x0_ref, x1_ref, dq0_ref, dq1_ref, dk0_ref, dk1_ref, dv0_ref, dv1_ref, ctx0_ref,
    ctx1_ref, attn_ref, send_ref, keep_ref, x_s, dq_s, dk_s, dv_s, ctx_s, attn_s, out_s, in_sems,
    out_sems,
):
    length, width = x0_ref.shape
    first, second = pl.ds(0, length), pl.ds(length, length)
    loads = []
    for a, b in (
        (x0_ref, x_s.at[first]), (x1_ref, x_s.at[second]), (dv0_ref, dv_s.at[first]),
        (dv1_ref, dv_s.at[second]), (dq0_ref, dq_s.at[first]), (dq1_ref, dq_s.at[second]),
        (ctx0_ref, ctx_s.at[:, first]), (ctx1_ref, ctx_s.at[:, second]), (attn_ref, attn_s),
        (dk0_ref, dk_s.at[first]), (dk1_ref, dk_s.at[second]),
    ):
        loads.append(pltpu.make_async_copy(a, b, in_sems.at[len(loads)]))
        loads[-1].start()
    mine = place_ref[0] == 0
    x = x_s[...]
    step = 256
    copies = []

    def place(part, columns, low, high):
        for n, (ref, kept) in enumerate(((send_ref, False), (keep_ref, True))):
            spot = pl.ds((n * 2 + part) * width, width)
            out_s[spot, columns] = jnp.where(mine == kept, low, high).astype(LOW)

    def flush(part):
        for n, ref in enumerate((send_ref, keep_ref)):
            spot = pl.ds((n * 2 + part) * width, width)
            copies.append(
                pltpu.make_async_copy(
                    out_s.at[spot, :], ref.at[pl.ds(part * width, width), :],
                    out_sems.at[len(copies)],
                )
            )
            copies[-1].start()

    for load in loads[:6]:
        load.wait()
    x = x_s[...]
    for start in range(0, width, step):
        columns = pl.ds(start, step)
        place(0, columns, tn(x, dq_s[:, columns]) * SCORE_SCALE, tn(x, dv_s[:, columns]))
    flush(0)
    for load in loads[6:]:
        load.wait()
    for start in range(0, width, step):
        columns = pl.ds(start, step)
        place(1, columns, tn(x, dk_s[:, columns]), nn(ctx_s[...], attn_s[:, columns]))
    flush(1)
    for copy in copies:
        copy.wait()


def square_grads(place, xs, dqs, dks, dvs, ctxs, attn, *earlier):
    length, width = xs[0].shape
    rows = length * len(xs)
    tokens = pltpu.VMEM((rows, width), LOW)
    out = jax.ShapeDtypeStruct((2 * width, width), LOW)
    return pl.pallas_call(
        ignoring(square_kernel, 12, len(earlier)),
        out_shape=(out, out),
        in_specs=[IN_SMEM] + [ANY] * (11 + len(earlier)),
        out_specs=(ANY, ANY),
        scratch_shapes=[
            tokens, tokens, tokens, tokens, pltpu.VMEM((width, rows), LOW), tokens,
            pltpu.VMEM((4 * width, width), LOW),
            pltpu.SemaphoreType.DMA((11,)),
            pltpu.SemaphoreType.DMA((4,)),
        ],
        compiler_params=pltpu.CompilerParams(vmem_limit_bytes=VMEM_LIMIT),
        cost_estimate=cost(8 * rows * width * width),
        name="square_grads",
    )(place, *xs, *dqs, *dks, *dvs, *ctxs, attn, *earlier)


def merge_kernel(own_ref, got_ref, out_ref, sems):
    rows = own_ref.shape[0]
    copies = [
        pltpu.make_async_copy(ref, out_ref.at[pl.ds(n * rows, rows), :], sems.at[n])
        for n, ref in enumerate((own_ref, got_ref))
    ]
    for copy in copies:
        copy.start()
    for copy in copies:
        copy.wait()


def merge(own, got):
    rows, width = own.shape
    return pl.pallas_call(
        merge_kernel,
        out_shape=jax.ShapeDtypeStruct((2 * rows, width), own.dtype),
        in_specs=[ANY, ANY],
        out_specs=ANY,
        scratch_shapes=[pltpu.SemaphoreType.DMA((2,))],
        cost_estimate=cost(0),
        name="merge",
    )(own, got)


def pick_kernel(place_ref, value_ref, out_ref, sem):
    copy = pltpu.make_async_copy(value_ref.at[place_ref[0]], out_ref, sem)
    copy.start()
    copy.wait()


def pick(value, place, *earlier):
    return pl.pallas_call(
        ignoring(pick_kernel, 2, len(earlier)),
        out_shape=jax.ShapeDtypeStruct(value.shape[1:], value.dtype),
        in_specs=[IN_SMEM, ANY] + [ANY] * len(earlier),
        out_specs=ANY,
        scratch_shapes=[pltpu.SemaphoreType.DMA],
        cost_estimate=cost(0),
        name="pick",
    )(place.astype(jnp.int32).reshape(1), value, *earlier)


def own_pieces(value, slot, slots, *earlier):
    count = lax.axis_size("seq")
    me = lax.axis_index("seq")
    pieces = [lax.dynamic_index_in_dim(value, me * slots + slot, 0, keepdims=False)]
    for shift in range(1, count):
        block = pick(value, (me + shift) % count * slots + slot, *earlier)
        pairs = [(source, (source + shift) % count) for source in range(count)]
        pieces.append(lax.ppermute(block, "seq", pairs))
    return pieces


def return_pieces(pieces, link_type):
    count = lax.axis_size("seq")
    me = lax.axis_index("seq")
    slots = pieces[0].shape[0]
    out = jnp.zeros((slots * count,) + pieces[0].shape[1:], pieces[0].dtype)
    out = lax.dynamic_update_slice_in_dim(out, pieces[0], me * slots, 0)
    for shift in range(1, count):
        pairs = [(source, (source - shift) % count) for source in range(count)]
        got = lax.ppermute(pieces[shift].astype(link_type), "seq", pairs).astype(out.dtype)
        out = lax.dynamic_update_slice_in_dim(out, got, ((me + shift) % count) * slots, 0)
    return out


def swap(value, axis, bit):
    count = lax.axis_size(axis)
    return lax.ppermute(value, axis, [(source, source ^ bit) for source in range(count)])


def bit_of(axis, bit):
    return (lax.axis_index(axis) // bit) % 2


def chip_orders():
    dp, seq = lax.axis_size("dp"), lax.axis_size("seq")
    along_dp = [("dp", 2**i) for i in range(1, dp.bit_length() - 1)]
    along_seq = [("seq", 2**i) for i in range(seq.bit_length() - 1)]
    x, z, y = along_dp[0], along_dp[1], along_seq[0]
    rest = along_dp[2:] + along_seq[1:]
    return [x, z, y] + rest, [y, x, z] + rest, [z, y, x] + rest


HALVINGS = 4


def half_sum(first, second, which):
    half = first.shape[0] // 2
    a = lax.dynamic_slice_in_dim(first, which * half, half, 0).astype(WIDE)
    b = lax.dynamic_slice_in_dim(second, which * half, half, 0).astype(WIDE)
    return (a + b).astype(LOW)


class Reduction:
    def __init__(self, first, second, order):
        self.first, self.second, self.order = first, second, order
        self.step = 0

    def send(self):
        axis, bit = self.order[self.step]
        mine = bit_of(axis, bit)
        sent = half_sum(self.first, self.second, 1 - mine)
        self.first, self.second = half_sum(self.first, self.second, mine), swap(sent, axis, bit)
        self.step += 1
        return sent

    def finish(self):
        while self.step < HALVINGS:
            self.send()
        share = (self.first.astype(WIDE) + self.second.astype(WIDE)).astype(LOW)
        for axis, bit in self.order[HALVINGS:]:
            share = (share.astype(WIDE) + swap(share, axis, bit).astype(WIDE)).astype(LOW)
        for step in reversed(range(1, HALVINGS)):
            share = merge(share, swap(share, *self.order[step]))
        near, far = share, swap(share, *self.order[0])
        return [near, far, swap(near, "dp", 1), swap(far, "dp", 1)]


def place_in(order):
    place = 0
    for axis, bit in order[:HALVINGS]:
        place = place * 2 + bit_of(axis, bit)
    return place


def found_block(place, half, refs, index):
    core, me = place
    near_own, far_own, near_other, far_other = refs
    block = near_own.shape[0] >> (HALVINGS - 1)
    spot = index ^ me
    blocks = 1 << (HALVINGS - 1)
    rows = pl.ds(pl.multiple_of(lax.rem(spot, blocks) * block, block), block)
    near = jnp.where(core == half, near_own[rows, :], near_other[rows, :])
    far = jnp.where(core == half, far_own[rows, :], far_other[rows, :])
    return jnp.where(spot < blocks, near, far).astype(WIDE)


def finish_kernel(place_ref, near_own, far_own, near_other, far_other, out_ref, *, turned):
    half, tile = pl.program_id(0), pl.program_id(1)
    refs = (near_own, far_own, near_other, far_other)
    place = (place_ref[0], place_ref[1])
    block = near_own.shape[0] >> (HALVINGS - 1)
    count = out_ref.shape[1 if turned else 0] // block
    found = [found_block(place, half, refs, tile * count + j) for j in range(count)]
    if turned:
        out_ref[...] = jnp.concatenate(found, axis=0).T
    else:
        for j in range(count):
            out_ref[j * block : (j + 1) * block, :] = found[j]


def finish(place, arrays, turned):
    rows, width = arrays[0].shape
    tile = rows // 2
    if turned:
        shape = (width, 4 * rows)
        spec = pl.BlockSpec((width, tile), lambda h, t, *_: (0, h * 4 + t))
    else:
        shape = (4 * rows, width)
        spec = pl.BlockSpec((tile, width), lambda h, t, *_: (h * 4 + t, 0))
    return pl.pallas_call(
        functools.partial(finish_kernel, turned=turned),
        out_shape=jax.ShapeDtypeStruct(shape, WIDE),
        grid_spec=pltpu.PrefetchScalarGridSpec(
            num_scalar_prefetch=1,
            grid=(2, 4),
            in_specs=[whole(array.shape) for array in arrays],
            out_specs=spec,
        ),
        compiler_params=pltpu.CompilerParams(vmem_limit_bytes=VMEM_LIMIT),
        cost_estimate=cost(0),
        name="finish",
    )(place, *arrays)


def finish_square_kernel(place_ref, *refs):
    parts = (len(refs) - 4) // 4
    out_refs = refs[4 * parts :]
    width = refs[0].shape[1]
    block = refs[0].shape[0] >> (HALVINGS - 1)
    each = block << HALVINGS
    for half in range(2):
        for row in range(0, each * parts, block):
            part = row // each
            place = (place_ref[0], place_ref[1 + part])
            index = (row - part * each) // block
            out = out_refs[half * 2 + row // width]
            out[row % width : row % width + block, :] = found_block(
                place, half, refs[4 * part : 4 * part + 4], index
            )


def finish_square(place, parts):
    width = parts[0][0].shape[1]
    shape = jax.ShapeDtypeStruct((width, width), WIDE)
    args = [array for part in parts for array in part]
    return pl.pallas_call(
        finish_square_kernel,
        out_shape=(shape,) * 4,
        grid_spec=pltpu.PrefetchScalarGridSpec(
            num_scalar_prefetch=1,
            grid=(1,),
            in_specs=[whole(arg.shape) for arg in args],
            out_specs=(whole(shape.shape),) * 4,
        ),
        compiler_params=pltpu.CompilerParams(vmem_limit_bytes=VMEM_LIMIT),
        cost_estimate=cost(0),
        name="finish_square",
    )(place, *args)


def on_device(
    inputs, cotangent, w_query, b_query, w_key, w_value, b_value, w_out, b_out, gain_one,
    shift_one, w_up, b_up, w_down, b_down, gain_two, shift_two, live_counts, valid_mask, segments,
):
    seqs, piece, width = inputs.shape
    count = lax.axis_size("seq")
    slots = seqs // count
    length = piece * count
    core = bit_of("dp", 1).astype(jnp.int32)
    orders = chip_orders()
    core_place = core.reshape(1)

    vectors = jnp.stack(
        [b_query, b_value, b_out, gain_one, shift_one, b_down, gain_two, shift_two]
    ).astype(WIDE)
    bias_up = b_up.astype(WIDE).reshape(1, -1)
    live = (jnp.arange(seqs) < live_counts[0]).astype(jnp.int32)
    code = segments * 2 + valid_mask * live[:, None]
    codes = jnp.stack([jnp.concatenate(own_pieces(code, slot, slots)) for slot in range(slots)])
    segs = codes // 2
    weight = codes % 2
    marks = jnp.where(weight > 0, segs, -1)
    xs, got = [], []
    for slot in range(slots):
        pieces = own_pieces(inputs, slot, slots, *got)
        got = pieces[-1:]
        xs.append(jnp.concatenate(pieces))
    forward = []
    cots = []
    for slot in range(slots):
        forward.append(attend(slot, xs[slot], segs, marks, vectors, w_query, w_key, w_value, w_out))
    for slot in range(slots):
        cots += own_pieces(cotangent, slot, slots, forward[0][0])
    (slope, mid_low, result, grad_h2, grad_feed, down_sent, down_kept, sums_two, stat_two) = (
        feed_forward(
            core_place, [each[5] for each in forward], jnp.concatenate(cots), marks, w_up, bias_up,
            w_down, vectors,
        )
    )
    along_x, along_y, along_z = orders
    down = Reduction(down_kept, swap(down_sent, "dp", 1), along_x)
    waited = down.send()
    grad_h1, grad_attn, grad_ctx, up_sent, up_kept, up_sums, sums_one = feed_back(
        core_place, grad_feed, grad_h2, slope, [each[6] for each in forward],
        [each[7] for each in forward], mid_low, w_up, w_down, w_out, vectors, waited,
    )
    up = Reduction(up_kept, swap(up_sent, "dp", 1), along_y)
    backward = []
    waiting = [[down.send(), up.send()], [down.send()]]
    for slot in range(slots):
        backward.append(
            attend_back(
                slot, *forward[slot][:4], grad_ctx, forward[slot][4], segs, marks, grad_h1,
                w_query, w_key, w_value, *waiting[min(slot, 1)],
            )
        )
    square_sent, square_kept = square_grads(
        core_place, xs, *([each[i] for each in backward] for i in range(3)),
        [each[3] for each in forward], grad_attn, down.send(), up.send(),
    )
    square_got = swap(square_sent, "dp", 1)
    each_rows = square_kept.shape[0] // len(orders)
    thirds = []
    for part, order in enumerate(orders):
        inside = slice(part * each_rows, (part + 1) * each_rows)
        thirds.append(Reduction(square_kept[inside], square_got[inside], order))
    places = [place_in(order).astype(jnp.int32) for order in orders]
    grad_w_down = finish(jnp.stack([core, places[0]]), down.finish(), False)
    grad_w_up = finish(jnp.stack([core, places[1]]), up.finish(), True)
    squares = finish_square(jnp.stack([core] + places), [third.finish() for third in thirds])

    result = result.reshape(slots, length, width)
    result_out = return_pieces(
        [result[:, i * piece : (i + 1) * piece] for i in range(count)], LOW
    )
    stats = [
        sum(each[8][0, 0] for each in forward),
        sum(each[8][1, 0] for each in forward),
        stat_two[0, 0],
        stat_two[1, 0],
        jnp.sum(weight).astype(WIDE),
    ]
    stats = jnp.concatenate([jnp.stack(stats), jnp.zeros((width - 5,), WIDE)]).reshape(1, width)
    small = jnp.concatenate(
        [
            sum(each[4][0:2] for each in backward),
            sums_one[0:3],
            sums_two[0:3],
            stats,
            jnp.sum(up_sums, axis=0).reshape(-1, width),
        ],
        axis=0,
    )
    for axis, bit in [("dp", 1)] + orders[0]:
        small = small + swap(small, axis, bit)
    rms_values = jnp.sqrt(small[8, :4] / (width * small[8, 4]))

    grad_inputs = jnp.stack([each[3] for each in backward])
    grad_out = return_pieces(
        [grad_inputs[:, i * piece : (i + 1) * piece] for i in range(count)], LOW
    )
    return (
        result_out,
        grad_out,
        squares[0],
        small[0],
        squares[1],
        squares[2],
        small[1],
        squares[3],
        small[4],
        small[2],
        small[3],
        grad_w_up,
        small[9:].reshape(-1),
        grad_w_down,
        small[7],
        small[5],
        small[6],
        rms_values,
    )


def solution(mesh):
    split = P("dp", "seq", None)
    pair = P("dp", "seq")
    return jax.shard_map(
        on_device,
        mesh=mesh,
        in_specs=(split, split) + (P(),) * 15 + (P("dp"), pair, pair),
        out_specs=(split, split) + (P(),) * 16,
        check_vma=False,
    )
```

```python
import functools

import jax
import jax.numpy as jnp
from jax import lax
from jax.experimental import pallas as pl
from jax.experimental.pallas import tpu as pltpu
from jax.sharding import PartitionSpec as P

HEAD_DIM = 64
EPSILON = 1e-05
NEGATIVE = -1e30
SCORE_SCALE = 0.125
LOW = jnp.bfloat16
WIDE = jnp.float32
VMEM_LIMIT = 63 * 1024 * 1024
HIDDEN_STEP = 768
TILE = 256
ROWS = 32
ROWS_NORM = 16
ANY = pl.BlockSpec(memory_space=pltpu.HBM)
IN_VMEM = pl.BlockSpec(memory_space=pltpu.VMEM)
IN_SMEM = pl.BlockSpec(memory_space=pltpu.SMEM)

ERF_P = 0.3275911
ERF_C = (0.254829592, -0.284496736, 1.421413741, -1.453152027, 1.061405429)
ROOT_HALF = 0.7071067811865476
DENSITY = 0.3989422804014327


def nn(left, right):
    return jnp.dot(left, right, preferred_element_type=WIDE)


def nt(left, right):
    return lax.dot_general(
        left, right, (((1,), (1,)), ((), ())), preferred_element_type=WIDE
    )


def tn(left, right):
    return lax.dot_general(
        left, right, (((0,), (0,)), ((), ())), preferred_element_type=WIDE
    )


def gelu_pair(hidden):
    tail_exp = jnp.exp(hidden * hidden * -0.5)
    slow = 1.0 + (ERF_P * ROOT_HALF) * jnp.abs(hidden)
    t = pl.reciprocal(slow, approx=True)
    t = t * (2.0 - slow * t)
    c1, c2, c3, c4, c5 = (0.5 * c for c in ERF_C)
    tail = ((((c5 * t + c4) * t + c3) * t + c2) * t + c1) * t * tail_exp
    below = jnp.where(hidden >= 0.0, 1.0 - tail, tail)
    return hidden * below, below + hidden * (DENSITY * tail_exp)


def lane_half(half):
    lane = lax.broadcasted_iota(jnp.int32, (1, 2 * HEAD_DIM), 1)
    inside = (lane < HEAD_DIM) if half == 0 else (lane >= HEAD_DIM)
    return inside.astype(WIDE).astype(LOW)


def fill_bias(bias_ref, seg_row, mark_col):
    length = bias_ref.shape[0]
    key_place = lax.broadcasted_iota(jnp.int32, (length, length), 0)
    query_place = lax.broadcasted_iota(jnp.int32, (length, length), 1)
    visible = (mark_col == seg_row) | (key_place == query_place)
    bias_ref[...] = jnp.where(visible, 0.0, NEGATIVE)


def total(rows_weight, values):
    per_row = jnp.sum(values * values, axis=1, keepdims=True) * rows_weight
    return jnp.sum(per_row, axis=0, keepdims=True)


def column(row):
    return jnp.broadcast_to(row.astype(WIDE), (8, row.shape[1])).T[:, 0:1]


VECTORS = ("b_query", "b_value", "b_out", "gain_one", "shift_one", "b_down", "gain_two", "shift_two")


def vector(ref, name):
    place = VECTORS.index(name)
    return ref[place : place + 1, :]


def attend_kernel(
    place_ref, seg_ref, mark_ref, vectors_ref, wq_ref, wk_ref, wv_ref, wo_ref, inputs_ref, *refs,
    pieces,
):
    (
        q_ref, k_ref, v_ref, x_ref, ctx_ref, lse_ref, mid_ref, norm_ref, rstd_ref, stat_ref,
        wq_s, wk_s, wv_s, wo_s, q_s, k_s, v_s, x_s, bias_s, score_s, chance_s, weight_s, in_sems,
        out_sems,
    ) = refs[pieces - 1 :]
    length, model = x_s.shape
    piece = length // pieces
    loads = [
        pltpu.make_async_copy(a, b, in_sems.at[n])
        for n, (a, b) in enumerate(
            ((wk_ref, wk_s), (wq_ref, wq_s), (wv_ref, wv_s), (wo_ref, wo_s))
        )
    ]
    tokens_in = [
        pltpu.make_async_copy(a, x_s.at[pl.ds(n * piece, piece), :], in_sems.at[4 + n])
        for n, a in enumerate((inputs_ref.at[place_ref[0] + place_ref[1]],) + refs[: pieces - 1])
    ]
    for load in tokens_in + loads:
        load.start()
    stores = [
        pltpu.make_async_copy(a, b, out_sems.at[n])
        for n, (a, b) in enumerate(((k_s, k_ref), (q_s, q_ref), (v_s, v_ref), (x_s, x_ref)))
    ]
    own = pl.ds(place_ref[1], 1)
    mark_col = column(mark_ref[own, :])
    weight_s[...] = (mark_col >= 0).astype(WIDE)
    fill_bias(bias_s, seg_ref[own, :].astype(WIDE), mark_col)
    heads = model // HEAD_DIM
    width = 2 * HEAD_DIM
    for load in tokens_in:
        load.wait()
    stores[3].start()
    loads[0].wait()
    k_s[...] = nn(x_s[...], wk_s[...]).astype(LOW)
    stores[0].start()
    loads[1].wait()
    q_s[...] = ((nn(x_s[...], wq_s[...]) + vector(vectors_ref, "b_query")) * SCORE_SCALE).astype(LOW)
    stores[1].start()
    loads[2].wait()
    v_s[...] = (nn(x_s[...], wv_s[...]) + vector(vectors_ref, "b_value")).astype(LOW)
    stores[2].start()

    def lanes(head):
        return pl.ds(head // 2 * width, width)

    def scores(head):
        keys = k_s[:, lanes(head)] * lane_half(head % 2)
        score_s[head % 2] = nt(keys, q_s[:, lanes(head)])

    def soften(head):
        here, chance = score_s.at[head % 2], chance_s.at[head % 2]
        top = jnp.full((8, length), NEGATIVE, WIDE)
        for row in range(0, length, ROWS):
            block = here[row : row + ROWS, :] + bias_s[row : row + ROWS, :]
            here[row : row + ROWS, :] = block
            top = jnp.maximum(top, jnp.max(block.reshape(-1, 8, length), axis=0))
        top = jnp.max(top, axis=0, keepdims=True)
        amount = jnp.zeros((8, length), WIDE)
        for row in range(0, length, ROWS):
            block = jnp.exp(here[row : row + ROWS, :] - top)
            chance[row : row + ROWS, :] = block.astype(LOW)
            amount = amount + jnp.sum(block.reshape(-1, 8, length), axis=0)
        amount = jnp.sum(amount, axis=0, keepdims=True)
        lse_ref[head : head + 1, :] = top + jnp.log(amount)
        return 1.0 / amount

    def combine(head, share, turned):
        part = turned[head % 2 * HEAD_DIM : (head % 2 + 1) * HEAD_DIM]
        summed = nn(part, chance_s[head % 2]) * share
        ctx_ref[head * HEAD_DIM : (head + 1) * HEAD_DIM, :] = summed.astype(LOW)

    scores(0)
    waiting = None
    for head in range(heads):
        share = soften(head)
        if head % 2 == 0:
            turned = v_s[:, lanes(head)].T
        if head + 1 < heads:
            scores(head + 1)
        if waiting is not None:
            combine(*waiting)
        waiting = (head, share, turned)
    combine(*waiting)
    loads[3].wait()
    attention_all = tn(ctx_ref[...], wo_s[...])
    bias, gain, shift = (vector(vectors_ref, n) for n in ("b_out", "gain_one", "shift_one"))
    stats = [jnp.zeros((1, 1), WIDE) for _ in range(2)]
    for row in range(0, length, ROWS_NORM):
        at = pl.ds(row, ROWS_NORM)
        attention = attention_all[row : row + ROWS_NORM] + bias
        rows = x_s[at, :].astype(WIDE)
        total_in = rows + attention
        center = total_in - jnp.mean(total_in, axis=1, keepdims=True)
        rstd = lax.rsqrt(jnp.mean(center * center, axis=1, keepdims=True) + EPSILON)
        normal = center * rstd
        mid_ref[at, :] = normal * gain + shift
        norm_ref[at, :] = normal.astype(LOW)
        rstd_ref[at, :] = rstd
        row_weight = weight_s[at, :]
        stats[0] = stats[0] + total(row_weight, rows)
        stats[1] = stats[1] + total(row_weight, attention)
    stat_ref[...] = jnp.concatenate(
        [jnp.broadcast_to(stat, (1, 128)) for stat in stats] + [jnp.zeros((6, 128), WIDE)], axis=0
    )
    for store in stores:
        store.wait()


def cost():
    return pl.CostEstimate(flops=10**8, transcendentals=0, bytes_accessed=0)


def ignoring(kernel, inputs, extra):
    def wrapped(*refs):
        return kernel(*refs[:inputs], *refs[inputs + extra :])

    return wrapped


def whole(shape):
    return pl.BlockSpec(shape, lambda *_: (0,) * len(shape), pipeline_mode=pl.Buffered(1))


def attend(place, inputs, got, segs, marks, vectors, wq, wk, wv, wo, *earlier):
    pieces = len(got) + 1
    length, width = inputs.shape[1] * pieces, inputs.shape[2]
    heads = width // HEAD_DIM
    lse_rows = heads + (-heads) % 8
    tokens_out = jax.ShapeDtypeStruct((length, width), LOW)
    shapes = (
        tokens_out, tokens_out, tokens_out, tokens_out,
        jax.ShapeDtypeStruct((width, length), LOW),
        jax.ShapeDtypeStruct((lse_rows, length), WIDE),
        jax.ShapeDtypeStruct((length, width), WIDE),
        tokens_out,
        jax.ShapeDtypeStruct((length, 1), WIDE),
        jax.ShapeDtypeStruct((8, 128), WIDE),
    )
    args = (place, segs, marks, vectors, wq, wk, wv, wo, inputs, *got)
    weight = pltpu.VMEM((width, width), LOW)
    tokens = pltpu.VMEM((length, width), LOW)
    return pl.pallas_call(
        ignoring(
            functools.partial(attend_kernel, pieces=pieces), len(args), len(earlier)
        ),
        out_shape=shapes,
        in_specs=[IN_SMEM] + [IN_VMEM] * 3 + [ANY] * (4 + pieces + len(earlier)),
        out_specs=(ANY,) * 4 + (IN_VMEM,) * 6,
        scratch_shapes=[weight] * 4 + [tokens] * 4 + [
            pltpu.VMEM((length, length), WIDE),
            pltpu.VMEM((2, length, length), WIDE),
            pltpu.VMEM((2, length, length), LOW),
            pltpu.VMEM((length, 1), WIDE),
            pltpu.SemaphoreType.DMA((4 + pieces,)),
            pltpu.SemaphoreType.DMA((4,)),
        ],
        compiler_params=pltpu.CompilerParams(vmem_limit_bytes=VMEM_LIMIT),
        cost_estimate=cost(),
        name="attend",
    )(*args, *earlier)


def norm_back(grad, normal, rstd, gain):
    pulled = grad * gain
    return rstd * (
        pulled
        - jnp.mean(pulled, axis=1, keepdims=True)
        - normal * jnp.mean(pulled * normal, axis=1, keepdims=True)
    )


def row_total(values):
    return jnp.sum(values, axis=0, keepdims=True)


def feed_kernel(
    place_ref, mid0_ref, mid1_ref, cot_ref, mark_ref, bu_ref, vectors_ref, wu_ref, wd_ref, *refs,
    pieces,
):
    (
    slope_ref, low_ref, result_ref, grad_ref, grad_low_ref, send_ref, keep_ref, sums_ref, stat_ref,
    mid_s, cot_s, wu_s, wd_s, act_s, slope_s, low_s, result_s, grad_s, grad_low_s, out_s,
    feed_s, weight_s, in_sems, up_sems, down_sems, tile_sems, out_sems,
    ) = refs[pieces - 1 :]
    length, width = mid0_ref.shape
    rows = cot_s.shape[0]
    piece = length // pieces
    hidden = wu_ref.shape[1]
    half = hidden // 2
    chunks = hidden // HIDDEN_STEP
    tile = TILE
    mine = place_ref[0]

    def place_of(chunk, count=1):
        part, inside = divmod(chunk * HIDDEN_STEP, half)
        start = (mine if part else 1 - mine) * half + inside
        return pl.ds(pl.multiple_of(start, HIDDEN_STEP), count * HIDDEN_STEP)

    def own(chunk):
        return pl.ds(chunk * HIDDEN_STEP, HIDDEN_STEP)

    first_in = pltpu.make_async_copy(mid0_ref, mid_s.at[pl.ds(0, length)], in_sems.at[0])
    second_in = pltpu.make_async_copy(mid1_ref, mid_s.at[pl.ds(length, length)], in_sems.at[1])
    cot_in = []
    for slot in range(rows // length):
        own_piece = cot_ref.at[place_ref[1] + slot]
        for part, ref in enumerate([own_piece] + [ref.at[slot] for ref in refs[: pieces - 1]]):
            spot = pl.ds(slot * length + part * piece, piece)
            sem = in_sems.at[2 + len(cot_in)]
            cot_in.append(pltpu.make_async_copy(ref, cot_s.at[spot, :], sem))
    ups = [
        pltpu.make_async_copy(wu_ref.at[:, place_of(c)], wu_s.at[:, own(c)], up_sems.at[c])
        for c in range(chunks)
    ]
    downs = [
        pltpu.make_async_copy(wd_ref.at[place_of(c), :], wd_s.at[own(c), :], down_sems.at[c])
        for c in range(chunks)
    ]
    first_in.start()
    for chunk in range(chunks):
        ups[chunk].start()
        downs[chunk].start()
    second_in.start()
    for copy in cot_in:
        copy.start()
    sums_ref[...] = jnp.zeros_like(sums_ref)
    stat_ref[...] = jnp.zeros_like(stat_ref)
    for slot in range(mark_ref.shape[0]):
        mark_col = column(mark_ref[slot : slot + 1, :])
        weight_s[pl.ds(slot * length, length), :] = (mark_col >= 0).astype(WIDE)

    def tile_copies(index):
        spot = pl.ds(pl.multiple_of(index * tile, tile), tile)
        pairs = (
            (low_s, low_ref), (result_s, result_ref), (grad_s, grad_ref),
            (grad_low_s, grad_low_ref),
        )
        copies = [
            pltpu.make_async_copy(a.at[spot, :], b.at[spot, :], tile_sems.at[n, index])
            for n, (a, b) in enumerate(pairs)
        ]
        for part in range(2):
            own_half = slope_s.at[spot, pl.ds(part * half, half)]
            there = slope_ref.at[spot, place_of(part * chunks // 2, chunks // 2)]
            copies.append(pltpu.make_async_copy(own_half, there, tile_sems.at[4 + part, index]))
        return copies

    def inside(index, row, count=ROWS):
        return pl.ds(pl.multiple_of(index * tile + row, count), count)

    def work(index, opening):
        spot = pl.ds(pl.multiple_of(index * tile, tile), tile)
        for row in range(0, tile, ROWS):
            low_s[inside(index, row), :] = mid_s[inside(index, row), :].astype(LOW)
        middle_low = low_s[spot, :]

        def up(chunk):
            if opening:
                ups[chunk].wait()
            return nn(middle_low, wu_s[:, own(chunk)])

        def down(chunk, feed):
            if opening:
                downs[chunk].wait()
            more = nn(act_s[spot, own(chunk)], wd_s[own(chunk), :])
            return more if feed is None else feed + more

        feed = None
        ahead = up(0)
        for chunk in range(chunks):
            bias = bu_ref[:, place_of(chunk)]
            for row in range(0, tile, ROWS):
                active, slope = gelu_pair(ahead[row : row + ROWS] + bias)
                act_s[inside(index, row), own(chunk)] = active.astype(LOW)
                slope_s[inside(index, row), own(chunk)] = slope.astype(LOW)
            if chunk + 1 < chunks:
                ahead = up(chunk + 1)
            if chunk > 0:
                feed = down(chunk - 1, feed)
        feed_s[...] = down(chunks - 1, feed)

    def norm(index):
        gain, shift, bias = (vector(vectors_ref, n) for n in ("gain_two", "shift_two", "b_down"))
        sums = [jnp.zeros((1, width), WIDE) for _ in range(3)]
        stats = [jnp.zeros((1, 1), WIDE) for _ in range(2)]
        for row in range(0, tile, ROWS_NORM):
            here = inside(index, row, ROWS_NORM)
            feed_here = feed_s[row : row + ROWS_NORM, :] + bias
            total_in = mid_s[here, :] + feed_here
            center = total_in - jnp.mean(total_in, axis=1, keepdims=True)
            rstd = lax.rsqrt(jnp.mean(center * center, axis=1, keepdims=True) + EPSILON)
            normal = center * rstd
            result = normal * gain + shift
            result_s[here, :] = result.astype(LOW)
            weight = weight_s[here, :]
            grad_result = cot_s[here, :].astype(WIDE) * weight
            grad = norm_back(grad_result, normal, rstd, gain)
            grad_s[here, :] = grad
            grad_low = grad.astype(LOW)
            grad_low_s[here, :] = grad_low
            sums[0] = sums[0] + row_total(grad_result * normal)
            sums[1] = sums[1] + row_total(grad_result)
            sums[2] = sums[2] + row_total(grad_low.astype(WIDE))
            stats[0] = stats[0] + total(weight, feed_here)
            stats[1] = stats[1] + total(weight, result)
        for copy in tile_copies(index):
            copy.start()
        for n in range(3):
            sums_ref[n : n + 1, :] += sums[n]
        for n in range(2):
            stat_ref[n : n + 1, :] += jnp.broadcast_to(stats[n], (1, 128))

    first_in.wait()
    work(0, True)
    second_in.wait()
    for copy in cot_in:
        copy.wait()

    def turn(index, carried):
        norm(index - 1)
        work(index, False)
        return carried

    lax.fori_loop(1, rows // tile, turn, 0)
    norm(rows // tile - 1)
    outer(act_s, grad_low_s, out_s, (send_ref, keep_ref), out_sems)
    for index in range(rows // tile):
        for copy in tile_copies(index):
            copy.wait()


def outer(left_s, right_s, out_s, targets, sems, loads=()):
    places = [
        ref.at[pl.ds(row, HIDDEN_STEP), :]
        for ref in targets
        for row in range(0, ref.shape[0], HIDDEN_STEP)
    ]
    copies = []
    for step, target in enumerate(places):
        spot = pl.ds(step * HIDDEN_STEP, HIDDEN_STEP)
        if loads:
            loads[step].wait()
        out_s[spot, :] = tn(left_s[:, spot], right_s[...]).astype(LOW)
        copies.append(pltpu.make_async_copy(out_s.at[spot, :], target, sems.at[step]))
        copies[-1].start()
    for copy in copies:
        copy.wait()


def feed_forward(place, mids, cot, got, marks, wu, bu, wd, vectors, *earlier):
    length, width = mids[0].shape
    rows = length * len(mids)
    pieces = len(got) + 1
    hidden = wu.shape[1]
    half = hidden // 2
    chunks = hidden // HIDDEN_STEP
    shapes = (
        jax.ShapeDtypeStruct((rows, hidden), LOW),
        jax.ShapeDtypeStruct((rows, width), LOW),
        jax.ShapeDtypeStruct((rows, width), LOW),
        jax.ShapeDtypeStruct((rows, width), WIDE),
        jax.ShapeDtypeStruct((rows, width), LOW),
        jax.ShapeDtypeStruct((half, width), LOW),
        jax.ShapeDtypeStruct((half, width), LOW),
        jax.ShapeDtypeStruct((8, width), WIDE),
        jax.ShapeDtypeStruct((8, 128), WIDE),
    )
    return pl.pallas_call(
        ignoring(functools.partial(feed_kernel, pieces=pieces), 8 + pieces, len(earlier)),
        out_shape=shapes,
        in_specs=[IN_SMEM] + [ANY] * 3 + [IN_VMEM] * 3 + [ANY] * (1 + pieces + len(earlier)),
        out_specs=(ANY,) * 7 + (IN_VMEM,) * 2,
        scratch_shapes=[
            pltpu.VMEM((rows, width), WIDE),
            pltpu.VMEM((rows, width), LOW),
            pltpu.VMEM((width, hidden), LOW),
            pltpu.VMEM((hidden, width), LOW),
            pltpu.VMEM((rows, hidden), LOW),
            pltpu.VMEM((rows, hidden), LOW),
            pltpu.VMEM((rows, width), LOW),
            pltpu.VMEM((rows, width), LOW),
            pltpu.VMEM((rows, width), WIDE),
            pltpu.VMEM((rows, width), LOW),
            pltpu.VMEM((hidden, width), LOW),
            pltpu.VMEM((TILE, width), WIDE),
            pltpu.VMEM((rows, 1), WIDE),
            pltpu.SemaphoreType.DMA((2 + pieces * len(mids),)),
            pltpu.SemaphoreType.DMA((chunks,)),
            pltpu.SemaphoreType.DMA((chunks,)),
            pltpu.SemaphoreType.DMA((6, rows // TILE)),
            pltpu.SemaphoreType.DMA((chunks,)),
        ],
        compiler_params=pltpu.CompilerParams(vmem_limit_bytes=VMEM_LIMIT),
        cost_estimate=cost(),
        name="feed_forward",
    )(place, mids[0], mids[1], cot, marks, bu, vectors, wu, wd, *got, *earlier)


def feed_back_kernel(
    place_ref, grad_low_ref, grad_ref, slope_ref, norm0_ref, norm1_ref, wu_ref, wd_ref,
    wo_ref, rstd0_ref, rstd1_ref, vectors_ref,
    grad_one_ref, attn_ref, ctx_ref, hid_ref, up_sums_ref, sums_ref,
    grad_low_s, grad_s, slope_s, norm_s, wu_s, wd_s, wo_s, rstd_s, grad_one_s, attn_s,
    ctx_s, middle_s,
    in_sems, slope_sems, up_sems, down_sems, tile_sems, ctx_sems,
):
    length = norm0_ref.shape[0]
    rows, width = grad_low_ref.shape
    hidden = wu_ref.shape[1]
    half = hidden // 2
    chunks = hidden // HIDDEN_STEP
    tile = TILE
    marks = [[1 - place_ref[n], place_ref[n]] for n in range(2)]
    each = hidden // 4

    def place_of(chunk):
        quarter, inside = divmod(chunk * HIDDEN_STEP, each)
        start = marks[0][quarter // 2] * half + marks[1][quarter % 2] * each + inside
        return pl.ds(pl.multiple_of(start, HIDDEN_STEP), HIDDEN_STEP)

    def own(chunk):
        return pl.ds(chunk * HIDDEN_STEP, HIDDEN_STEP)

    def spot_of(index):
        return pl.ds(pl.multiple_of(index * tile, tile), tile)

    slopes = [
        pltpu.make_async_copy(
            slope_ref.at[spot_of(i), place_of(c)],
            slope_s.at[spot_of(i), own(c)],
            slope_sems.at[chunks * i + c],
        )
        for i in range(rows // tile)
        for c in range(chunks)
    ]
    ups = [
        pltpu.make_async_copy(wu_ref.at[:, place_of(c)], wu_s.at[:, own(c)], up_sems.at[c])
        for c in range(chunks)
    ]
    downs = [
        pltpu.make_async_copy(wd_ref.at[place_of(c), :], wd_s.at[own(c), :], down_sems.at[c])
        for c in range(chunks)
    ]
    others = [
        pltpu.make_async_copy(a, b, in_sems.at[n])
        for n, (a, b) in enumerate(
            (
                (grad_low_ref, grad_low_s),
                (grad_ref, grad_s),
                (norm0_ref, norm_s.at[pl.ds(0, length)]),
                (norm1_ref, norm_s.at[pl.ds(length, length)]),
                (wo_ref, wo_s),
            )
        )
    ]
    others[0].start()
    downs[0].start()
    slopes[0].start()
    ups[0].start()
    for chunk in range(1, chunks):
        downs[chunk].start()
        slopes[chunk].start()
        ups[chunk].start()
    for copy in others[1:5] + slopes[chunks:]:
        copy.start()
    rstd_s[pl.ds(0, length), :] = rstd0_ref[...]
    rstd_s[pl.ds(length, length), :] = rstd1_ref[...]
    sums_ref[...] = jnp.zeros_like(sums_ref)
    up_sums_ref[...] = jnp.zeros_like(up_sums_ref)

    def tile_copies(index):
        spot = spot_of(index)
        pairs = ((grad_one_s, grad_one_ref), (attn_s, attn_ref), (slope_s, hid_ref))
        return [
            pltpu.make_async_copy(a.at[spot, :], b.at[spot, :], tile_sems.at[n, index])
            for n, (a, b) in enumerate(pairs)
        ]

    def inside(index, row, count=ROWS):
        return pl.ds(pl.multiple_of(index * tile + row, count), count)

    def work(index, opening):
        spot = spot_of(index)
        grad_low = grad_low_s[spot, :]

        def back(chunk):
            if opening:
                downs[chunk].wait()
            return nt(grad_low, wd_s[own(chunk), :])

        def forth(chunk, grad):
            if opening:
                ups[chunk].wait()
            more = nt(slope_s[spot, own(chunk)], wu_s[:, own(chunk)])
            return more if grad is None else grad + more

        ahead = back(0)
        grad_middle = None
        for chunk in range(chunks):
            if opening:
                slopes[chunk].wait()
            sums = jnp.zeros((8, HIDDEN_STEP), WIDE)
            for row in range(0, tile, ROWS):
                at = inside(index, row)
                slope = slope_s[at, own(chunk)].astype(WIDE)
                grad_hidden = (ahead[row : row + ROWS] * slope).astype(LOW)
                slope_s[at, own(chunk)] = grad_hidden
                sums = sums + jnp.sum(
                    grad_hidden.astype(WIDE).reshape(-1, 8, HIDDEN_STEP), axis=0
                )
            up_sums_ref[:, place_of(chunk)] += sums
            if chunk + 1 < chunks:
                ahead = back(chunk + 1)
            if chunk > 0:
                grad_middle = forth(chunk - 1, grad_middle)
        middle_s[...] = forth(chunks - 1, grad_middle)

    def norm(index):
        gain = vector(vectors_ref, "gain_one")
        sums = [jnp.zeros((1, width), WIDE) for _ in range(3)]
        for row in range(0, tile, ROWS_NORM):
            at = inside(index, row, ROWS_NORM)
            grad = middle_s[row : row + ROWS_NORM, :] + grad_s[at, :]
            normal = norm_s[at, :].astype(WIDE)
            grad_one = norm_back(grad, normal, rstd_s[at, :], gain)
            grad_one_s[at, :] = grad_one
            attn = grad_one.astype(LOW)
            attn_s[at, :] = attn
            sums[0] = sums[0] + row_total(grad * normal)
            sums[1] = sums[1] + row_total(grad)
            sums[2] = sums[2] + row_total(attn.astype(WIDE))
        for copy in tile_copies(index):
            copy.start()
        for n in range(3):
            sums_ref[n : n + 1, :] += sums[n]

    def project(index):
        spot = spot_of(index)
        turned = nt(wo_s[...], attn_s[spot, :]).astype(LOW)
        slot, inner = divmod(index * tile, length)
        ctx_s[slot, :, inner : inner + tile] = turned
        copy = pltpu.make_async_copy(
            ctx_s.at[slot, :, pl.ds(inner, tile)], ctx_ref.at[slot, :, pl.ds(inner, tile)],
            ctx_sems.at[index],
        )
        copy.start()
        return copy

    others[0].wait()
    work(0, True)
    for copy in slopes[chunks:] + others[1:5]:
        copy.wait()

    def turn(index, carried):
        norm(index - 1)
        work(index, False)
        return carried

    lax.fori_loop(1, rows // tile, turn, 0)
    norm(rows // tile - 1)
    copies = [project(index) for index in range(rows // tile)]
    for copy in copies:
        copy.wait()
    for index in range(rows // tile):
        for copy in tile_copies(index):
            copy.wait()


def feed_back(place, grad_low, grad, slope, norms, rstds, wu, wd, wo, vectors, *earlier):
    rows, width = grad.shape
    length = norms[0].shape[0]
    hidden = wu.shape[1]
    chunks = hidden // HIDDEN_STEP
    shapes = (
        jax.ShapeDtypeStruct((rows, width), WIDE),
        jax.ShapeDtypeStruct((rows, width), LOW),
        jax.ShapeDtypeStruct((rows // length, width, length), LOW),
        jax.ShapeDtypeStruct((rows, hidden), LOW),
        jax.ShapeDtypeStruct((8, hidden), WIDE),
        jax.ShapeDtypeStruct((8, width), WIDE),
    )
    return pl.pallas_call(
        ignoring(feed_back_kernel, 12, len(earlier)),
        out_shape=shapes,
        in_specs=[IN_SMEM] + [ANY] * 8 + [IN_VMEM] * 3 + [ANY] * len(earlier),
        out_specs=(ANY,) * 4 + (IN_VMEM,) * 2,
        scratch_shapes=[
            pltpu.VMEM((rows, width), LOW),
            pltpu.VMEM((rows, width), WIDE),
            pltpu.VMEM((rows, hidden), LOW),
            pltpu.VMEM((rows, width), LOW),
            pltpu.VMEM((width, hidden), LOW),
            pltpu.VMEM((hidden, width), LOW),
            pltpu.VMEM((width, width), LOW),
            pltpu.VMEM((rows, 1), WIDE),
            pltpu.VMEM((rows, width), WIDE),
            pltpu.VMEM((rows, width), LOW),
            pltpu.VMEM((rows // length, width, length), LOW),
            pltpu.VMEM((TILE, width), WIDE),
            pltpu.SemaphoreType.DMA((5,)),
            pltpu.SemaphoreType.DMA((chunks * rows // TILE,)),
            pltpu.SemaphoreType.DMA((chunks,)),
            pltpu.SemaphoreType.DMA((chunks,)),
            pltpu.SemaphoreType.DMA((3, rows // TILE)),
            pltpu.SemaphoreType.DMA((rows // TILE,)),
        ],
        compiler_params=pltpu.CompilerParams(vmem_limit_bytes=VMEM_LIMIT),
        cost_estimate=cost(),
        name="feed_back",
    )(
        place, grad_low, grad, slope, norms[0], norms[1], wu, wd, wo, rstds[0], rstds[1],
        vectors, *earlier,
    )


def up_grads_kernel(
    hid_ref, low_ref, early_ref, late_ref, keep_ref, hid_s, low_s, out_s, in_sems, out_sems
):
    steps = hid_ref.shape[1] // HIDDEN_STEP
    low_in = pltpu.make_async_copy(low_ref, low_s, in_sems.at[steps])
    low_in.start()
    loads = []
    for step in range(steps):
        spot = pl.ds(step * HIDDEN_STEP, HIDDEN_STEP)
        copy = pltpu.make_async_copy(hid_ref.at[:, spot], hid_s.at[:, spot], in_sems.at[step])
        copy.start()
        loads.append(copy)
    low_in.wait()
    outer(hid_s, low_s, out_s, (early_ref, late_ref, keep_ref), out_sems, loads)


def up_grads(hid, mid_low, *earlier):
    rows, hidden = hid.shape
    width = mid_low.shape[1]
    quarter = jax.ShapeDtypeStruct((hidden // 4, width), LOW)
    chunks = hidden // HIDDEN_STEP
    return pl.pallas_call(
        ignoring(up_grads_kernel, 2, len(earlier)),
        out_shape=(quarter, quarter, jax.ShapeDtypeStruct((hidden // 2, width), LOW)),
        in_specs=[ANY] * (2 + len(earlier)),
        out_specs=(ANY,) * 3,
        scratch_shapes=[
            pltpu.VMEM((rows, hidden), LOW),
            pltpu.VMEM((rows, width), LOW),
            pltpu.VMEM((hidden, width), LOW),
            pltpu.SemaphoreType.DMA((chunks + 1,)),
            pltpu.SemaphoreType.DMA((chunks,)),
        ],
        compiler_params=pltpu.CompilerParams(vmem_limit_bytes=VMEM_LIMIT),
        cost_estimate=cost(),
        name="up_grads",
    )(hid, mid_low, *earlier)


def attend_back_kernel(
    place_ref, seg_ref, mark_ref, lse_ref, q_ref, k_ref, v_ref, ctx_ref, grad_ctx_ref, grad_one_ref, wq_ref,
    wk_ref, wv_ref,
    dq_ref, dk_ref, dv_ref, grad_in_ref, sums_ref,
    q_s, k_s, v_s, ctx_s, grad_ctx_s, grad_one_s, wq_s, wk_s, wv_s, bias_s, score_s, pull_s,
    chance_s, grad_s, in_sems,
):
    length, model = q_ref.shape
    slot = place_ref[0]
    heads = model // HEAD_DIM
    width = 2 * HEAD_DIM
    loads = [
        pltpu.make_async_copy(a, b, in_sems.at[n])
        for n, (a, b) in enumerate(
            (
                (k_ref, k_s), (q_ref, q_s), (v_ref, v_s), (grad_ctx_ref.at[slot], grad_ctx_s),
                (ctx_ref, ctx_s), (wq_ref, wq_s), (wk_ref, wk_s), (wv_ref, wv_s),
                (grad_one_ref.at[pl.ds(pl.multiple_of(slot * length, length), length), :], grad_one_s),
            )
        )
    ]
    for load in loads:
        load.start()
    mark_col = column(mark_ref[pl.ds(slot, 1), :])
    fill_bias(bias_s, seg_ref[pl.ds(slot, 1), :].astype(WIDE), mark_col)

    def lanes(head):
        return pl.ds(head // 2 * width, width)

    def rows_of(head):
        return pl.ds(head * HEAD_DIM, HEAD_DIM)

    def products(head):
        score_s[head % 2] = nt(k_s[:, lanes(head)] * lane_half(head % 2), q_s[:, lanes(head)])
        values = v_s[:, lanes(head)] * lane_half(head % 2)
        pull_s[head % 2] = nn(values, grad_ctx_s[lanes(head), :])

    def soften(head):
        score, pull = score_s.at[head % 2], pull_s.at[head % 2]
        chance, grad = chance_s.at[head % 2], grad_s.at[head % 2]
        shared = grad_ctx_s[rows_of(head), :].astype(WIDE) * ctx_s[rows_of(head), :].astype(WIDE)
        delta = jnp.sum(shared, axis=0, keepdims=True)
        lse = lse_ref[head : head + 1, :]
        for row in range(0, length, ROWS):
            at = slice(row, row + ROWS)
            block = jnp.exp(score[at, :] + bias_s[at, :] - lse)
            chance[at, :] = block.astype(LOW)
            grad[at, :] = (block * (pull[at, :] - delta)).astype(LOW)

    def combine(head, turned):
        part_v = nt(chance_s[head % 2], grad_ctx_s[lanes(head), :])
        part_k = nn(grad_s[head % 2], q_s[:, lanes(head)])
        part = turned[head % 2 * HEAD_DIM : (head % 2 + 1) * HEAD_DIM]
        return part_v, part_k, nn(part, grad_s[head % 2])

    def keep(head, one, two):
        first = lax.broadcasted_iota(jnp.int32, one[0].shape, 1) < HEAD_DIM
        dv_ref[:, lanes(head)] = jnp.where(first, one[0], two[0]).astype(LOW)
        dk_ref[:, lanes(head)] = jnp.where(first, one[1], two[1]).astype(LOW)
        dq_ref[:, lanes(head)] = jnp.concatenate([one[2], two[2]], axis=0).T.astype(LOW)

    for load in loads[:4]:
        load.wait()
    products(0)
    loads[4].wait()
    waiting = None
    found = []
    for head in range(heads):
        soften(head)
        if head % 2 == 0:
            turned = k_s[:, lanes(head)].T
        if len(found) == 2:
            keep(head - 2, *found)
            found = []
        if head + 1 < heads:
            products(head + 1)
        if waiting is not None:
            found.append(combine(*waiting))
        waiting = (head, turned)
    found.append(combine(*waiting))
    keep(heads - 1, *found)
    for load in loads[5:]:
        load.wait()
    grad_in_ref[...] = (
        grad_one_s[...]
        + nt(dq_ref[...], wq_s[...]) * SCORE_SCALE
        + nt(dk_ref[...], wk_s[...])
        + nt(dv_ref[...], wv_s[...])
    )
    sums_ref[...] = jnp.concatenate(
        [
            row_total(dq_ref[...].astype(WIDE)) * SCORE_SCALE,
            row_total(dv_ref[...].astype(WIDE)),
            jnp.zeros((6, model), WIDE),
        ],
        axis=0,
    )


def attend_back(place, q, k, v, ctx, grad_ctx, lse, segs, marks, grad_one, wq, wk, wv, *earlier):
    length, width = q.shape
    heads = width // HEAD_DIM
    shapes = (
        jax.ShapeDtypeStruct((length, width), LOW),
        jax.ShapeDtypeStruct((length, width), LOW),
        jax.ShapeDtypeStruct((length, width), LOW),
        jax.ShapeDtypeStruct((length, width), WIDE),
        jax.ShapeDtypeStruct((8, width), WIDE),
    )
    tokens = pltpu.VMEM((length, width), LOW)
    turned = pltpu.VMEM((width, length), LOW)
    weight = pltpu.VMEM((width, width), LOW)
    return pl.pallas_call(
        ignoring(attend_back_kernel, 13, len(earlier)),
        out_shape=shapes,
        in_specs=[IN_SMEM] + [IN_VMEM] * 3 + [ANY] * (9 + len(earlier)),
        out_specs=(IN_VMEM,) * 5,
        scratch_shapes=[
            tokens, tokens, tokens, turned, turned, pltpu.VMEM((length, width), WIDE),
            weight, weight, weight,
            pltpu.VMEM((length, length), WIDE),
            pltpu.VMEM((2, length, length), WIDE),
            pltpu.VMEM((2, length, length), WIDE),
            pltpu.VMEM((2, length, length), LOW),
            pltpu.VMEM((2, length, length), LOW),
            pltpu.SemaphoreType.DMA((9,)),
        ],
        compiler_params=pltpu.CompilerParams(vmem_limit_bytes=VMEM_LIMIT),
        cost_estimate=cost(),
        name="attend_back",
    )(place, segs, marks, lse, q, k, v, ctx, grad_ctx, grad_one, wq, wk, wv, *earlier)


def square_kernel(
    place_ref, x0_ref, x1_ref, dq0_ref, dq1_ref, dk0_ref, dk1_ref, dv0_ref, dv1_ref, ctx0_ref,
    ctx1_ref, attn_ref, send_ref, keep_ref, x_s, dq_s, dk_s, dv_s, ctx_s, attn_s, out_s, in_sems,
    out_sems,
):
    length, width = x0_ref.shape
    first, second = pl.ds(0, length), pl.ds(length, length)
    loads = []
    for a, b in (
        (x0_ref, x_s.at[first]), (x1_ref, x_s.at[second]), (dv0_ref, dv_s.at[first]),
        (dv1_ref, dv_s.at[second]), (dq0_ref, dq_s.at[first]), (dq1_ref, dq_s.at[second]),
        (ctx0_ref, ctx_s.at[:, first]), (ctx1_ref, ctx_s.at[:, second]), (attn_ref, attn_s),
        (dk0_ref, dk_s.at[first]), (dk1_ref, dk_s.at[second]),
    ):
        loads.append(pltpu.make_async_copy(a, b, in_sems.at[len(loads)]))
        loads[-1].start()
    mine = place_ref[0] == 0
    x = x_s[...]
    step = 256
    copies = []

    def place(part, columns, low, high):
        for n, (ref, kept) in enumerate(((send_ref, False), (keep_ref, True))):
            spot = pl.ds((n * 2 + part) * width, width)
            out_s[spot, columns] = jnp.where(mine == kept, low, high).astype(LOW)

    def flush(part):
        for n, ref in enumerate((send_ref, keep_ref)):
            spot = pl.ds((n * 2 + part) * width, width)
            copies.append(
                pltpu.make_async_copy(
                    out_s.at[spot, :], ref.at[pl.ds(part * width, width), :],
                    out_sems.at[len(copies)],
                )
            )
            copies[-1].start()

    for load in loads[:6]:
        load.wait()
    x = x_s[...]
    for start in range(0, width, step):
        columns = pl.ds(start, step)
        place(0, columns, tn(x, dq_s[:, columns]) * SCORE_SCALE, tn(x, dv_s[:, columns]))
    flush(0)
    for load in loads[6:]:
        load.wait()
    for start in range(0, width, step):
        columns = pl.ds(start, step)
        place(1, columns, tn(x, dk_s[:, columns]), nn(ctx_s[...], attn_s[:, columns]))
    flush(1)
    for copy in copies:
        copy.wait()


def square_grads(place, xs, dqs, dks, dvs, ctxs, attn, *earlier):
    length, width = xs[0].shape
    rows = length * len(xs)
    tokens = pltpu.VMEM((rows, width), LOW)
    out = jax.ShapeDtypeStruct((2 * width, width), LOW)
    return pl.pallas_call(
        ignoring(square_kernel, 12, len(earlier)),
        out_shape=(out, out),
        in_specs=[IN_SMEM] + [ANY] * (11 + len(earlier)),
        out_specs=(ANY, ANY),
        scratch_shapes=[
            tokens, tokens, tokens, tokens, pltpu.VMEM((width, rows), LOW), tokens,
            pltpu.VMEM((4 * width, width), LOW),
            pltpu.SemaphoreType.DMA((11,)),
            pltpu.SemaphoreType.DMA((4,)),
        ],
        compiler_params=pltpu.CompilerParams(vmem_limit_bytes=VMEM_LIMIT),
        cost_estimate=cost(),
        name="square_grads",
    )(place, *xs, *dqs, *dks, *dvs, *ctxs, attn, *earlier)


def pick_kernel(place_ref, value_ref, out_ref):
    out_ref[...] = value_ref[0]


def pick(value, place, *earlier):
    shape = value.shape[1:]
    if len(shape) == 1:
        return lax.dynamic_index_in_dim(value, place, 0, keepdims=False)
    return pl.pallas_call(
        ignoring(pick_kernel, 2, len(earlier)),
        out_shape=jax.ShapeDtypeStruct(shape, value.dtype),
        grid_spec=pltpu.PrefetchScalarGridSpec(
            num_scalar_prefetch=1,
            grid=(1,),
            in_specs=[pl.BlockSpec((1,) + shape, lambda i, p: (p[0], 0, 0))] + [ANY] * len(earlier),
            out_specs=pl.BlockSpec(shape, lambda i, p: (0, 0)),
        ),
        cost_estimate=cost(),
        name="pick",
    )(place.astype(jnp.int32).reshape(1), value, *earlier)


def other_pieces(value, slot, slots, *earlier):
    count = lax.axis_size("seq")
    me = lax.axis_index("seq")
    found = []
    for shift in range(1, count):
        block = pick(value, (me + shift) % count * slots + slot, *earlier)
        pairs = [(source, (source + shift) % count) for source in range(count)]
        found.append(lax.ppermute(block, "seq", pairs))
    return found


def send_back(value, piece):
    count = lax.axis_size("seq")
    found = []
    for shift in range(1, count):
        part = value[:, shift * piece : (shift + 1) * piece].astype(LOW)
        pairs = [(source, (source - shift) % count) for source in range(count)]
        found.append(lax.ppermute(part, "seq", pairs))
    return found


def join_kernel(me_ref, *refs, slots):
    out_ref = refs[-1]
    count = len(refs) - 1
    owner = pl.program_id(0) // slots
    shift = lax.rem(owner - me_ref[0] + count, count)
    for n, ref in enumerate(refs[:-1]):

        @pl.when(shift == n)
        def _(ref=ref):
            out_ref[...] = ref[...].astype(out_ref.dtype)


def join(me, own, got, *earlier):
    slots, _, width = own.shape
    piece = got[0].shape[1]
    count = len(got) + 1
    spec = pl.BlockSpec((1, piece, width), lambda i, p: (lax.rem(i, slots), 0, 0))
    return pl.pallas_call(
        ignoring(functools.partial(join_kernel, slots=slots), 1 + count, len(earlier)),
        out_shape=jax.ShapeDtypeStruct((slots * count, piece, width), own.dtype),
        grid_spec=pltpu.PrefetchScalarGridSpec(
            num_scalar_prefetch=1,
            grid=(slots * count,),
            in_specs=[spec] * count + [ANY] * len(earlier),
            out_specs=pl.BlockSpec((1, piece, width), lambda i, p: (i, 0, 0)),
        ),
        compiler_params=pltpu.CompilerParams(vmem_limit_bytes=VMEM_LIMIT),
        cost_estimate=cost(),
        name="join",
    )(me, own, *got, *earlier)


def swap(value, axis, bit):
    count = lax.axis_size(axis)
    return lax.ppermute(value, axis, [(source, source ^ bit) for source in range(count)])


def bit_of(axis, bit):
    return (lax.axis_index(axis) // bit) % 2


CORE = ("dp", 1)
HALVINGS = 5
STEP_ROWS = 32


def chip_axes():
    dp, seq = lax.axis_size("dp"), lax.axis_size("seq")
    along_dp = [("dp", 2**i) for i in range(1, dp.bit_length() - 1)]
    along_seq = [("seq", 2**i) for i in range(seq.bit_length() - 1)]
    return along_dp[0], along_seq[0], along_dp[1], along_dp[2:] + along_seq[1:]


class Chain:
    def __init__(self, bits):
        self.last = ()
        self.bits = bits

    def run(self, function, *args):
        out = function(*args, *self.last)
        arrays = out if isinstance(out, (tuple, list)) else (out,)
        self.last = (min(arrays, key=lambda array: array.size),)
        return out

    def round(self, *tasks):
        outs = list(self.run(round_call, self.bits, [task[:-1] for task in tasks]))
        for task in tasks:
            count = 2 if task[0] == "halve" else 1
            task[-1](*[outs.pop(0) for _ in range(count)])


def add_rows(first, first_start, second, second_start, out, rows):
    def step(index, carried):
        spots = [
            pl.ds(pl.multiple_of(start + index * STEP_ROWS, STEP_ROWS), STEP_ROWS)
            for start in (first_start, second_start, 0)
        ]
        both = first[spots[0], :].astype(WIDE) + second[spots[1], :].astype(WIDE)
        out[spots[2], :] = both.astype(LOW)
        return carried

    lax.fori_loop(0, rows // STEP_ROWS, step, 0)


def round_kernel(bits_ref, *refs, plan, inputs):
    outs = list(refs[inputs:])
    for kind, places, meta in plan:
        first, second = refs[places[0]], refs[places[1]]
        if kind == "halve":
            rows, offset, which = meta
            mine = bits_ref[which]
            for bit in (1 - mine, mine):
                start = offset + bit * rows
                add_rows(first, start, second, start, outs.pop(0), rows)
        elif kind == "add":
            add_rows(first, meta, second, 0, outs.pop(0), second.shape[0])
        elif kind == "merge":
            rows = first.shape[0]
            out = outs.pop(0)
            out[:rows, :] = first[...]
            out[rows:, :] = second[...]
        else:
            outs.pop(0)[...] = first[...] + second[...]


def round_call(bits, tasks, *earlier):
    arrays, plan, shapes = [], [], []
    for kind, pair, meta in tasks:
        places = []
        for array in pair:
            known = [n for n, other in enumerate(arrays) if other is array]
            if not known:
                arrays.append(array)
            places.append(known[0] if known else len(arrays) - 1)
        plan.append((kind, places, meta))
        rows, width = pair[0].shape
        if kind == "halve":
            shapes += [jax.ShapeDtypeStruct((meta[0], width), LOW)] * 2
        elif kind == "merge":
            shapes.append(jax.ShapeDtypeStruct((2 * rows, width), LOW))
        elif kind == "add":
            shapes.append(jax.ShapeDtypeStruct(pair[1].shape, LOW))
        else:
            shapes.append(jax.ShapeDtypeStruct((rows, width), pair[0].dtype))
    return pl.pallas_call(
        ignoring(
            functools.partial(round_kernel, plan=plan, inputs=len(arrays)),
            1 + len(arrays),
            len(earlier),
        ),
        out_shape=tuple(shapes),
        in_specs=[IN_SMEM] + [IN_VMEM] * len(arrays) + [ANY] * len(earlier),
        out_specs=(IN_VMEM,) * len(shapes),
        compiler_params=pltpu.CompilerParams(vmem_limit_bytes=VMEM_LIMIT),
        cost_estimate=cost(),
        name="round",
    )(bits, *arrays, *earlier)


class Reduction:
    def __init__(self, kept, got, order, names, offset=0, count=None):
        self.order, self.names = order, names
        self.first, self.second = kept, got
        self.count = kept.shape[0] if count is None else count
        self.offset = offset
        self.step = 1
        self.back = [axis for axis in order[:HALVINGS] if axis != CORE]

    def send(self):
        axis = self.order[self.step]
        rows, offset = self.count // 2, self.offset

        def found(sent, kept):
            self.first, self.second = kept, swap(sent, *axis)
            self.count, self.offset = rows, 0
            self.step += 1

        meta = (rows, offset, self.names.index(axis))
        return "halve", (self.first, self.second), meta, found

    def send_early(self, early):
        axis = self.order[self.step]

        def found(sent):
            self.sent = swap(sent, *axis)

        return "add", (self.first, early), 0, found

    def send_late(self, late):
        def found(kept):
            self.first, self.second = kept, self.sent
            self.count, self.offset = late.shape[0], 0
            self.step += 1

        return "add", (self.first, late), late.shape[0], found

    def share(self):
        def found(share):
            self.have = share
            if self.step < len(self.order):
                self.first, self.second = share, swap(share, *self.order[self.step])
                self.step += 1
            else:
                self.step = len(self.back) - 1
                self.got = swap(share, *self.back[self.step])

        return "add", (self.first, self.second), 0, found

    def more_shares(self):
        return len(self.order) - HALVINGS

    def gather(self):
        def found(merged):
            self.step -= 1
            self.have, self.got = merged, swap(merged, *self.back[self.step])

        return "merge", (self.have, self.got), None, found

    def halves(self):
        return [self.have, self.got, swap(self.have, *CORE), swap(self.got, *CORE)]

    def place(self):
        place = 0
        for axis in self.back:
            place = place * 2 + bit_of(*axis)
        return place.astype(jnp.int32)


def found_block(core, me, refs, index, core_place):
    near_own, far_own, near_other, far_other = refs
    blocks = 1 << (HALVINGS - 2)
    block = near_own.shape[0] // blocks
    below = HALVINGS - 1 - core_place
    owner = (index >> below) & 1
    rest = ((index >> (below + 1)) << below) | (index & ((1 << below) - 1))
    spot = rest ^ me
    rows = pl.ds(pl.multiple_of(lax.rem(spot, blocks) * block, block), block)
    near = jnp.where(core == owner, near_own[rows, :], near_other[rows, :])
    far = jnp.where(core == owner, far_own[rows, :], far_other[rows, :])
    return jnp.where(spot < blocks, near, far).astype(WIDE)


def finish_kernel(place_ref, *refs, turned, core_place):
    refs, out_ref = refs[:4], refs[4]
    block = refs[0].shape[0] >> (HALVINGS - 2)
    count = out_ref.shape[1 if turned else 0] // block
    tile = pl.program_id(0)
    found = [
        found_block(place_ref[0], place_ref[1], refs, tile * count + j, core_place)
        for j in range(count)
    ]
    if turned:
        out_ref[...] = jnp.concatenate(found, axis=0).T
    else:
        for j in range(count):
            out_ref[j * block : (j + 1) * block, :] = found[j]


def finish(place, arrays, turned, core_place, *earlier):
    rows, width = arrays[0].shape
    tile = rows // 2
    if turned:
        shape = (width, 4 * rows)
        spec = pl.BlockSpec((width, tile), lambda t, *_: (0, t))
    else:
        shape = (4 * rows, width)
        spec = pl.BlockSpec((tile, width), lambda t, *_: (t, 0))
    return pl.pallas_call(
        ignoring(
            functools.partial(finish_kernel, turned=turned, core_place=core_place),
            5,
            len(earlier),
        ),
        out_shape=jax.ShapeDtypeStruct(shape, WIDE),
        grid_spec=pltpu.PrefetchScalarGridSpec(
            num_scalar_prefetch=1,
            grid=(8,),
            in_specs=[whole(array.shape) for array in arrays] + [ANY] * len(earlier),
            out_specs=spec,
        ),
        compiler_params=pltpu.CompilerParams(vmem_limit_bytes=VMEM_LIMIT),
        cost_estimate=cost(),
        name="finish",
    )(place, *arrays, *earlier)


def finish_square_kernel(place_ref, *refs):
    parts = (len(refs) - 4) // 4
    out_refs = refs[4 * parts :]
    width = refs[0].shape[1]
    block = refs[0].shape[0] >> (HALVINGS - 2)
    each = block << (HALVINGS - 1)
    for half in range(2):
        for row in range(0, each * parts, block):
            part = row // each
            index = (row - part * each) // block + (half << (HALVINGS - 1))
            out = out_refs[half * 2 + row // width]
            out[row % width : row % width + block, :] = found_block(
                place_ref[0], place_ref[1 + part], refs[4 * part : 4 * part + 4], index, 0
            )


def finish_square(place, parts, *earlier):
    width = parts[0][0].shape[1]
    shape = jax.ShapeDtypeStruct((width, width), WIDE)
    args = [array for part in parts for array in part]
    return pl.pallas_call(
        ignoring(finish_square_kernel, 1 + len(args), len(earlier)),
        out_shape=(shape,) * 4,
        grid_spec=pltpu.PrefetchScalarGridSpec(
            num_scalar_prefetch=1,
            grid=(1,),
            in_specs=[whole(arg.shape) for arg in args] + [ANY] * len(earlier),
            out_specs=(whole(shape.shape),) * 4,
        ),
        compiler_params=pltpu.CompilerParams(vmem_limit_bytes=VMEM_LIMIT),
        cost_estimate=cost(),
        name="finish_square",
    )(place, *args, *earlier)


def on_device(
    inputs, cotangent, w_query, b_query, w_key, w_value, b_value, w_out, b_out, gain_one,
    shift_one, w_up, b_up, w_down, b_down, gain_two, shift_two, live_counts, valid_mask, segments,
):
    seqs, piece, width = inputs.shape
    count = lax.axis_size("seq")
    me = lax.axis_index("seq").astype(jnp.int32)
    slots = seqs // count
    length = piece * count
    x, y, z, rest = chip_axes()
    names = [CORE, x, y, z] + rest
    bits = jnp.stack([bit_of(*axis).astype(jnp.int32) for axis in names])
    core = bits[0]
    chain = Chain(bits)
    chain.last = (segments,)
    base = (me * slots).reshape(1)

    x_got = []
    for slot in range(slots):
        x_got.append(other_pieces(inputs, slot, slots, *(x_got[-1][-1:] if x_got else ())))
    vectors = jnp.concatenate(
        [v.reshape(1, -1) for v in (
            b_query, b_value, b_out, gain_one, shift_one, b_down, gain_two, shift_two
        )]
    ).astype(WIDE)
    bias_up = b_up.astype(WIDE).reshape(1, -1)
    live = (jnp.arange(seqs) < live_counts[0]).astype(jnp.int32)
    code = segments * 2 + valid_mask * live[:, None]
    codes = jnp.stack(
        [
            jnp.concatenate(
                [lax.dynamic_index_in_dim(code, base[0] + slot, 0, keepdims=False)]
                + other_pieces(code, slot, slots)
            )
            for slot in range(slots)
        ]
    )
    segs = codes // 2
    weight = codes % 2
    marks = jnp.where(weight > 0, segs, -1)

    forward = []
    for slot in range(slots):
        forward.append(
            chain.run(
                attend, jnp.stack([base[0], jnp.int32(slot)]), inputs, x_got[slot], segs, marks, vectors, w_query, w_key,
                w_value, w_out,
            )
        )
    cot_got = [[] for _ in range(count - 1)]
    for slot in range(slots):
        for n, got in enumerate(other_pieces(cotangent, slot, slots, x_got[-1][-1], forward[0][9])):
            cot_got[n].append(got)
    cot_got = [jnp.stack(got) for got in cot_got]
    (slope, mid_low, result, grad_h2, grad_feed, down_sent, down_kept, sums_two, stat_two) = (
        chain.run(
            feed_forward, jnp.concatenate([bits[1:2], base]), [each[6] for each in forward],
            cotangent, cot_got, marks, w_up, bias_up, w_down, vectors,
        )
    )
    down = Reduction(down_kept, swap(down_sent, *x), [x, CORE, z, y] + rest, names)
    result = result.reshape(slots, length, width)
    result_got = send_back(result, piece)
    grad_h1, grad_attn, grad_ctx, grad_hid, up_sums, sums_one = chain.run(
        feed_back, jnp.stack([bits[2], core]), grad_feed, grad_h2, slope,
        [each[7] for each in forward], [each[8] for each in forward], w_up, w_down, w_out,
        vectors,
    )
    up_early, up_late, up_kept = chain.run(up_grads, grad_hid, mid_low, *result_got)
    up_early, up_late = swap(up_early, *y), swap(up_late, *y)
    up = Reduction(up_kept, None, [y, CORE, x, z] + rest, names)
    backward = []
    for slot in range(slots):
        q, k, v, _, ctx, lse = forward[slot][:6]
        backward.append(
            chain.run(
                attend_back, jnp.full((1,), slot, jnp.int32), q, k, v, ctx, grad_ctx, lse, segs, marks, grad_h1, w_query,
                w_key, w_value,
            )
        )
    grad_inputs = jnp.stack([each[3] for each in backward])
    grad_got = send_back(grad_inputs, piece)
    stats = [
        sum(each[9][0, 0] for each in forward),
        sum(each[9][1, 0] for each in forward),
        stat_two[0, 0],
        stat_two[1, 0],
        jnp.sum(weight).astype(WIDE),
    ]
    stats = jnp.concatenate([jnp.stack(stats), jnp.zeros((width - 5,), WIDE)]).reshape(1, width)
    small = jnp.concatenate(
        [
            sum(each[4][0:2] for each in backward),
            sums_one[0:3],
            sums_two[0:3],
            stats,
            jnp.sum(up_sums, axis=0).reshape(-1, width),
        ],
        axis=0,
    )
    small_axes = [CORE, x, z, y] + rest
    small = [small, swap(small, *small_axes.pop(0))]

    def step_small():
        def found(total_so_far):
            small[:] = [total_so_far]
            if small_axes:
                small.append(swap(total_so_far, *small_axes.pop(0)))

        return "small", tuple(small), None, found

    chain.round(down.send())
    square_sent, square_kept = chain.run(
        square_grads, bits[0:1], [each[3] for each in forward],
        *([each[i] for each in backward] for i in range(3)), [each[4] for each in forward],
        grad_attn, up_early,
    )
    square_got = swap(square_sent, *CORE)
    third_orders = [[CORE, x, z, y] + rest, [CORE, y, x, z] + rest, [CORE, z, y, x] + rest]
    each_rows = square_kept.shape[0] // len(third_orders)
    thirds = [
        Reduction(square_kept, square_got, order, names, part * each_rows, each_rows)
        for part, order in enumerate(third_orders)
    ]

    def each_third(step):
        return [step(third) for third in thirds]

    chain.round(*each_third(Reduction.send), down.send(), up.send_early(up_early), step_small())
    chain.round(*each_third(Reduction.send), down.send(), up.send_late(up_late), step_small())
    chain.round(*each_third(Reduction.send), down.send(), up.send(), step_small())
    for _ in range(down.more_shares()):
        chain.round(down.share())
    chain.round(*each_third(Reduction.send), down.share(), up.send(), step_small())
    result_out = chain.run(join, me.reshape(1), result, result_got)
    for _ in range(down.more_shares()):
        chain.round(*each_third(Reduction.share))
    chain.round(*each_third(Reduction.share), down.gather(), up.send(), step_small())
    grad_out = chain.run(join, me.reshape(1), grad_inputs, grad_got)
    for _ in range(up.more_shares()):
        chain.round(up.share(), step_small())
    chain.round(*each_third(Reduction.gather), down.gather(), up.share())
    chain.round(*each_third(Reduction.gather), down.gather(), up.gather())
    chain.round(*each_third(Reduction.gather), up.gather())
    chain.round(up.gather())
    small = small[0]
    grad_w_down = chain.run(
        finish, jnp.stack([core, down.place()]), down.halves(), False, 1
    )
    squares = chain.run(
        finish_square, jnp.stack([core] + [third.place() for third in thirds]),
        [third.halves() for third in thirds],
    )
    grad_w_up = chain.run(finish, jnp.stack([core, up.place()]), up.halves(), True, 1)
    rms_values = jnp.sqrt(small[8, :4] / (width * small[8, 4]))
    return (
        result_out,
        grad_out,
        squares[0],
        small[0],
        squares[1],
        squares[2],
        small[1],
        squares[3],
        small[4],
        small[2],
        small[3],
        grad_w_up,
        small[9:].reshape(-1),
        grad_w_down,
        small[7],
        small[5],
        small[6],
        rms_values,
    )


def solution(mesh):
    split = P("dp", "seq", None)
    pair = P("dp", "seq")
    return jax.shard_map(
        on_device,
        mesh=mesh,
        in_specs=(split, split) + (P(),) * 15 + (P("dp"), pair, pair),
        out_specs=(split, split) + (P(),) * 16,
        check_vma=False,
    )
```

```python
import functools

import jax
import jax.numpy as jnp
from jax import lax
from jax.experimental import pallas as pl
from jax.experimental.pallas import tpu as pltpu
from jax.sharding import PartitionSpec as P

HEAD_DIM = 64
EPSILON = 1e-05
NEGATIVE = -1e30
SCORE_SCALE = 0.125
LOW = jnp.bfloat16
WIDE = jnp.float32
VMEM_LIMIT = 63 * 1024 * 1024
SMALL_LIMIT = 20 * 1024 * 1024
HIDDEN_STEP = 768
TILE = 256
ROWS = 32
ROWS_NORM = 16
ANY = pl.BlockSpec(memory_space=pltpu.HBM)
IN_VMEM = pl.BlockSpec(memory_space=pltpu.VMEM)
IN_SMEM = pl.BlockSpec(memory_space=pltpu.SMEM)

ERF_P = 0.3275911
ERF_C = (0.254829592, -0.284496736, 1.421413741, -1.453152027, 1.061405429)
ROOT_HALF = 0.7071067811865476
DENSITY = 0.3989422804014327


def nn(left, right):
    return jnp.dot(left, right, preferred_element_type=WIDE)


def nt(left, right):
    return lax.dot_general(
        left, right, (((1,), (1,)), ((), ())), preferred_element_type=WIDE
    )


def tn(left, right):
    return lax.dot_general(
        left, right, (((0,), (0,)), ((), ())), preferred_element_type=WIDE
    )


def gelu_pair(hidden):
    tail_exp = jnp.exp(hidden * hidden * -0.5)
    slow = 1.0 + (ERF_P * ROOT_HALF) * jnp.abs(hidden)
    t = pl.reciprocal(slow, approx=True)
    t = t * (2.0 - slow * t)
    c1, c2, c3, c4, c5 = (0.5 * c for c in ERF_C)
    tail = ((((c5 * t + c4) * t + c3) * t + c2) * t + c1) * t * tail_exp
    below = jnp.where(hidden >= 0.0, 1.0 - tail, tail)
    return hidden * below, below + hidden * (DENSITY * tail_exp)


def lane_half(half):
    lane = lax.broadcasted_iota(jnp.int32, (1, 2 * HEAD_DIM), 1)
    inside = (lane < HEAD_DIM) if half == 0 else (lane >= HEAD_DIM)
    return inside.astype(WIDE).astype(LOW)


def fill_bias(bias_ref, seg_row, mark_col):
    length = bias_ref.shape[0]
    key_place = lax.broadcasted_iota(jnp.int32, (length, length), 0)
    query_place = lax.broadcasted_iota(jnp.int32, (length, length), 1)
    visible = (mark_col == seg_row) | (key_place == query_place)
    bias_ref[...] = jnp.where(visible, 0.0, NEGATIVE)


def total(rows_weight, values):
    per_row = jnp.sum(values * values, axis=1, keepdims=True) * rows_weight
    return jnp.sum(per_row, axis=0, keepdims=True)


def column(row):
    return jnp.broadcast_to(row.astype(WIDE), (8, row.shape[1])).T[:, 0:1]


VECTORS = ("b_query", "b_value", "b_out", "gain_one", "shift_one", "b_down", "gain_two", "shift_two")


def vector(ref, name):
    place = VECTORS.index(name)
    return ref[place : place + 1, :]


def attend_kernel(
    place_ref, seg_ref, mark_ref, vectors_ref, wq_ref, wk_ref, wv_ref, wo_ref, inputs_ref, *refs,
    pieces,
):
    (
        q_ref, k_ref, v_ref, x_ref, ctx_ref, lse_ref, mid_ref, norm_ref, rstd_ref, stat_ref,
        wq_s, wk_s, wv_s, wo_s, q_s, k_s, v_s, x_s, bias_s, score_s, chance_s, weight_s, in_sems,
        out_sems,
    ) = refs[pieces - 1 :]
    length, model = x_s.shape
    piece = length // pieces
    loads = [
        pltpu.make_async_copy(a, b, in_sems.at[n])
        for n, (a, b) in enumerate(
            ((wk_ref, wk_s), (wq_ref, wq_s), (wv_ref, wv_s), (wo_ref, wo_s))
        )
    ]
    tokens_in = [
        pltpu.make_async_copy(a, x_s.at[pl.ds(n * piece, piece), :], in_sems.at[4 + n])
        for n, a in enumerate((inputs_ref.at[place_ref[0] + place_ref[1]],) + refs[: pieces - 1])
    ]
    for load in tokens_in + loads:
        load.start()
    stores = [
        pltpu.make_async_copy(a, b, out_sems.at[n])
        for n, (a, b) in enumerate(((k_s, k_ref), (q_s, q_ref), (v_s, v_ref), (x_s, x_ref)))
    ]
    own = pl.ds(place_ref[1], 1)
    mark_col = column(mark_ref[own, :])
    weight_s[...] = (mark_col >= 0).astype(WIDE)
    fill_bias(bias_s, seg_ref[own, :].astype(WIDE), mark_col)
    heads = model // HEAD_DIM
    width = 2 * HEAD_DIM
    for load in tokens_in:
        load.wait()
    stores[3].start()
    loads[0].wait()
    k_s[...] = nn(x_s[...], wk_s[...]).astype(LOW)
    stores[0].start()
    loads[1].wait()
    q_s[...] = ((nn(x_s[...], wq_s[...]) + vector(vectors_ref, "b_query")) * SCORE_SCALE).astype(LOW)
    stores[1].start()
    loads[2].wait()
    v_s[...] = (nn(x_s[...], wv_s[...]) + vector(vectors_ref, "b_value")).astype(LOW)
    stores[2].start()

    def lanes(head):
        return pl.ds(head // 2 * width, width)

    def scores(head):
        keys = k_s[:, lanes(head)] * lane_half(head % 2)
        score_s[head % 2] = nt(keys, q_s[:, lanes(head)])

    def soften(head):
        here, chance = score_s.at[head % 2], chance_s.at[head % 2]
        top = jnp.full((8, length), NEGATIVE, WIDE)
        for row in range(0, length, ROWS):
            block = here[row : row + ROWS, :] + bias_s[row : row + ROWS, :]
            here[row : row + ROWS, :] = block
            top = jnp.maximum(top, jnp.max(block.reshape(-1, 8, length), axis=0))
        top = jnp.max(top, axis=0, keepdims=True)
        amount = jnp.zeros((8, length), WIDE)
        for row in range(0, length, ROWS):
            block = jnp.exp(here[row : row + ROWS, :] - top)
            chance[row : row + ROWS, :] = block.astype(LOW)
            amount = amount + jnp.sum(block.reshape(-1, 8, length), axis=0)
        amount = jnp.sum(amount, axis=0, keepdims=True)
        lse_ref[head : head + 1, :] = top + jnp.log(amount)
        return 1.0 / amount

    def combine(head, share, turned):
        part = turned[head % 2 * HEAD_DIM : (head % 2 + 1) * HEAD_DIM]
        summed = nn(part, chance_s[head % 2]) * share
        ctx_ref[head * HEAD_DIM : (head + 1) * HEAD_DIM, :] = summed.astype(LOW)

    scores(0)
    waiting = None
    for head in range(heads):
        share = soften(head)
        if head % 2 == 0:
            turned = v_s[:, lanes(head)].T
        if head + 1 < heads:
            scores(head + 1)
        if waiting is not None:
            combine(*waiting)
        waiting = (head, share, turned)
    combine(*waiting)
    loads[3].wait()
    attention_all = tn(ctx_ref[...], wo_s[...])
    bias, gain, shift = (vector(vectors_ref, n) for n in ("b_out", "gain_one", "shift_one"))
    stats = [jnp.zeros((1, 1), WIDE) for _ in range(2)]
    for row in range(0, length, ROWS_NORM):
        at = pl.ds(row, ROWS_NORM)
        attention = attention_all[row : row + ROWS_NORM] + bias
        rows = x_s[at, :].astype(WIDE)
        total_in = rows + attention
        center = total_in - jnp.mean(total_in, axis=1, keepdims=True)
        rstd = lax.rsqrt(jnp.mean(center * center, axis=1, keepdims=True) + EPSILON)
        normal = center * rstd
        mid_ref[at, :] = normal * gain + shift
        norm_ref[at, :] = normal.astype(LOW)
        rstd_ref[at, :] = rstd
        row_weight = weight_s[at, :]
        stats[0] = stats[0] + total(row_weight, rows)
        stats[1] = stats[1] + total(row_weight, attention)
    stat_ref[...] = jnp.concatenate(
        [jnp.broadcast_to(stat, (1, 128)) for stat in stats] + [jnp.zeros((6, 128), WIDE)], axis=0
    )
    for store in stores:
        store.wait()


def cost():
    return pl.CostEstimate(flops=10**8, transcendentals=0, bytes_accessed=0)


def ignoring(kernel, inputs, extra):
    def wrapped(*refs):
        return kernel(*refs[:inputs], *refs[inputs + extra :])

    return wrapped


def whole(shape):
    return pl.BlockSpec(shape, lambda *_: (0,) * len(shape), pipeline_mode=pl.Buffered(1))


def attend(place, inputs, got, segs, marks, vectors, wq, wk, wv, wo, *earlier):
    pieces = len(got) + 1
    length, width = inputs.shape[1] * pieces, inputs.shape[2]
    heads = width // HEAD_DIM
    lse_rows = heads + (-heads) % 8
    tokens_out = jax.ShapeDtypeStruct((length, width), LOW)
    shapes = (
        tokens_out, tokens_out, tokens_out, tokens_out,
        jax.ShapeDtypeStruct((width, length), LOW),
        jax.ShapeDtypeStruct((lse_rows, length), WIDE),
        jax.ShapeDtypeStruct((length, width), WIDE),
        tokens_out,
        jax.ShapeDtypeStruct((length, 1), WIDE),
        jax.ShapeDtypeStruct((8, 128), WIDE),
    )
    args = (place, segs, marks, vectors, wq, wk, wv, wo, inputs, *got)
    weight = pltpu.VMEM((width, width), LOW)
    tokens = pltpu.VMEM((length, width), LOW)
    return pl.pallas_call(
        ignoring(
            functools.partial(attend_kernel, pieces=pieces), len(args), len(earlier)
        ),
        out_shape=shapes,
        in_specs=[IN_SMEM] + [IN_VMEM] * 3 + [ANY] * (4 + pieces + len(earlier)),
        out_specs=(ANY,) * 4 + (IN_VMEM,) * 6,
        scratch_shapes=[weight] * 4 + [tokens] * 4 + [
            pltpu.VMEM((length, length), WIDE),
            pltpu.VMEM((2, length, length), WIDE),
            pltpu.VMEM((2, length, length), LOW),
            pltpu.VMEM((length, 1), WIDE),
            pltpu.SemaphoreType.DMA((4 + pieces,)),
            pltpu.SemaphoreType.DMA((4,)),
        ],
        compiler_params=pltpu.CompilerParams(vmem_limit_bytes=VMEM_LIMIT),
        cost_estimate=cost(),
        name="attend",
    )(*args, *earlier)


def norm_back(grad, normal, rstd, gain):
    pulled = grad * gain
    return rstd * (
        pulled
        - jnp.mean(pulled, axis=1, keepdims=True)
        - normal * jnp.mean(pulled * normal, axis=1, keepdims=True)
    )


def row_total(values):
    return jnp.sum(values, axis=0, keepdims=True)


def feed_kernel(
    place_ref, mid0_ref, mid1_ref, cot_ref, mark_ref, bu_ref, vectors_ref, wu_ref, wd_ref, *refs,
    pieces,
):
    (
    slope_ref, low_ref, own_ref, sent_ref, grad_ref, grad_low_ref, down_ref, sums_ref, stat_ref,
    mid_s, cot_s, wu_s, wd_s, act_s, slope_s, low_s, result_s, grad_s, grad_low_s, out_s,
    feed_s, weight_s, in_sems, up_sems, down_sems, tile_sems, out_sems,
    ) = refs[pieces - 1 :]
    length, width = mid0_ref.shape
    rows = cot_s.shape[0]
    piece = length // pieces
    hidden = wu_ref.shape[1]
    half = hidden // 2
    chunks = hidden // HIDDEN_STEP
    tile = TILE
    def own(chunk):
        return pl.ds(chunk * HIDDEN_STEP, HIDDEN_STEP)

    first_in = pltpu.make_async_copy(mid0_ref, mid_s.at[pl.ds(0, length)], in_sems.at[0])
    second_in = pltpu.make_async_copy(mid1_ref, mid_s.at[pl.ds(length, length)], in_sems.at[1])
    cot_in = []
    for slot in range(rows // length):
        own_piece = cot_ref.at[place_ref[0] + slot]
        for part, ref in enumerate([own_piece] + [ref.at[slot] for ref in refs[: pieces - 1]]):
            spot = pl.ds(slot * length + part * piece, piece)
            sem = in_sems.at[2 + len(cot_in)]
            cot_in.append(pltpu.make_async_copy(ref, cot_s.at[spot, :], sem))
    ups = [
        pltpu.make_async_copy(wu_ref.at[:, own(c)], wu_s.at[:, own(c)], up_sems.at[c])
        for c in range(chunks)
    ]
    downs = [
        pltpu.make_async_copy(wd_ref.at[own(c), :], wd_s.at[own(c), :], down_sems.at[c])
        for c in range(chunks)
    ]
    first_in.start()
    for chunk in range(chunks):
        ups[chunk].start()
        downs[chunk].start()
    second_in.start()
    for copy in cot_in:
        copy.start()
    sums_ref[...] = jnp.zeros_like(sums_ref)
    stat_ref[...] = jnp.zeros_like(stat_ref)
    for slot in range(mark_ref.shape[0]):
        mark_col = column(mark_ref[slot : slot + 1, :])
        weight_s[pl.ds(slot * length, length), :] = (mark_col >= 0).astype(WIDE)

    def tile_copies(index):
        spot = pl.ds(pl.multiple_of(index * tile, tile), tile)
        pairs = (
            (low_s, low_ref), (grad_s, grad_ref), (grad_low_s, grad_low_ref), (slope_s, slope_ref),
        )
        return [
            pltpu.make_async_copy(a.at[spot, :], b.at[spot, :], tile_sems.at[n, index])
            for n, (a, b) in enumerate(pairs)
        ]

    def inside(index, row, count=ROWS):
        return pl.ds(pl.multiple_of(index * tile + row, count), count)

    def work(index, opening):
        spot = pl.ds(pl.multiple_of(index * tile, tile), tile)
        for row in range(0, tile, ROWS):
            low_s[inside(index, row), :] = mid_s[inside(index, row), :].astype(LOW)
        middle_low = low_s[spot, :]

        def up(chunk):
            if opening:
                ups[chunk].wait()
            return nn(middle_low, wu_s[:, own(chunk)])

        def down(chunk, feed):
            if opening:
                downs[chunk].wait()
            more = nn(act_s[spot, own(chunk)], wd_s[own(chunk), :])
            return more if feed is None else feed + more

        feed = None
        ahead = up(0)
        for chunk in range(chunks):
            bias = bu_ref[:, own(chunk)]
            for row in range(0, tile, ROWS):
                active, slope = gelu_pair(ahead[row : row + ROWS] + bias)
                act_s[inside(index, row), own(chunk)] = active.astype(LOW)
                slope_s[inside(index, row), own(chunk)] = slope.astype(LOW)
            if chunk + 1 < chunks:
                ahead = up(chunk + 1)
            if chunk > 0:
                feed = down(chunk - 1, feed)
        feed_s[...] = down(chunks - 1, feed)

    def norm(index):
        gain, shift, bias = (vector(vectors_ref, n) for n in ("gain_two", "shift_two", "b_down"))
        sums = [jnp.zeros((1, width), WIDE) for _ in range(3)]
        stats = [jnp.zeros((1, 1), WIDE) for _ in range(2)]
        for row in range(0, tile, ROWS_NORM):
            here = inside(index, row, ROWS_NORM)
            feed_here = feed_s[row : row + ROWS_NORM, :] + bias
            total_in = mid_s[here, :] + feed_here
            center = total_in - jnp.mean(total_in, axis=1, keepdims=True)
            rstd = lax.rsqrt(jnp.mean(center * center, axis=1, keepdims=True) + EPSILON)
            normal = center * rstd
            result = normal * gain + shift
            result_s[here, :] = result.astype(LOW)
            weight = weight_s[here, :]
            grad_result = cot_s[here, :].astype(WIDE) * weight
            grad = norm_back(grad_result, normal, rstd, gain)
            grad_s[here, :] = grad
            grad_low = grad.astype(LOW)
            grad_low_s[here, :] = grad_low
            sums[0] = sums[0] + row_total(grad_result * normal)
            sums[1] = sums[1] + row_total(grad_result)
            sums[2] = sums[2] + row_total(grad_low.astype(WIDE))
            stats[0] = stats[0] + total(weight, feed_here)
            stats[1] = stats[1] + total(weight, result)
        for copy in tile_copies(index):
            copy.start()
        for n in range(3):
            sums_ref[n : n + 1, :] += sums[n]
        for n in range(2):
            stat_ref[n : n + 1, :] += jnp.broadcast_to(stats[n], (1, 128))

    first_in.wait()
    work(0, True)
    second_in.wait()
    for copy in cot_in:
        copy.wait()

    def turn(index, carried):
        norm(index - 1)
        work(index, False)
        return carried

    lax.fori_loop(1, rows // tile, turn, 0)
    norm(rows // tile - 1)
    results = []
    for slot in range(rows // length):
        for part in range(pieces):
            spot = pl.ds(slot * length + part * piece, piece)
            target = sent_ref.at[part - 1, slot] if part else own_ref.at[slot]
            sem = in_sems.at[2 + len(results)]
            results.append(pltpu.make_async_copy(result_s.at[spot, :], target, sem))
            results[-1].start()
    outer(act_s, grad_low_s, out_s, (down_ref,), out_sems)
    for copy in results:
        copy.wait()
    for index in range(rows // tile):
        for copy in tile_copies(index):
            copy.wait()


def outer(left_s, right_s, out_s, targets, sems, loads=()):
    places = [
        ref.at[pl.ds(row, HIDDEN_STEP), :]
        for ref in targets
        for row in range(0, ref.shape[0], HIDDEN_STEP)
    ]
    copies = []
    for step, target in enumerate(places):
        spot = pl.ds(step * HIDDEN_STEP, HIDDEN_STEP)
        if loads:
            loads[step].wait()
        out_s[spot, :] = tn(left_s[:, spot], right_s[...]).astype(LOW)
        copies.append(pltpu.make_async_copy(out_s.at[spot, :], target, sems.at[step]))
        copies[-1].start()
    for copy in copies:
        copy.wait()


def feed_forward(place, mids, cot, got, marks, wu, bu, wd, vectors, *earlier):
    length, width = mids[0].shape
    rows = length * len(mids)
    pieces = len(got) + 1
    hidden = wu.shape[1]
    chunks = hidden // HIDDEN_STEP
    shapes = (
        jax.ShapeDtypeStruct((rows, hidden), LOW),
        jax.ShapeDtypeStruct((rows, width), LOW),
        jax.ShapeDtypeStruct((len(mids), length // pieces, width), LOW),
        jax.ShapeDtypeStruct((pieces - 1, len(mids), length // pieces, width), LOW),
        jax.ShapeDtypeStruct((rows, width), WIDE),
        jax.ShapeDtypeStruct((rows, width), LOW),
        jax.ShapeDtypeStruct((hidden, width), LOW),
        jax.ShapeDtypeStruct((8, width), WIDE),
        jax.ShapeDtypeStruct((8, 128), WIDE),
    )
    return pl.pallas_call(
        ignoring(functools.partial(feed_kernel, pieces=pieces), 8 + pieces, len(earlier)),
        out_shape=shapes,
        in_specs=[IN_SMEM] + [ANY] * 3 + [IN_VMEM] * 3 + [ANY] * (1 + pieces + len(earlier)),
        out_specs=(ANY,) * 7 + (IN_VMEM,) * 2,
        scratch_shapes=[
            pltpu.VMEM((rows, width), WIDE),
            pltpu.VMEM((rows, width), LOW),
            pltpu.VMEM((width, hidden), LOW),
            pltpu.VMEM((hidden, width), LOW),
            pltpu.VMEM((rows, hidden), LOW),
            pltpu.VMEM((rows, hidden), LOW),
            pltpu.VMEM((rows, width), LOW),
            pltpu.VMEM((rows, width), LOW),
            pltpu.VMEM((rows, width), WIDE),
            pltpu.VMEM((rows, width), LOW),
            pltpu.VMEM((hidden, width), LOW),
            pltpu.VMEM((TILE, width), WIDE),
            pltpu.VMEM((rows, 1), WIDE),
            pltpu.SemaphoreType.DMA((2 + pieces * len(mids),)),
            pltpu.SemaphoreType.DMA((chunks,)),
            pltpu.SemaphoreType.DMA((chunks,)),
            pltpu.SemaphoreType.DMA((4, rows // TILE)),
            pltpu.SemaphoreType.DMA((chunks,)),
        ],
        compiler_params=pltpu.CompilerParams(vmem_limit_bytes=VMEM_LIMIT),
        cost_estimate=cost(),
        name="feed_forward",
    )(place, mids[0], mids[1], cot, marks, bu, vectors, wu, wd, *got, *earlier)


def feed_back_kernel(
    place_ref, grad_low_ref, grad_ref, slope_ref, norm0_ref, norm1_ref, wu_ref, wd_ref,
    wo_ref, rstd0_ref, rstd1_ref, vectors_ref,
    grad_one_ref, attn_ref, ctx_ref, hid_ref, up_sums_ref, sums_ref,
    grad_low_s, grad_s, slope_s, norm_s, wu_s, wd_s, wo_s, rstd_s, grad_one_s, attn_s,
    ctx_s, middle_s,
    in_sems, slope_sems, up_sems, down_sems, tile_sems, ctx_sems,
):
    length = norm0_ref.shape[0]
    rows, width = grad_low_ref.shape
    hidden = wu_ref.shape[1]
    half = hidden // 2
    chunks = hidden // HIDDEN_STEP
    tile = TILE
    marks = [[1 - place_ref[n], place_ref[n]] for n in range(2)]
    each = hidden // 4

    def place_of(chunk):
        quarter, inside = divmod(chunk * HIDDEN_STEP, each)
        start = marks[0][quarter // 2] * half + marks[1][quarter % 2] * each + inside
        return pl.ds(pl.multiple_of(start, HIDDEN_STEP), HIDDEN_STEP)

    def own(chunk):
        return pl.ds(chunk * HIDDEN_STEP, HIDDEN_STEP)

    def spot_of(index):
        return pl.ds(pl.multiple_of(index * tile, tile), tile)

    slopes = [
        pltpu.make_async_copy(
            slope_ref.at[spot_of(i), place_of(c)],
            slope_s.at[spot_of(i), own(c)],
            slope_sems.at[chunks * i + c],
        )
        for i in range(rows // tile)
        for c in range(chunks)
    ]
    ups = [
        pltpu.make_async_copy(wu_ref.at[:, place_of(c)], wu_s.at[:, own(c)], up_sems.at[c])
        for c in range(chunks)
    ]
    downs = [
        pltpu.make_async_copy(wd_ref.at[place_of(c), :], wd_s.at[own(c), :], down_sems.at[c])
        for c in range(chunks)
    ]
    others = [
        pltpu.make_async_copy(a, b, in_sems.at[n])
        for n, (a, b) in enumerate(
            (
                (grad_low_ref, grad_low_s),
                (grad_ref, grad_s),
                (norm0_ref, norm_s.at[pl.ds(0, length)]),
                (norm1_ref, norm_s.at[pl.ds(length, length)]),
                (wo_ref, wo_s),
            )
        )
    ]
    others[0].start()
    downs[0].start()
    slopes[0].start()
    ups[0].start()
    for chunk in range(1, chunks):
        downs[chunk].start()
        slopes[chunk].start()
        ups[chunk].start()
    for copy in others[1:5] + slopes[chunks:]:
        copy.start()
    rstd_s[pl.ds(0, length), :] = rstd0_ref[...]
    rstd_s[pl.ds(length, length), :] = rstd1_ref[...]
    sums_ref[...] = jnp.zeros_like(sums_ref)
    up_sums_ref[...] = jnp.zeros_like(up_sums_ref)

    def tile_copies(index):
        spot = spot_of(index)
        pairs = ((grad_one_s, grad_one_ref), (attn_s, attn_ref), (slope_s, hid_ref))
        return [
            pltpu.make_async_copy(a.at[spot, :], b.at[spot, :], tile_sems.at[n, index])
            for n, (a, b) in enumerate(pairs)
        ]

    def inside(index, row, count=ROWS):
        return pl.ds(pl.multiple_of(index * tile + row, count), count)

    def work(index, opening):
        spot = spot_of(index)
        grad_low = grad_low_s[spot, :]

        def back(chunk):
            if opening:
                downs[chunk].wait()
            return nt(grad_low, wd_s[own(chunk), :])

        def forth(chunk, grad):
            if opening:
                ups[chunk].wait()
            more = nt(slope_s[spot, own(chunk)], wu_s[:, own(chunk)])
            return more if grad is None else grad + more

        ahead = back(0)
        grad_middle = None
        for chunk in range(chunks):
            if opening:
                slopes[chunk].wait()
            sums = jnp.zeros((8, HIDDEN_STEP), WIDE)
            for row in range(0, tile, ROWS):
                at = inside(index, row)
                slope = slope_s[at, own(chunk)].astype(WIDE)
                grad_hidden = (ahead[row : row + ROWS] * slope).astype(LOW)
                slope_s[at, own(chunk)] = grad_hidden
                sums = sums + jnp.sum(
                    grad_hidden.astype(WIDE).reshape(-1, 8, HIDDEN_STEP), axis=0
                )
            up_sums_ref[:, place_of(chunk)] += sums
            if chunk + 1 < chunks:
                ahead = back(chunk + 1)
            if chunk > 0:
                grad_middle = forth(chunk - 1, grad_middle)
        middle_s[...] = forth(chunks - 1, grad_middle)

    def norm(index):
        gain = vector(vectors_ref, "gain_one")
        sums = [jnp.zeros((1, width), WIDE) for _ in range(3)]
        for row in range(0, tile, ROWS_NORM):
            at = inside(index, row, ROWS_NORM)
            grad = middle_s[row : row + ROWS_NORM, :] + grad_s[at, :]
            normal = norm_s[at, :].astype(WIDE)
            grad_one = norm_back(grad, normal, rstd_s[at, :], gain)
            grad_one_s[at, :] = grad_one
            attn = grad_one.astype(LOW)
            attn_s[at, :] = attn
            sums[0] = sums[0] + row_total(grad * normal)
            sums[1] = sums[1] + row_total(grad)
            sums[2] = sums[2] + row_total(attn.astype(WIDE))
        for copy in tile_copies(index):
            copy.start()
        for n in range(3):
            sums_ref[n : n + 1, :] += sums[n]

    def project(index):
        spot = spot_of(index)
        turned = nt(wo_s[...], attn_s[spot, :]).astype(LOW)
        slot, inner = divmod(index * tile, length)
        ctx_s[slot, :, inner : inner + tile] = turned
        copy = pltpu.make_async_copy(
            ctx_s.at[slot, :, pl.ds(inner, tile)], ctx_ref.at[slot, :, pl.ds(inner, tile)],
            ctx_sems.at[index],
        )
        copy.start()
        return copy

    others[0].wait()
    work(0, True)
    for copy in slopes[chunks:] + others[1:5]:
        copy.wait()

    def turn(index, carried):
        norm(index - 1)
        work(index, False)
        return carried

    lax.fori_loop(1, rows // tile, turn, 0)
    norm(rows // tile - 1)
    copies = [project(index) for index in range(rows // tile)]
    for copy in copies:
        copy.wait()
    for index in range(rows // tile):
        for copy in tile_copies(index):
            copy.wait()


def feed_back(place, grad_low, grad, slope, norms, rstds, wu, wd, wo, vectors, *earlier):
    rows, width = grad.shape
    length = norms[0].shape[0]
    hidden = wu.shape[1]
    chunks = hidden // HIDDEN_STEP
    shapes = (
        jax.ShapeDtypeStruct((rows, width), WIDE),
        jax.ShapeDtypeStruct((rows, width), LOW),
        jax.ShapeDtypeStruct((rows // length, width, length), LOW),
        jax.ShapeDtypeStruct((rows, hidden), LOW),
        jax.ShapeDtypeStruct((8, hidden), WIDE),
        jax.ShapeDtypeStruct((8, width), WIDE),
    )
    return pl.pallas_call(
        ignoring(feed_back_kernel, 12, len(earlier)),
        out_shape=shapes,
        in_specs=[IN_SMEM] + [ANY] * 8 + [IN_VMEM] * 3 + [ANY] * len(earlier),
        out_specs=(ANY,) * 4 + (IN_VMEM,) * 2,
        scratch_shapes=[
            pltpu.VMEM((rows, width), LOW),
            pltpu.VMEM((rows, width), WIDE),
            pltpu.VMEM((rows, hidden), LOW),
            pltpu.VMEM((rows, width), LOW),
            pltpu.VMEM((width, hidden), LOW),
            pltpu.VMEM((hidden, width), LOW),
            pltpu.VMEM((width, width), LOW),
            pltpu.VMEM((rows, 1), WIDE),
            pltpu.VMEM((rows, width), WIDE),
            pltpu.VMEM((rows, width), LOW),
            pltpu.VMEM((rows // length, width, length), LOW),
            pltpu.VMEM((TILE, width), WIDE),
            pltpu.SemaphoreType.DMA((5,)),
            pltpu.SemaphoreType.DMA((chunks * rows // TILE,)),
            pltpu.SemaphoreType.DMA((chunks,)),
            pltpu.SemaphoreType.DMA((chunks,)),
            pltpu.SemaphoreType.DMA((3, rows // TILE)),
            pltpu.SemaphoreType.DMA((rows // TILE,)),
        ],
        compiler_params=pltpu.CompilerParams(vmem_limit_bytes=VMEM_LIMIT),
        cost_estimate=cost(),
        name="feed_back",
    )(
        place, grad_low, grad, slope, norms[0], norms[1], wu, wd, wo, rstds[0], rstds[1],
        vectors, *earlier,
    )


def up_grads_kernel(
    hid_ref, low_ref, early_ref, late_ref, keep_ref, hid_s, low_s, out_s, in_sems, out_sems
):
    steps = hid_ref.shape[1] // HIDDEN_STEP
    low_in = pltpu.make_async_copy(low_ref, low_s, in_sems.at[steps])
    low_in.start()
    loads = []
    for step in range(steps):
        spot = pl.ds(step * HIDDEN_STEP, HIDDEN_STEP)
        copy = pltpu.make_async_copy(hid_ref.at[:, spot], hid_s.at[:, spot], in_sems.at[step])
        copy.start()
        loads.append(copy)
    low_in.wait()
    outer(hid_s, low_s, out_s, (early_ref, late_ref, keep_ref), out_sems, loads)


def up_grads(hid, mid_low, *earlier):
    rows, hidden = hid.shape
    width = mid_low.shape[1]
    quarter = jax.ShapeDtypeStruct((hidden // 4, width), LOW)
    chunks = hidden // HIDDEN_STEP
    return pl.pallas_call(
        ignoring(up_grads_kernel, 2, len(earlier)),
        out_shape=(quarter, quarter, jax.ShapeDtypeStruct((hidden // 2, width), LOW)),
        in_specs=[ANY] * (2 + len(earlier)),
        out_specs=(ANY,) * 3,
        scratch_shapes=[
            pltpu.VMEM((rows, hidden), LOW),
            pltpu.VMEM((rows, width), LOW),
            pltpu.VMEM((hidden, width), LOW),
            pltpu.SemaphoreType.DMA((chunks + 1,)),
            pltpu.SemaphoreType.DMA((chunks,)),
        ],
        compiler_params=pltpu.CompilerParams(vmem_limit_bytes=VMEM_LIMIT),
        cost_estimate=cost(),
        name="up_grads",
    )(hid, mid_low, *earlier)


def attend_back_kernel(
    place_ref, seg_ref, mark_ref, lse_ref, q_ref, k_ref, v_ref, ctx_ref, grad_ctx_ref, grad_one_ref, wq_ref,
    wk_ref, wv_ref,
    dq_ref, dk_ref, dv_ref, own_ref, sent_ref, sums_ref,
    q_s, k_s, v_s, ctx_s, grad_ctx_s, grad_one_s, wq_s, wk_s, wv_s, bias_s, score_s, pull_s,
    chance_s, grad_s, in_sems,
):
    length, model = q_ref.shape
    slot = place_ref[0]
    heads = model // HEAD_DIM
    width = 2 * HEAD_DIM
    loads = [
        pltpu.make_async_copy(a, b, in_sems.at[n])
        for n, (a, b) in enumerate(
            (
                (k_ref, k_s), (q_ref, q_s), (v_ref, v_s), (grad_ctx_ref.at[slot], grad_ctx_s),
                (ctx_ref, ctx_s), (wq_ref, wq_s), (wk_ref, wk_s), (wv_ref, wv_s),
                (grad_one_ref.at[pl.ds(pl.multiple_of(slot * length, length), length), :], grad_one_s),
            )
        )
    ]
    for load in loads:
        load.start()
    mark_col = column(mark_ref[pl.ds(slot, 1), :])
    fill_bias(bias_s, seg_ref[pl.ds(slot, 1), :].astype(WIDE), mark_col)

    def lanes(head):
        return pl.ds(head // 2 * width, width)

    def rows_of(head):
        return pl.ds(head * HEAD_DIM, HEAD_DIM)

    def products(head):
        score_s[head % 2] = nt(k_s[:, lanes(head)] * lane_half(head % 2), q_s[:, lanes(head)])
        values = v_s[:, lanes(head)] * lane_half(head % 2)
        pull_s[head % 2] = nn(values, grad_ctx_s[lanes(head), :])

    def soften(head):
        score, pull = score_s.at[head % 2], pull_s.at[head % 2]
        chance, grad = chance_s.at[head % 2], grad_s.at[head % 2]
        shared = grad_ctx_s[rows_of(head), :].astype(WIDE) * ctx_s[rows_of(head), :].astype(WIDE)
        delta = jnp.sum(shared, axis=0, keepdims=True)
        lse = lse_ref[head : head + 1, :]
        for row in range(0, length, ROWS):
            at = slice(row, row + ROWS)
            block = jnp.exp(score[at, :] + bias_s[at, :] - lse)
            chance[at, :] = block.astype(LOW)
            grad[at, :] = (block * (pull[at, :] - delta)).astype(LOW)

    def combine(head, turned):
        part_v = nt(chance_s[head % 2], grad_ctx_s[lanes(head), :])
        part_k = nn(grad_s[head % 2], q_s[:, lanes(head)])
        part = turned[head % 2 * HEAD_DIM : (head % 2 + 1) * HEAD_DIM]
        return part_v, part_k, nn(part, grad_s[head % 2])

    def keep(head, one, two):
        first = lax.broadcasted_iota(jnp.int32, one[0].shape, 1) < HEAD_DIM
        dv_ref[:, lanes(head)] = jnp.where(first, one[0], two[0]).astype(LOW)
        dk_ref[:, lanes(head)] = jnp.where(first, one[1], two[1]).astype(LOW)
        dq_ref[:, lanes(head)] = jnp.concatenate([one[2], two[2]], axis=0).T.astype(LOW)

    for load in loads[:4]:
        load.wait()
    products(0)
    loads[4].wait()
    waiting = None
    found = []
    for head in range(heads):
        soften(head)
        if head % 2 == 0:
            turned = k_s[:, lanes(head)].T
        if len(found) == 2:
            keep(head - 2, *found)
            found = []
        if head + 1 < heads:
            products(head + 1)
        if waiting is not None:
            found.append(combine(*waiting))
        waiting = (head, turned)
    found.append(combine(*waiting))
    keep(heads - 1, *found)
    for load in loads[5:]:
        load.wait()
    piece = own_ref.shape[0]
    for rows, ref in ((pl.ds(0, piece), own_ref), (pl.ds(piece, length - piece), sent_ref)):
        grad = (
            grad_one_s[rows, :]
            + nt(dq_ref[rows, :], wq_s[...]) * SCORE_SCALE
            + nt(dk_ref[rows, :], wk_s[...])
            + nt(dv_ref[rows, :], wv_s[...])
        )
        ref[...] = grad.astype(ref.dtype)
    sums_ref[...] = jnp.concatenate(
        [
            row_total(dq_ref[...].astype(WIDE)) * SCORE_SCALE,
            row_total(dv_ref[...].astype(WIDE)),
            jnp.zeros((6, model), WIDE),
        ],
        axis=0,
    )


def attend_back(piece, place, q, k, v, ctx, grad_ctx, lse, segs, marks, grad_one, wq, wk, wv, *earlier):
    length, width = q.shape
    heads = width // HEAD_DIM
    shapes = (
        jax.ShapeDtypeStruct((length, width), LOW),
        jax.ShapeDtypeStruct((length, width), LOW),
        jax.ShapeDtypeStruct((length, width), LOW),
        jax.ShapeDtypeStruct((piece, width), WIDE),
        jax.ShapeDtypeStruct((length - piece, width), LOW),
        jax.ShapeDtypeStruct((8, width), WIDE),
    )
    tokens = pltpu.VMEM((length, width), LOW)
    turned = pltpu.VMEM((width, length), LOW)
    weight = pltpu.VMEM((width, width), LOW)
    return pl.pallas_call(
        ignoring(attend_back_kernel, 13, len(earlier)),
        out_shape=shapes,
        in_specs=[IN_SMEM] + [IN_VMEM] * 3 + [ANY] * (9 + len(earlier)),
        out_specs=(IN_VMEM,) * 6,
        scratch_shapes=[
            tokens, tokens, tokens, turned, turned, pltpu.VMEM((length, width), WIDE),
            weight, weight, weight,
            pltpu.VMEM((length, length), WIDE),
            pltpu.VMEM((2, length, length), WIDE),
            pltpu.VMEM((2, length, length), WIDE),
            pltpu.VMEM((2, length, length), LOW),
            pltpu.VMEM((2, length, length), LOW),
            pltpu.SemaphoreType.DMA((9,)),
        ],
        compiler_params=pltpu.CompilerParams(vmem_limit_bytes=VMEM_LIMIT),
        cost_estimate=cost(),
        name="attend_back",
    )(place, segs, marks, lse, q, k, v, ctx, grad_ctx, grad_one, wq, wk, wv, *earlier)


def square_kernel(
    place_ref, x0_ref, x1_ref, dq0_ref, dq1_ref, dk0_ref, dk1_ref, dv0_ref, dv1_ref, ctx0_ref,
    ctx1_ref, attn_ref, send0_ref, send1_ref, keep0_ref, keep1_ref, x_s, dq_s, dk_s, dv_s, ctx_s, attn_s, out_s, in_sems,
    out_sems,
):
    length, width = x0_ref.shape
    first, second = pl.ds(0, length), pl.ds(length, length)
    loads = []
    for a, b in (
        (x0_ref, x_s.at[first]), (x1_ref, x_s.at[second]), (dv0_ref, dv_s.at[first]),
        (dv1_ref, dv_s.at[second]), (dq0_ref, dq_s.at[first]), (dq1_ref, dq_s.at[second]),
        (ctx0_ref, ctx_s.at[:, first]), (ctx1_ref, ctx_s.at[:, second]), (attn_ref, attn_s),
        (dk0_ref, dk_s.at[first]), (dk1_ref, dk_s.at[second]),
    ):
        loads.append(pltpu.make_async_copy(a, b, in_sems.at[len(loads)]))
        loads[-1].start()
    mine = place_ref[0] == 0
    x = x_s[...]
    step = 256
    copies = []

    def place(part, columns, low, high):
        for n, kept in enumerate((False, True)):
            spot = pl.ds((n * 2 + part) * width, width)
            out_s[spot, columns] = jnp.where(mine == kept, low, high).astype(LOW)

    def flush(part):
        for n, ref in enumerate(((send0_ref, send1_ref)[part], (keep0_ref, keep1_ref)[part])):
            spot = pl.ds((n * 2 + part) * width, width)
            copies.append(
                pltpu.make_async_copy(out_s.at[spot, :], ref, out_sems.at[len(copies)])
            )
            copies[-1].start()

    for load in loads[:6]:
        load.wait()
    x = x_s[...]
    for start in range(0, width, step):
        columns = pl.ds(start, step)
        place(0, columns, tn(x, dq_s[:, columns]) * SCORE_SCALE, tn(x, dv_s[:, columns]))
    flush(0)
    for load in loads[6:]:
        load.wait()
    for start in range(0, width, step):
        columns = pl.ds(start, step)
        place(1, columns, tn(x, dk_s[:, columns]), nn(ctx_s[...], attn_s[:, columns]))
    flush(1)
    for copy in copies:
        copy.wait()


def square_grads(place, xs, dqs, dks, dvs, ctxs, attn, *earlier):
    length, width = xs[0].shape
    rows = length * len(xs)
    tokens = pltpu.VMEM((rows, width), LOW)
    out = jax.ShapeDtypeStruct((width, width), LOW)
    return pl.pallas_call(
        ignoring(square_kernel, 12, len(earlier)),
        out_shape=(out,) * 4,
        in_specs=[IN_SMEM] + [ANY] * (11 + len(earlier)),
        out_specs=(ANY,) * 4,
        scratch_shapes=[
            tokens, tokens, tokens, tokens, pltpu.VMEM((width, rows), LOW), tokens,
            pltpu.VMEM((4 * width, width), LOW),
            pltpu.SemaphoreType.DMA((11,)),
            pltpu.SemaphoreType.DMA((4,)),
        ],
        compiler_params=pltpu.CompilerParams(vmem_limit_bytes=VMEM_LIMIT),
        cost_estimate=cost(),
        name="square_grads",
    )(place, *xs, *dqs, *dks, *dvs, *ctxs, attn, *earlier)


def pick_kernel(place_ref, value_ref, out_ref):
    out_ref[...] = value_ref[0]


def pick(value, place, *earlier):
    shape = value.shape[1:]
    if len(shape) == 1:
        return lax.dynamic_index_in_dim(value, place, 0, keepdims=False)
    return pl.pallas_call(
        ignoring(pick_kernel, 2, len(earlier)),
        out_shape=jax.ShapeDtypeStruct(shape, value.dtype),
        grid_spec=pltpu.PrefetchScalarGridSpec(
            num_scalar_prefetch=1,
            grid=(1,),
            in_specs=[pl.BlockSpec((1,) + shape, lambda i, p: (p[0], 0, 0))] + [ANY] * len(earlier),
            out_specs=pl.BlockSpec(shape, lambda i, p: (0, 0)),
        ),
        cost_estimate=cost(),
        name="pick",
    )(place.astype(jnp.int32).reshape(1), value, *earlier)


def other_pieces(value, slot, slots, *earlier):
    count = lax.axis_size("seq")
    me = lax.axis_index("seq")
    found = []
    for shift in range(1, count):
        block = pick(value, (me + shift) % count * slots + slot, *earlier)
        pairs = [(source, (source + shift) % count) for source in range(count)]
        found.append(lax.ppermute(block, "seq", pairs))
    return found


def send_back(parts, shifts=None):
    count = lax.axis_size("seq")
    found = []
    for shift in range(1, count):
        pairs = [(source, (source + shift) % count) for source in range(count)]
        found.append(lax.ppermute(parts[shift - 1], "seq", pairs))
    return found


def join_kernel(me_ref, *refs, slots, count):
    out_ref = refs[-1]
    index = pl.program_id(0)
    shift = lax.rem(index // slots - me_ref[0] + count, count)
    for n in range(count):
        for slot in range(slots):

            @pl.when((shift == n) & (lax.rem(index, slots) == slot))
            def _(n=n, slot=slot):
                value = refs[n][slot] if len(refs) == count + 1 else refs[n * slots + slot][...]
                out_ref[0] = value.astype(out_ref.dtype)


def join(me, arrays, slots, count, *earlier):
    piece, width = arrays[0].shape[-2:]
    return pl.pallas_call(
        ignoring(
            functools.partial(join_kernel, slots=slots, count=count), 1 + len(arrays), len(earlier)
        ),
        out_shape=jax.ShapeDtypeStruct((slots * count, piece, width), arrays[0].dtype),
        grid_spec=pltpu.PrefetchScalarGridSpec(
            num_scalar_prefetch=1,
            grid=(slots * count,),
            in_specs=[whole(array.shape) for array in arrays] + [ANY] * len(earlier),
            out_specs=pl.BlockSpec((1, piece, width), lambda i, p: (i, 0, 0)),
        ),
        compiler_params=pltpu.CompilerParams(vmem_limit_bytes=SMALL_LIMIT),
        cost_estimate=cost(),
        name="join",
    )(me, *arrays, *earlier)


def collect_kernel(sums0_ref, sums1_ref, one_ref, two_ref, up_ref, *refs):
    stat_refs, mark_ref, out_ref = refs[:-2], refs[-2], refs[-1]
    width = out_ref.shape[1]
    out_ref[0:2, :] = sums0_ref[0:2, :] + sums1_ref[0:2, :]
    out_ref[2:5, :] = one_ref[0:3, :]
    out_ref[5:8, :] = two_ref[0:3, :]
    lane = lax.broadcasted_iota(jnp.int32, (1, width), 1)
    known = (mark_ref[...] >= 0).astype(WIDE)
    tokens = jnp.sum(jnp.sum(known, axis=1, keepdims=True), axis=0, keepdims=True)
    fed = stat_refs[2]
    stats = (
        stat_refs[0][0:1, 0:1] + stat_refs[1][0:1, 0:1],
        stat_refs[0][1:2, 0:1] + stat_refs[1][1:2, 0:1],
        fed[0:1, 0:1], fed[1:2, 0:1], tokens,
    )
    row = jnp.zeros((1, width), WIDE)
    for n, stat in enumerate(stats):
        row = jnp.where(lane == n, stat, row)
    out_ref[8:9, :] = row
    parts = up_ref.shape[1] // width
    for n in range(parts):
        out_ref[9 + n : 10 + n, :] = row_total(up_ref[:, n * width : (n + 1) * width])
    left = out_ref.shape[0] - 9 - parts
    out_ref[9 + parts :, :] = jnp.zeros((left, width), WIDE)


def collect(sums, sums_one, sums_two, up_sums, stats, marks, *earlier):
    width = sums_one.shape[1]
    rows = 9 + up_sums.shape[1] // width
    args = (*sums, sums_one, sums_two, up_sums, *stats, marks)
    return pl.pallas_call(
        ignoring(collect_kernel, len(args), len(earlier)),
        out_shape=jax.ShapeDtypeStruct((rows + (-rows) % 8, width), WIDE),
        in_specs=[IN_VMEM] * len(args) + [ANY] * len(earlier),
        out_specs=IN_VMEM,
        compiler_params=pltpu.CompilerParams(vmem_limit_bytes=VMEM_LIMIT),
        cost_estimate=cost(),
        name="collect",
    )(*args, *earlier)


def swap(value, axis, bit):
    count = lax.axis_size(axis)
    return lax.ppermute(value, axis, [(source, source ^ bit) for source in range(count)])


def bit_of(axis, bit):
    return (lax.axis_index(axis) // bit) % 2


CORE = ("dp", 1)
HALVINGS = 5
STEP_ROWS = 16


def chip_axes():
    dp, seq = lax.axis_size("dp"), lax.axis_size("seq")
    along_dp = [("dp", 2**i) for i in range(1, dp.bit_length() - 1)]
    along_seq = [("seq", 2**i) for i in range(seq.bit_length() - 1)]
    return along_dp[0], along_seq[0], along_dp[1], along_dp[2:] + along_seq[1:]


class Chain:
    def __init__(self, bits):
        self.last = ()
        self.bits = bits

    def run(self, function, *args):
        out = function(*args, *self.last)
        arrays = out if isinstance(out, (tuple, list)) else (out,)
        self.last = (min(arrays, key=lambda array: array.size),)
        return out

    def round(self, *tasks):
        outs = list(self.run(round_call, self.bits, [task[:-1] for task in tasks]))
        for task in tasks:
            count = 2 if task[0] == "halve" else 1
            task[-1](*[outs.pop(0) for _ in range(count)])


def add_rows(first, first_start, second, second_start, out, rows):
    def step(index, carried):
        spots = [
            pl.ds(pl.multiple_of(start + index * STEP_ROWS, STEP_ROWS), STEP_ROWS)
            for start in (first_start, second_start, 0)
        ]
        both = first[spots[0], :].astype(WIDE) + second[spots[1], :].astype(WIDE)
        out[spots[2], :] = both.astype(LOW)
        return carried

    lax.fori_loop(0, rows // STEP_ROWS, step, 0)


def round_kernel(bits_ref, *refs, plan, inputs):
    outs = list(refs[inputs:])
    for kind, places, meta in plan:
        first, second = refs[places[0]], refs[places[1]]
        if kind == "halve":
            rows, offset, which = meta
            mine = bits_ref[which]
            for bit in (1 - mine, mine):
                start = offset + bit * rows
                add_rows(first, start, second, start, outs.pop(0), rows)
        elif kind == "add":
            add_rows(first, meta, second, 0, outs.pop(0), second.shape[0])
        elif kind == "merge":
            rows = first.shape[0]
            out = outs.pop(0)
            out[:rows, :] = first[...]
            out[rows:, :] = second[...]
        else:
            outs.pop(0)[...] = first[...] + second[...]


def round_call(bits, tasks, *earlier):
    arrays, plan, shapes = [], [], []
    for kind, pair, meta in tasks:
        places = []
        for array in pair:
            known = [n for n, other in enumerate(arrays) if other is array]
            if not known:
                arrays.append(array)
            places.append(known[0] if known else len(arrays) - 1)
        plan.append((kind, places, meta))
        rows, width = pair[0].shape
        if kind == "halve":
            shapes += [jax.ShapeDtypeStruct((meta[0], width), LOW)] * 2
        elif kind == "merge":
            shapes.append(jax.ShapeDtypeStruct((2 * rows, width), LOW))
        elif kind == "add":
            shapes.append(jax.ShapeDtypeStruct(pair[1].shape, LOW))
        else:
            shapes.append(jax.ShapeDtypeStruct((rows, width), pair[0].dtype))
    return pl.pallas_call(
        ignoring(
            functools.partial(round_kernel, plan=plan, inputs=len(arrays)),
            1 + len(arrays),
            len(earlier),
        ),
        out_shape=tuple(shapes),
        in_specs=[IN_SMEM] + [IN_VMEM] * len(arrays) + [ANY] * len(earlier),
        out_specs=(IN_VMEM,) * len(shapes),
        compiler_params=pltpu.CompilerParams(vmem_limit_bytes=SMALL_LIMIT),
        cost_estimate=cost(),
        name="round",
    )(bits, *arrays, *earlier)


class Reduction:
    def __init__(self, kept, got, order, names, back):
        self.order, self.names, self.back = order, names, back
        self.first, self.second = kept, got
        self.count, self.offset = kept.shape[0], 0
        self.step = 1

    def send(self):
        axis = self.order[self.step]
        rows, offset = self.count // 2, self.offset

        def found(sent, kept):
            self.first, self.second = kept, swap(sent, *axis)
            self.count, self.offset = rows, 0
            self.step += 1

        meta = (rows, offset, self.names.index(axis))
        return "halve", (self.first, self.second), meta, found

    def send_early(self, early):
        axis = self.order[self.step]

        def found(sent):
            self.sent = swap(sent, *axis)

        return "add", (self.first, early), 0, found

    def send_late(self, late):
        def found(kept):
            self.first, self.second = kept, self.sent
            self.count, self.offset = late.shape[0], 0
            self.step += 1

        return "add", (self.first, late), late.shape[0], found

    def share(self):
        def found(share):
            self.have = share
            if self.step < len(self.order):
                self.first, self.second = share, swap(share, *self.order[self.step])
                self.step += 1
            else:
                self.step = len(self.back) - 1
                self.got = swap(share, *self.back[self.step])

        return "add", (self.first, self.second), 0, found

    def more_shares(self):
        return len(self.order) - HALVINGS

    def gather(self):
        def found(merged):
            self.step -= 1
            self.have, self.got = merged, swap(merged, *self.back[self.step])

        return "merge", (self.have, self.got), None, found

    def halves(self):
        return [self.have, self.got, swap(self.have, *CORE), swap(self.got, *CORE)]

    def moves(self):
        chips = [axis for axis in self.order[:HALVINGS] if axis != CORE]
        return [len(chips) - 1 - chips.index(axis) for axis in self.back]

    def place(self):
        place = 0
        for axis in self.back:
            place = place * 2 + bit_of(*axis)
        return place.astype(jnp.int32)


def attach_kernel(small_ref, part_ref, out_ref):
    rows = small_ref.shape[0]
    out_ref[:rows, :] = small_ref[...].astype(LOW)
    out_ref[rows:, :] = part_ref[...]


def attach(small, part, *earlier):
    rows = small.shape[0] + part.shape[0]
    return pl.pallas_call(
        ignoring(attach_kernel, 2, len(earlier)),
        out_shape=jax.ShapeDtypeStruct((rows, part.shape[1]), LOW),
        in_specs=[IN_VMEM] * 2 + [ANY] * len(earlier),
        out_specs=IN_VMEM,
        compiler_params=pltpu.CompilerParams(vmem_limit_bytes=SMALL_LIMIT),
        cost_estimate=cost(),
        name="attach",
    )(small, part, *earlier)


def detach_kernel(value_ref, small_ref, out_ref):
    count, rows, _ = value_ref.shape
    few = small_ref.shape[0]
    each = rows - few
    total_here = jnp.zeros(small_ref.shape, WIDE)
    for n in range(count):
        total_here = total_here + value_ref[n, :few, :].astype(WIDE)
        out_ref[n * each : (n + 1) * each, :] = value_ref[n, few:, :].astype(WIDE)

    @pl.when(pl.program_id(0) == 0)
    def _():
        small_ref[...] = jnp.zeros_like(small_ref)

    small_ref[...] += total_here


def detach(value, few, *earlier):
    count, rows, width = value.shape
    steps = 8
    return pl.pallas_call(
        ignoring(detach_kernel, 1, len(earlier)),
        out_shape=(
            jax.ShapeDtypeStruct((few, width), WIDE),
            jax.ShapeDtypeStruct((count * (rows - few), width), WIDE),
        ),
        grid=(steps,),
        in_specs=[pl.BlockSpec((count // steps, rows, width), lambda t: (t, 0, 0))]
        + [ANY] * len(earlier),
        out_specs=(
            whole((few, width)),
            pl.BlockSpec((count // steps * (rows - few), width), lambda t: (t, 0)),
        ),
        compiler_params=pltpu.CompilerParams(
            vmem_limit_bytes=SMALL_LIMIT, dimension_semantics=("arbitrary",)
        ),
        cost_estimate=cost(),
        name="detach",
    )(value, *earlier)


def spot_of_block(index, moves):
    spot = 0
    for move in moves:
        spot = spot * 2 + ((index >> move) & 1)
    return spot


def turn_kernel(place_ref, own, other, *refs, moves):
    out_ref = refs[-1]
    blocks = 1 << (HALVINGS - 2)
    block = own.shape[0] // blocks
    count = out_ref.shape[1] // block
    tile = place_ref[2] * 4 + pl.program_id(0)
    mine = place_ref[0] == ((tile >> 1) & 1)
    start = ((tile >> 2) << (HALVINGS - 2)) + (tile & 1) * count
    found = []
    for j in range(count):
        spot = spot_of_block(start + j, moves) ^ place_ref[1]
        at = pl.ds(pl.multiple_of(lax.rem(spot, blocks) * block, block), block)
        found.append(jnp.where(mine, own[at, :], other[at, :]).astype(WIDE))
    out_ref[...] = jnp.concatenate(found, axis=0).T


def turn(place, own, other, moves, into, *earlier):
    rows, width = own.shape
    into = () if into is None else (into,)
    return pl.pallas_call(
        ignoring(functools.partial(turn_kernel, moves=moves), 3 + len(into), len(earlier)),
        out_shape=jax.ShapeDtypeStruct((width, 4 * rows), WIDE),
        grid_spec=pltpu.PrefetchScalarGridSpec(
            num_scalar_prefetch=1,
            grid=(4,),
            in_specs=[whole(own.shape)] * 2 + [ANY] * (len(into) + len(earlier)),
            out_specs=pl.BlockSpec((width, rows // 2), lambda t, p: (0, p[2] * 4 + t)),
        ),
        input_output_aliases={3: 0} if into else {},
        compiler_params=pltpu.CompilerParams(vmem_limit_bytes=SMALL_LIMIT),
        cost_estimate=cost(),
        name="turn",
    )(place, own, other, *into, *earlier)


def gate_kernel(value_ref, out_ref):
    pass


def gate(value, *earlier):
    return pl.pallas_call(
        ignoring(gate_kernel, 1, len(earlier)),
        out_shape=jax.ShapeDtypeStruct(value.shape, value.dtype),
        in_specs=[pl.BlockSpec(memory_space=pl.ANY)] + [ANY] * len(earlier),
        out_specs=pl.BlockSpec(memory_space=pl.ANY),
        input_output_aliases={0: 0},
        compiler_params=pltpu.CompilerParams(vmem_limit_bytes=SMALL_LIMIT),
        cost_estimate=cost(),
        name="gate",
    )(value, *earlier)


def finish_kernel(
    place_ref, near_own, far_own, near_other, far_other, low_ref, high_ref, *, moves
):
    blocks = 1 << (HALVINGS - 2)
    block = near_own.shape[0] // blocks
    step = pl.program_id(0)
    half = step // 4
    rows = low_ref.shape[0]
    for out_ref, owner in ((low_ref, 0), (high_ref, 1)):

        @pl.when(half == owner)
        def _(out_ref=out_ref, owner=owner):
            for j in range(rows // block):
                index = lax.rem(step, 4) * (rows // block) + j
                spot = spot_of_block(index, moves) ^ place_ref[1]
                at = pl.ds(pl.multiple_of(lax.rem(spot, blocks) * block, block), block)
                mine = place_ref[0] == owner
                near = jnp.where(mine, near_own[at, :], near_other[at, :])
                far = jnp.where(mine, far_own[at, :], far_other[at, :])
                found = jnp.where(spot < blocks, near, far)
                out_ref[j * block : (j + 1) * block, :] = found.astype(WIDE)


def finish(place, arrays, moves, *earlier):
    rows, width = arrays[0].shape
    shape = jax.ShapeDtypeStruct((2 * rows, width), WIDE)
    tile = rows // 2
    return pl.pallas_call(
        ignoring(functools.partial(finish_kernel, moves=moves), 5, len(earlier)),
        out_shape=(shape, shape),
        grid_spec=pltpu.PrefetchScalarGridSpec(
            num_scalar_prefetch=1,
            grid=(8,),
            in_specs=[whole(array.shape) for array in arrays] + [ANY] * len(earlier),
            out_specs=(
                pl.BlockSpec((tile, width), lambda t, p: (jnp.minimum(t, 3), 0)),
                pl.BlockSpec((tile, width), lambda t, p: (jnp.maximum(t - 4, 0), 0)),
            ),
        ),
        compiler_params=pltpu.CompilerParams(vmem_limit_bytes=SMALL_LIMIT),
        cost_estimate=cost(),
        name="finish",
    )(place, *arrays, *earlier)


def on_device(
    inputs, cotangent, w_query, b_query, w_key, w_value, b_value, w_out, b_out, gain_one,
    shift_one, w_up, b_up, w_down, b_down, gain_two, shift_two, live_counts, valid_mask, segments,
):
    seqs, piece, width = inputs.shape
    count = lax.axis_size("seq")
    me = lax.axis_index("seq").astype(jnp.int32)
    slots = seqs // count
    length = piece * count
    x, y, z, rest = chip_axes()
    names = [CORE, x, y, z] + rest
    bits = jnp.stack([bit_of(*axis).astype(jnp.int32) for axis in names])
    core = bits[0]
    chain = Chain(bits)
    chain.last = (segments,)
    base = (me * slots).reshape(1)

    x_got = []
    for slot in range(slots):
        x_got.append(other_pieces(inputs, slot, slots, *(x_got[-1][-1:] if x_got else ())))
    vectors = jnp.concatenate(
        [v.reshape(1, -1) for v in (
            b_query, b_value, b_out, gain_one, shift_one, b_down, gain_two, shift_two
        )]
    ).astype(WIDE)
    bias_up = b_up.astype(WIDE).reshape(1, -1)
    live = (jnp.arange(seqs) < live_counts[0]).astype(jnp.int32)
    code = segments * 2 + valid_mask * live[:, None]
    codes = jnp.stack(
        [
            jnp.concatenate(
                [lax.dynamic_index_in_dim(code, base[0] + slot, 0, keepdims=False)]
                + other_pieces(code, slot, slots)
            )
            for slot in range(slots)
        ]
    )
    segs = codes // 2
    weight = codes % 2
    marks = jnp.where(weight > 0, segs, -1)

    forward = []
    for slot in range(slots):
        forward.append(
            chain.run(
                attend, jnp.stack([base[0], jnp.int32(slot)]), inputs, x_got[slot], segs, marks, vectors, w_query, w_key,
                w_value, w_out,
            )
        )
    cot_got = [[] for _ in range(count - 1)]
    for slot in range(slots):
        for n, got in enumerate(other_pieces(cotangent, slot, slots, x_got[-1][-1], forward[0][9])):
            cot_got[n].append(got)
    cot_got = [jnp.stack(got) for got in cot_got]
    slope, mid_low, result_own, result_sent, grad_h2, grad_feed, down, sums_two, stat_two = (
        chain.run(
            feed_forward, base, [each[6] for each in forward], cotangent, cot_got, marks, w_up,
            bias_up, w_down, vectors,
        )
    )
    everywhere = ("dp", "seq")
    down = lax.psum_scatter(down, everywhere, scatter_dimension=0, tiled=True)
    result_got = send_back([result_sent[n] for n in range(count - 1)])
    grad_h1, grad_attn, grad_ctx, grad_hid, up_sums, sums_one = chain.run(
        feed_back, jnp.stack([bits[2], core]), grad_feed, grad_h2, slope,
        [each[7] for each in forward], [each[8] for each in forward], w_up, w_down, w_out,
        vectors,
    )
    up_early, up_late, up_kept = chain.run(up_grads, grad_hid, mid_low, *result_got)
    up_early, up_late = swap(up_early, *y), swap(up_late, *y)
    last = rest[0]
    up = Reduction(up_kept, None, [y, CORE, z, x] + rest, names, [y, x, z, last])
    backward, grad_got = [], []
    for slot in range(slots):
        q, k, v, _, ctx, lse = forward[slot][:6]
        backward.append(
            chain.run(
                attend_back, piece, jnp.full((1,), slot, jnp.int32), q, k, v, ctx, grad_ctx, lse,
                segs, marks, grad_h1, w_query, w_key, w_value,
            )
        )
        sent = backward[-1][4]
        grad_got.append(
            send_back([sent[n * piece : (n + 1) * piece] for n in range(count - 1)])
        )
    small = chain.run(
        collect, [each[5] for each in backward], sums_one, sums_two, up_sums,
        [each[9] for each in forward] + [stat_two], marks,
    )
    chain.round(up.send_early(up_early))
    square_sent0, square_sent1, square_kept0, square_kept1 = chain.run(
        square_grads, bits[0:1], [each[3] for each in forward],
        *([each[i] for each in backward] for i in range(3)), [each[4] for each in forward],
        grad_attn,
    )
    squares = [
        Reduction(square_kept0, swap(square_sent0, *CORE), [CORE, x, y, z] + rest, names, [x, z, y, last]),
        Reduction(square_kept1, swap(square_sent1, *CORE), [CORE, y, z, x] + rest, names, [z, x, y, last]),
    ]

    def each_square(step):
        return [step(square) for square in squares]

    chain.round(up.send_late(up_late))
    chain.round(*each_square(Reduction.send), up.send())
    chain.round(*each_square(Reduction.send), up.send())
    few = small.shape[0]
    down = chain.run(attach, small, down)
    down = lax.all_gather(down, everywhere, axis=0, tiled=False)
    chain.round(*each_square(Reduction.send), up.send())
    for _ in range(up.more_shares()):
        chain.round(up.share())
    chain.round(*each_square(Reduction.send), up.share())
    result_out = chain.run(join, me.reshape(1), [result_own] + result_got, slots, count)
    for _ in range(up.more_shares()):
        chain.round(*each_square(Reduction.share))
    chain.round(*each_square(Reduction.share), up.gather())
    grad_arrays = [each[3] for each in backward]
    for n in range(count - 1):
        grad_arrays += [got[n] for got in grad_got]
    grad_out = chain.run(join, me.reshape(1), grad_arrays, slots, count)
    chain.round(*each_square(Reduction.gather), up.gather())
    chain.round(*each_square(Reduction.gather))
    small, grad_w_down = chain.run(detach, down, few)
    chain.round(*each_square(Reduction.gather), up.gather())
    finished = [
        chain.run(finish, jnp.stack([core, square.place()]), square.halves(), square.moves())
        for square in squares
    ]
    up_place = [core, up.place()]
    up_near = up.have, swap(up.have, *CORE)
    grad_w_up = chain.run(
        turn, jnp.stack(up_place + [bits[2]]), *up_near, up.moves(), None
    )
    far = chain.run(gate, up.got)
    grad_w_up = turn(
        jnp.stack(up_place + [1 - bits[2]]), far, swap(far, *CORE), up.moves(), grad_w_up
    )
    rms_values = jnp.sqrt(small[8, :4] / (width * small[8, 4]))
    hidden = w_up.shape[1]
    return (
        result_out,
        grad_out,
        finished[0][0],
        small[0],
        finished[1][0],
        finished[0][1],
        small[1],
        finished[1][1],
        small[4],
        small[2],
        small[3],
        grad_w_up,
        small[9 : 9 + hidden // width].reshape(-1),
        grad_w_down,
        small[7],
        small[5],
        small[6],
        rms_values,
    )


def solution(mesh):
    split = P("dp", "seq", None)
    pair = P("dp", "seq")
    return jax.shard_map(
        on_device,
        mesh=mesh,
        in_specs=(split, split) + (P(),) * 15 + (P("dp"), pair, pair),
        out_specs=(split, split) + (P(),) * 16,
        check_vma=False,
    )
```

```python
import functools

import jax
import jax.numpy as jnp
from jax import lax
from jax.experimental import pallas as pl
from jax.experimental.pallas import tpu as pltpu
from jax.sharding import PartitionSpec as P

HEAD_DIM = 64
EPSILON = 1e-05
NEGATIVE = -1e30
SCORE_SCALE = 0.125
LOW = jnp.bfloat16
WIDE = jnp.float32
VMEM_LIMIT = 63 * 1024 * 1024
SMALL_LIMIT = 20 * 1024 * 1024
HIDDEN_STEP = 768
TILE = 256
ROWS = 32
ROWS_NORM = 16
ANY = pl.BlockSpec(memory_space=pltpu.HBM)
IN_VMEM = pl.BlockSpec(memory_space=pltpu.VMEM)
IN_SMEM = pl.BlockSpec(memory_space=pltpu.SMEM)

ERF_P = 0.3275911
ERF_C = (0.254829592, -0.284496736, 1.421413741, -1.453152027, 1.061405429)
ROOT_HALF = 0.7071067811865476
DENSITY = 0.3989422804014327
EXP2_SCALE = -0.7213475204444817


def nn(left, right):
    return jnp.dot(left, right, preferred_element_type=WIDE)


def nt(left, right):
    return lax.dot_general(
        left, right, (((1,), (1,)), ((), ())), preferred_element_type=WIDE
    )


def tn(left, right):
    return lax.dot_general(
        left, right, (((0,), (0,)), ((), ())), preferred_element_type=WIDE
    )


def gelu_pair(hidden):
    size = jnp.abs(hidden)
    falling = jnp.exp2(hidden * hidden * EXP2_SCALE)
    t = pl.reciprocal(1.0 + (ERF_P * ROOT_HALF) * size, approx=True)
    c1, c2, c3, c4, c5 = (0.5 * c for c in ERF_C)
    shape = ((((c5 * t + c4) * t + c3) * t + c2) * t + c1) * t
    gone = falling * (shape - DENSITY * size)
    slope = jnp.where(hidden >= 0.0, 1.0 - gone, gone)
    return jnp.maximum(hidden, 0.0) - size * (shape * falling), slope


def lane_half(half):
    lane = lax.broadcasted_iota(jnp.int32, (1, 2 * HEAD_DIM), 1)
    inside = (lane < HEAD_DIM) if half == 0 else (lane >= HEAD_DIM)
    return inside.astype(WIDE).astype(LOW)


def fill_bias(bias_ref, seg_row, mark_col):
    length = bias_ref.shape[0]
    key_place = lax.broadcasted_iota(jnp.int32, (length, length), 0)
    query_place = lax.broadcasted_iota(jnp.int32, (length, length), 1)
    visible = (mark_col == seg_row) | (key_place == query_place)
    bias_ref[...] = jnp.where(visible, 0.0, NEGATIVE)


def total(rows_weight, values):
    per_row = jnp.sum(values * values, axis=1, keepdims=True) * rows_weight
    return jnp.sum(per_row, axis=0, keepdims=True)


def column(row):
    return jnp.broadcast_to(row.astype(WIDE), (8, row.shape[1])).T[:, 0:1]


VECTORS = ("b_query", "b_value", "b_out", "gain_one", "shift_one", "b_down", "gain_two", "shift_two")


def vector(ref, name):
    place = VECTORS.index(name)
    return ref[place : place + 1, :]


def attend_kernel(
    place_ref, seg_ref, mark_ref, vectors_ref, wq_ref, wk_ref, wv_ref, wo_ref, inputs_ref, *refs,
    pieces,
):
    (
        q_ref, k_ref, v_ref, x_ref, ctx_ref, lse_ref, mid_ref, norm_ref, rstd_ref, stat_ref,
        wq_s, wk_s, wv_s, wo_s, q_s, k_s, v_s, x_s, bias_s, score_s, chance_s, weight_s, in_sems,
        out_sems,
    ) = refs[pieces - 1 :]
    length, model = x_s.shape
    piece = length // pieces
    loads = [
        pltpu.make_async_copy(a, b, in_sems.at[n])
        for n, (a, b) in enumerate(
            ((wk_ref, wk_s), (wq_ref, wq_s), (wv_ref, wv_s), (wo_ref, wo_s))
        )
    ]
    tokens_in = [
        pltpu.make_async_copy(a, x_s.at[pl.ds(n * piece, piece), :], in_sems.at[4 + n])
        for n, a in enumerate((inputs_ref.at[place_ref[0] + place_ref[1]],) + refs[: pieces - 1])
    ]
    for load in tokens_in + loads:
        load.start()
    stores = [
        pltpu.make_async_copy(a, b, out_sems.at[n])
        for n, (a, b) in enumerate(((k_s, k_ref), (q_s, q_ref), (v_s, v_ref), (x_s, x_ref)))
    ]
    own = pl.ds(place_ref[1], 1)
    mark_col = column(mark_ref[own, :])
    weight_s[...] = (mark_col >= 0).astype(WIDE)
    fill_bias(bias_s, seg_ref[own, :].astype(WIDE), mark_col)
    heads = model // HEAD_DIM
    width = 2 * HEAD_DIM
    for load in tokens_in:
        load.wait()
    stores[3].start()
    loads[0].wait()
    k_s[...] = nn(x_s[...], wk_s[...]).astype(LOW)
    stores[0].start()
    loads[1].wait()
    q_s[...] = ((nn(x_s[...], wq_s[...]) + vector(vectors_ref, "b_query")) * SCORE_SCALE).astype(LOW)
    stores[1].start()
    loads[2].wait()
    v_s[...] = (nn(x_s[...], wv_s[...]) + vector(vectors_ref, "b_value")).astype(LOW)
    stores[2].start()

    def lanes(head):
        return pl.ds(head // 2 * width, width)

    def scores(head):
        keys = k_s[:, lanes(head)] * lane_half(head % 2)
        score_s[head % 2] = nt(keys, q_s[:, lanes(head)])

    def soften(head):
        here, chance = score_s.at[head % 2], chance_s.at[head % 2]
        top = jnp.full((8, length), NEGATIVE, WIDE)
        for row in range(0, length, ROWS):
            block = here[row : row + ROWS, :] + bias_s[row : row + ROWS, :]
            here[row : row + ROWS, :] = block
            top = jnp.maximum(top, jnp.max(block.reshape(-1, 8, length), axis=0))
        top = jnp.max(top, axis=0, keepdims=True)
        amount = jnp.zeros((8, length), WIDE)
        for row in range(0, length, ROWS):
            block = jnp.exp(here[row : row + ROWS, :] - top)
            chance[row : row + ROWS, :] = block.astype(LOW)
            amount = amount + jnp.sum(block.reshape(-1, 8, length), axis=0)
        amount = jnp.sum(amount, axis=0, keepdims=True)
        lse_ref[head : head + 1, :] = top + jnp.log(amount)
        return 1.0 / amount

    def combine(head, share, turned):
        part = turned[head % 2 * HEAD_DIM : (head % 2 + 1) * HEAD_DIM]
        summed = nn(part, chance_s[head % 2]) * share
        ctx_ref[head * HEAD_DIM : (head + 1) * HEAD_DIM, :] = summed.astype(LOW)

    scores(0)
    waiting = None
    for head in range(heads):
        share = soften(head)
        if head % 2 == 0:
            turned = v_s[:, lanes(head)].T
        if head + 1 < heads:
            scores(head + 1)
        if waiting is not None:
            combine(*waiting)
        waiting = (head, share, turned)
    combine(*waiting)
    loads[3].wait()
    attention_all = tn(ctx_ref[...], wo_s[...])
    bias, gain, shift = (vector(vectors_ref, n) for n in ("b_out", "gain_one", "shift_one"))
    stats = [jnp.zeros((1, 1), WIDE) for _ in range(2)]
    for row in range(0, length, ROWS_NORM):
        at = pl.ds(row, ROWS_NORM)
        attention = attention_all[row : row + ROWS_NORM] + bias
        rows = x_s[at, :].astype(WIDE)
        total_in = rows + attention
        center = total_in - jnp.mean(total_in, axis=1, keepdims=True)
        rstd = lax.rsqrt(jnp.mean(center * center, axis=1, keepdims=True) + EPSILON)
        normal = center * rstd
        mid_ref[at, :] = normal * gain + shift
        norm_ref[at, :] = normal.astype(LOW)
        rstd_ref[at, :] = rstd
        row_weight = weight_s[at, :]
        stats[0] = stats[0] + total(row_weight, rows)
        stats[1] = stats[1] + total(row_weight, attention)
    stat_ref[...] = jnp.concatenate(
        [jnp.broadcast_to(stat, (1, 128)) for stat in stats] + [jnp.zeros((6, 128), WIDE)], axis=0
    )
    for store in stores:
        store.wait()


def cost(flops=10**8):
    return pl.CostEstimate(flops=flops, transcendentals=0, bytes_accessed=0)


def ignoring(kernel, inputs, extra):
    def wrapped(*refs):
        return kernel(*refs[:inputs], *refs[inputs + extra :])

    return wrapped


def whole(shape):
    return pl.BlockSpec(shape, lambda *_: (0,) * len(shape), pipeline_mode=pl.Buffered(1))


def attend(place, inputs, got, segs, marks, vectors, wq, wk, wv, wo, *earlier):
    pieces = len(got) + 1
    length, width = inputs.shape[1] * pieces, inputs.shape[2]
    heads = width // HEAD_DIM
    lse_rows = heads + (-heads) % 8
    tokens_out = jax.ShapeDtypeStruct((length, width), LOW)
    shapes = (
        tokens_out, tokens_out, tokens_out, tokens_out,
        jax.ShapeDtypeStruct((width, length), LOW),
        jax.ShapeDtypeStruct((lse_rows, length), WIDE),
        jax.ShapeDtypeStruct((length, width), WIDE),
        tokens_out,
        jax.ShapeDtypeStruct((length, 1), WIDE),
        jax.ShapeDtypeStruct((8, 128), WIDE),
    )
    args = (place, segs, marks, vectors, wq, wk, wv, wo, inputs, *got)
    weight = pltpu.VMEM((width, width), LOW)
    tokens = pltpu.VMEM((length, width), LOW)
    return pl.pallas_call(
        ignoring(
            functools.partial(attend_kernel, pieces=pieces), len(args), len(earlier)
        ),
        out_shape=shapes,
        in_specs=[IN_SMEM] + [IN_VMEM] * 3 + [ANY] * (4 + pieces + len(earlier)),
        out_specs=(ANY,) * 4 + (IN_VMEM,) * 6,
        scratch_shapes=[weight] * 4 + [tokens] * 4 + [
            pltpu.VMEM((length, length), WIDE),
            pltpu.VMEM((2, length, length), WIDE),
            pltpu.VMEM((2, length, length), LOW),
            pltpu.VMEM((length, 1), WIDE),
            pltpu.SemaphoreType.DMA((4 + pieces,)),
            pltpu.SemaphoreType.DMA((4,)),
        ],
        compiler_params=pltpu.CompilerParams(vmem_limit_bytes=VMEM_LIMIT),
        cost_estimate=cost(),
        name="attend",
    )(*args, *earlier)


def norm_back(grad, normal, rstd, gain):
    pulled = grad * gain
    return rstd * (
        pulled
        - jnp.mean(pulled, axis=1, keepdims=True)
        - normal * jnp.mean(pulled * normal, axis=1, keepdims=True)
    )


def row_total(values):
    return jnp.sum(values, axis=0, keepdims=True)


def feed_kernel(
    place_ref, mid0_ref, mid1_ref, cot_ref, mark_ref, bu_ref, vectors_ref, wu_ref, wd_ref, *refs,
    pieces,
):
    (
    slope_ref, low_ref, own_ref, sent_ref, grad_ref, grad_low_ref, down_ref, sums_ref, stat_ref,
    mid_s, cot_s, wu_s, wd_s, act_s, slope_s, low_s, result_s, grad_s, grad_low_s, out_s,
    feed_s, weight_s, sum_s, in_sems, up_sems, down_sems, tile_sems, out_sems,
    ) = refs[pieces - 1 :]
    length, width = mid0_ref.shape
    rows = cot_s.shape[0]
    piece = length // pieces
    hidden = wu_ref.shape[1]
    half = hidden // 2
    chunks = hidden // HIDDEN_STEP
    tile = TILE
    def own(chunk):
        return pl.ds(chunk * HIDDEN_STEP, HIDDEN_STEP)

    first_in = pltpu.make_async_copy(mid0_ref, mid_s.at[pl.ds(0, length)], in_sems.at[0])
    second_in = pltpu.make_async_copy(mid1_ref, mid_s.at[pl.ds(length, length)], in_sems.at[1])
    cot_in = []
    for slot in range(rows // length):
        own_piece = cot_ref.at[place_ref[0] + slot]
        for part, ref in enumerate([own_piece] + [ref.at[slot] for ref in refs[: pieces - 1]]):
            spot = pl.ds(slot * length + part * piece, piece)
            sem = in_sems.at[2 + len(cot_in)]
            cot_in.append(pltpu.make_async_copy(ref, cot_s.at[spot, :], sem))
    ups = [
        pltpu.make_async_copy(wu_ref.at[:, own(c)], wu_s.at[:, own(c)], up_sems.at[c])
        for c in range(chunks)
    ]
    downs = [
        pltpu.make_async_copy(wd_ref.at[own(c), :], wd_s.at[own(c), :], down_sems.at[c])
        for c in range(chunks)
    ]
    first_in.start()
    for chunk in range(chunks):
        ups[chunk].start()
        downs[chunk].start()
    second_in.start()
    for copy in cot_in:
        copy.start()
    sums_ref[...] = jnp.zeros_like(sums_ref)
    stat_ref[...] = jnp.zeros_like(stat_ref)
    sum_s[...] = jnp.zeros_like(sum_s)
    for slot in range(mark_ref.shape[0]):
        mark_col = column(mark_ref[slot : slot + 1, :])
        weight_s[pl.ds(slot * length, length), :] = (mark_col >= 0).astype(WIDE)

    def tile_copies(index):
        spot = pl.ds(pl.multiple_of(index * tile, tile), tile)
        pairs = (
            (low_s, low_ref), (grad_s, grad_ref), (grad_low_s, grad_low_ref), (slope_s, slope_ref),
        )
        return [
            pltpu.make_async_copy(a.at[spot, :], b.at[spot, :], tile_sems.at[n, index])
            for n, (a, b) in enumerate(pairs)
        ]

    def inside(index, row, count=ROWS):
        return pl.ds(pl.multiple_of(index * tile + row, count), count)

    def work(index, opening):
        spot = pl.ds(pl.multiple_of(index * tile, tile), tile)
        for row in range(0, tile, ROWS):
            low_s[inside(index, row), :] = mid_s[inside(index, row), :].astype(LOW)
        middle_low = low_s[spot, :]

        def up(chunk):
            if opening:
                ups[chunk].wait()
            return nn(middle_low, wu_s[:, own(chunk)])

        def down(chunk, feed):
            if opening:
                downs[chunk].wait()
            more = nn(act_s[spot, own(chunk)], wd_s[own(chunk), :])
            return more if feed is None else feed + more

        before = pl.ds(pl.multiple_of((index - 1) * tile, tile), tile)
        feed = None
        ahead = up(0)
        for chunk in range(chunks):
            bias = bu_ref[:, own(chunk)]
            for row in range(0, tile, ROWS):
                active, slope = gelu_pair(ahead[row : row + ROWS] + bias)
                act_s[inside(index, row), own(chunk)] = active.astype(LOW)
                slope_s[inside(index, row), own(chunk)] = slope.astype(LOW)
            if chunk + 1 < chunks:
                ahead = up(chunk + 1)
            if chunk > 0:
                feed = down(chunk - 1, feed)
            if not opening:
                gather_outer(sum_s, act_s, grad_low_s, before, own(chunk))
        feed_s[...] = down(chunks - 1, feed)

    def norm(index):
        gain, shift, bias = (vector(vectors_ref, n) for n in ("gain_two", "shift_two", "b_down"))
        sums = [jnp.zeros((1, width), WIDE) for _ in range(3)]
        stats = [jnp.zeros((1, 1), WIDE) for _ in range(2)]
        for row in range(0, tile, ROWS_NORM):
            here = inside(index, row, ROWS_NORM)
            feed_here = feed_s[row : row + ROWS_NORM, :] + bias
            total_in = mid_s[here, :] + feed_here
            center = total_in - jnp.mean(total_in, axis=1, keepdims=True)
            rstd = lax.rsqrt(jnp.mean(center * center, axis=1, keepdims=True) + EPSILON)
            normal = center * rstd
            result = normal * gain + shift
            result_s[here, :] = result.astype(LOW)
            weight = weight_s[here, :]
            grad_result = cot_s[here, :].astype(WIDE) * weight
            grad = norm_back(grad_result, normal, rstd, gain)
            grad_s[here, :] = grad
            grad_low = grad.astype(LOW)
            grad_low_s[here, :] = grad_low
            sums[0] = sums[0] + row_total(grad_result * normal)
            sums[1] = sums[1] + row_total(grad_result)
            sums[2] = sums[2] + row_total(grad_low.astype(WIDE))
            stats[0] = stats[0] + total(weight, feed_here)
            stats[1] = stats[1] + total(weight, result)
        for n in range(3):
            sums_ref[n : n + 1, :] += sums[n]
        for n in range(2):
            stat_ref[n : n + 1, :] += jnp.broadcast_to(stats[n], (1, 128))

    first_in.wait()
    work(0, True)
    second_in.wait()
    for copy in cot_in:
        copy.wait()

    def turn(index, carried):
        norm(index - 1)
        work(index, False)
        for copy in tile_copies(index - 1):
            copy.start()
        return carried

    lax.fori_loop(1, rows // tile, turn, 0)
    norm(rows // tile - 1)
    for copy in tile_copies(rows // tile - 1):
        copy.start()
    results = []
    for slot in range(rows // length):
        for part in range(pieces):
            spot = pl.ds(slot * length + part * piece, piece)
            target = sent_ref.at[part - 1, slot] if part else own_ref.at[slot]
            sem = in_sems.at[2 + len(results)]
            results.append(pltpu.make_async_copy(result_s.at[spot, :], target, sem))
            results[-1].start()
    outer(act_s, grad_low_s, out_s, (down_ref,), out_sems, sum_s, pl.ds(rows - tile, tile))
    for copy in results:
        copy.wait()
    for index in range(rows // tile):
        for copy in tile_copies(index):
            copy.wait()


def gather_outer(sum_s, left_s, right_s, rows, columns):
    sum_s[columns, :] += tn(left_s[rows, columns], right_s[rows, :])


def outer(left_s, right_s, out_s, targets, sems, sum_s, rows):
    places = [
        ref.at[pl.ds(row, HIDDEN_STEP), :]
        for ref in targets
        for row in range(0, ref.shape[0], HIDDEN_STEP)
    ]
    copies = []
    for step, target in enumerate(places):
        spot = pl.ds(step * HIDDEN_STEP, HIDDEN_STEP)
        out_s[spot, :] = (sum_s[spot, :] + tn(left_s[rows, spot], right_s[rows, :])).astype(LOW)
        copies.append(pltpu.make_async_copy(out_s.at[spot, :], target, sems.at[step]))
        copies[-1].start()
    for copy in copies:
        copy.wait()


def feed_forward(place, mids, cot, got, marks, wu, bu, wd, vectors, *earlier):
    length, width = mids[0].shape
    rows = length * len(mids)
    pieces = len(got) + 1
    hidden = wu.shape[1]
    chunks = hidden // HIDDEN_STEP
    shapes = (
        jax.ShapeDtypeStruct((rows, hidden), LOW),
        jax.ShapeDtypeStruct((rows, width), LOW),
        jax.ShapeDtypeStruct((len(mids), length // pieces, width), LOW),
        jax.ShapeDtypeStruct((pieces - 1, len(mids), length // pieces, width), LOW),
        jax.ShapeDtypeStruct((rows, width), WIDE),
        jax.ShapeDtypeStruct((rows, width), LOW),
        jax.ShapeDtypeStruct((hidden, width), LOW),
        jax.ShapeDtypeStruct((8, width), WIDE),
        jax.ShapeDtypeStruct((8, 128), WIDE),
    )
    return pl.pallas_call(
        ignoring(functools.partial(feed_kernel, pieces=pieces), 8 + pieces, len(earlier)),
        out_shape=shapes,
        in_specs=[IN_SMEM] + [ANY] * 3 + [IN_VMEM] * 3 + [ANY] * (1 + pieces + len(earlier)),
        out_specs=(ANY,) * 7 + (IN_VMEM,) * 2,
        scratch_shapes=[
            pltpu.VMEM((rows, width), WIDE),
            pltpu.VMEM((rows, width), LOW),
            pltpu.VMEM((width, hidden), LOW),
            pltpu.VMEM((hidden, width), LOW),
            pltpu.VMEM((rows, hidden), LOW),
            pltpu.VMEM((rows, hidden), LOW),
            pltpu.VMEM((rows, width), LOW),
            pltpu.VMEM((rows, width), LOW),
            pltpu.VMEM((rows, width), WIDE),
            pltpu.VMEM((rows, width), LOW),
            pltpu.VMEM((hidden, width), LOW),
            pltpu.VMEM((TILE, width), WIDE),
            pltpu.VMEM((rows, 1), WIDE),
            pltpu.VMEM((hidden, width), WIDE),
            pltpu.SemaphoreType.DMA((2 + pieces * len(mids),)),
            pltpu.SemaphoreType.DMA((chunks,)),
            pltpu.SemaphoreType.DMA((chunks,)),
            pltpu.SemaphoreType.DMA((4, rows // TILE)),
            pltpu.SemaphoreType.DMA((chunks,)),
        ],
        compiler_params=pltpu.CompilerParams(vmem_limit_bytes=VMEM_LIMIT),
        cost_estimate=cost(),
        name="feed_forward",
    )(place, mids[0], mids[1], cot, marks, bu, vectors, wu, wd, *got, *earlier)


def feed_back_kernel(
    place_ref, grad_low_ref, grad_ref, slope_ref, norm0_ref, norm1_ref, low_ref, wu_ref, wd_ref,
    wo_ref, rstd0_ref, rstd1_ref, vectors_ref,
    grad_one_ref, attn_ref, ctx_ref, send_ref, keep_ref, up_sums_ref, sums_ref,
    grad_low_s, grad_s, slope_s, norm_s, low_s, wu_s, wd_s, wo_s, rstd_s, grad_one_s, attn_s,
    ctx_s, middle_s, sum_s, out_s,
    in_sems, slope_sems, up_sems, down_sems, tile_sems, ctx_sems, out_sems,
):
    length = norm0_ref.shape[0]
    rows, width = grad_low_ref.shape
    hidden = wu_ref.shape[1]
    half = hidden // 2
    chunks = hidden // HIDDEN_STEP
    tile = TILE
    mine = place_ref[0]

    def place_of(chunk):
        part, inside = divmod(chunk * HIDDEN_STEP, half)
        start = (mine if part else 1 - mine) * half + inside
        return pl.ds(pl.multiple_of(start, HIDDEN_STEP), HIDDEN_STEP)

    def own(chunk):
        return pl.ds(chunk * HIDDEN_STEP, HIDDEN_STEP)

    def spot_of(index):
        return pl.ds(pl.multiple_of(index * tile, tile), tile)

    slopes = [
        pltpu.make_async_copy(
            slope_ref.at[spot_of(i), place_of(c)],
            slope_s.at[spot_of(i), own(c)],
            slope_sems.at[chunks * i + c],
        )
        for i in range(rows // tile)
        for c in range(chunks)
    ]
    ups = [
        pltpu.make_async_copy(wu_ref.at[:, place_of(c)], wu_s.at[:, own(c)], up_sems.at[c])
        for c in range(chunks)
    ]
    downs = [
        pltpu.make_async_copy(wd_ref.at[place_of(c), :], wd_s.at[own(c), :], down_sems.at[c])
        for c in range(chunks)
    ]
    others = [
        pltpu.make_async_copy(a, b, in_sems.at[n])
        for n, (a, b) in enumerate(
            (
                (grad_low_ref, grad_low_s),
                (grad_ref, grad_s),
                (norm0_ref, norm_s.at[pl.ds(0, length)]),
                (norm1_ref, norm_s.at[pl.ds(length, length)]),
                (wo_ref, wo_s),
                (low_ref, low_s),
            )
        )
    ]
    others[0].start()
    downs[0].start()
    slopes[0].start()
    ups[0].start()
    for chunk in range(1, chunks):
        downs[chunk].start()
        slopes[chunk].start()
        ups[chunk].start()
    for copy in others[1:] + slopes[chunks:]:
        copy.start()
    rstd_s[pl.ds(0, length), :] = rstd0_ref[...]
    rstd_s[pl.ds(length, length), :] = rstd1_ref[...]
    sums_ref[...] = jnp.zeros_like(sums_ref)
    up_sums_ref[...] = jnp.zeros_like(up_sums_ref)
    sum_s[...] = jnp.zeros_like(sum_s)

    def tile_copies(index):
        spot = spot_of(index)
        pairs = ((grad_one_s, grad_one_ref), (attn_s, attn_ref))
        return [
            pltpu.make_async_copy(a.at[spot, :], b.at[spot, :], tile_sems.at[n, index])
            for n, (a, b) in enumerate(pairs)
        ]

    def inside(index, row, count=ROWS):
        return pl.ds(pl.multiple_of(index * tile + row, count), count)

    def work(index, opening):
        spot = spot_of(index)
        grad_low = grad_low_s[spot, :]

        def back(chunk):
            if opening:
                downs[chunk].wait()
            return nt(grad_low, wd_s[own(chunk), :])

        def forth(chunk, grad):
            if opening:
                ups[chunk].wait()
            more = nt(slope_s[spot, own(chunk)], wu_s[:, own(chunk)])
            return more if grad is None else grad + more

        before = pl.ds(pl.multiple_of((index - 1) * tile, tile), tile)
        ahead = back(0)
        grad_middle = None
        for chunk in range(chunks):
            if opening:
                slopes[chunk].wait()
            sums = jnp.zeros((8, HIDDEN_STEP), WIDE)
            for row in range(0, tile, ROWS):
                at = inside(index, row)
                slope = slope_s[at, own(chunk)].astype(WIDE)
                grad_hidden = (ahead[row : row + ROWS] * slope).astype(LOW)
                slope_s[at, own(chunk)] = grad_hidden
                sums = sums + jnp.sum(
                    grad_hidden.astype(WIDE).reshape(-1, 8, HIDDEN_STEP), axis=0
                )
            up_sums_ref[:, place_of(chunk)] += sums
            if chunk + 1 < chunks:
                ahead = back(chunk + 1)
            if chunk > 0:
                grad_middle = forth(chunk - 1, grad_middle)
            if not opening:
                gather_outer(sum_s, slope_s, low_s, before, own(chunk))
        middle_s[...] = forth(chunks - 1, grad_middle)

    def norm(index):
        gain = vector(vectors_ref, "gain_one")
        sums = [jnp.zeros((1, width), WIDE) for _ in range(3)]
        for row in range(0, tile, ROWS_NORM):
            at = inside(index, row, ROWS_NORM)
            grad = middle_s[row : row + ROWS_NORM, :] + grad_s[at, :]
            normal = norm_s[at, :].astype(WIDE)
            grad_one = norm_back(grad, normal, rstd_s[at, :], gain)
            grad_one_s[at, :] = grad_one
            attn = grad_one.astype(LOW)
            attn_s[at, :] = attn
            sums[0] = sums[0] + row_total(grad * normal)
            sums[1] = sums[1] + row_total(grad)
            sums[2] = sums[2] + row_total(attn.astype(WIDE))
        for n in range(3):
            sums_ref[n : n + 1, :] += sums[n]

    def project(index):
        spot = spot_of(index)
        turned = nt(wo_s[...], attn_s[spot, :]).astype(LOW)
        slot, inner = divmod(index * tile, length)
        ctx_s[slot, :, inner : inner + tile] = turned
        copy = pltpu.make_async_copy(
            ctx_s.at[slot, :, pl.ds(inner, tile)], ctx_ref.at[slot, :, pl.ds(inner, tile)],
            ctx_sems.at[index],
        )
        copy.start()
        return copy

    others[0].wait()
    work(0, True)
    for copy in slopes[chunks:] + others[1:]:
        copy.wait()

    def turn(index, carried):
        norm(index - 1)
        work(index, False)
        for copy in tile_copies(index - 1):
            copy.start()
        return carried

    lax.fori_loop(1, rows // tile, turn, 0)
    norm(rows // tile - 1)
    for copy in tile_copies(rows // tile - 1):
        copy.start()
    copies = [project(index) for index in range(rows // tile)]
    outer(
        slope_s, low_s, out_s, (send_ref, keep_ref), out_sems, sum_s,
        pl.ds(rows - tile, tile),
    )
    for copy in copies:
        copy.wait()
    for index in range(rows // tile):
        for copy in tile_copies(index):
            copy.wait()


def feed_back(place, grad_low, grad, slope, norms, rstds, mid_low, wu, wd, wo, vectors, *earlier):
    rows, width = grad.shape
    length = norms[0].shape[0]
    hidden = wu.shape[1]
    chunks = hidden // HIDDEN_STEP
    part = jax.ShapeDtypeStruct((hidden // 2, width), LOW)
    shapes = (
        jax.ShapeDtypeStruct((rows, width), WIDE),
        jax.ShapeDtypeStruct((rows, width), LOW),
        jax.ShapeDtypeStruct((rows // length, width, length), LOW),
        part, part,
        jax.ShapeDtypeStruct((8, hidden), WIDE),
        jax.ShapeDtypeStruct((8, width), WIDE),
    )
    return pl.pallas_call(
        ignoring(feed_back_kernel, 13, len(earlier)),
        out_shape=shapes,
        in_specs=[IN_SMEM] + [ANY] * 9 + [IN_VMEM] * 3 + [ANY] * len(earlier),
        out_specs=(ANY,) * 5 + (IN_VMEM,) * 2,
        scratch_shapes=[
            pltpu.VMEM((rows, width), LOW),
            pltpu.VMEM((rows, width), WIDE),
            pltpu.VMEM((rows, hidden), LOW),
            pltpu.VMEM((rows, width), LOW),
            pltpu.VMEM((rows, width), LOW),
            pltpu.VMEM((width, hidden), LOW),
            pltpu.VMEM((hidden, width), LOW),
            pltpu.VMEM((width, width), LOW),
            pltpu.VMEM((rows, 1), WIDE),
            pltpu.VMEM((rows, width), WIDE),
            pltpu.VMEM((rows, width), LOW),
            pltpu.VMEM((rows // length, width, length), LOW),
            pltpu.VMEM((TILE, width), WIDE),
            pltpu.VMEM((hidden, width), WIDE),
            pltpu.VMEM((hidden, width), LOW),
            pltpu.SemaphoreType.DMA((6,)),
            pltpu.SemaphoreType.DMA((chunks * rows // TILE,)),
            pltpu.SemaphoreType.DMA((chunks,)),
            pltpu.SemaphoreType.DMA((chunks,)),
            pltpu.SemaphoreType.DMA((2, rows // TILE)),
            pltpu.SemaphoreType.DMA((rows // TILE,)),
            pltpu.SemaphoreType.DMA((chunks,)),
        ],
        compiler_params=pltpu.CompilerParams(vmem_limit_bytes=VMEM_LIMIT),
        cost_estimate=cost(),
        name="feed_back",
    )(
        place, grad_low, grad, slope, norms[0], norms[1], mid_low, wu, wd, wo, rstds[0], rstds[1],
        vectors, *earlier,
    )


def attend_back_kernel(
    place_ref, seg_ref, mark_ref, lse_ref, q_ref, k_ref, v_ref, ctx_ref, grad_ctx_ref, grad_one_ref, wq_ref,
    wk_ref, wv_ref,
    dq_ref, dk_ref, dv_ref, own_ref, sent_ref, sums_ref,
    q_s, k_s, v_s, ctx_s, grad_ctx_s, grad_one_s, wq_s, wk_s, wv_s, bias_s, score_s, pull_s,
    chance_s, grad_s, in_sems,
):
    length, model = q_ref.shape
    slot = place_ref[0]
    heads = model // HEAD_DIM
    width = 2 * HEAD_DIM
    loads = [
        pltpu.make_async_copy(a, b, in_sems.at[n])
        for n, (a, b) in enumerate(
            (
                (k_ref, k_s), (q_ref, q_s), (v_ref, v_s), (grad_ctx_ref.at[slot], grad_ctx_s),
                (ctx_ref, ctx_s), (wq_ref, wq_s), (wk_ref, wk_s), (wv_ref, wv_s),
                (grad_one_ref.at[pl.ds(pl.multiple_of(slot * length, length), length), :], grad_one_s),
            )
        )
    ]
    for load in loads:
        load.start()
    mark_col = column(mark_ref[pl.ds(slot, 1), :])
    fill_bias(bias_s, seg_ref[pl.ds(slot, 1), :].astype(WIDE), mark_col)

    def lanes(head):
        return pl.ds(head // 2 * width, width)

    def rows_of(head):
        return pl.ds(head * HEAD_DIM, HEAD_DIM)

    def products(head):
        score_s[head % 2] = nt(k_s[:, lanes(head)] * lane_half(head % 2), q_s[:, lanes(head)])
        values = v_s[:, lanes(head)] * lane_half(head % 2)
        pull_s[head % 2] = nn(values, grad_ctx_s[lanes(head), :])

    def soften(head):
        score, pull = score_s.at[head % 2], pull_s.at[head % 2]
        chance, grad = chance_s.at[head % 2], grad_s.at[head % 2]
        shared = grad_ctx_s[rows_of(head), :].astype(WIDE) * ctx_s[rows_of(head), :].astype(WIDE)
        delta = jnp.sum(shared, axis=0, keepdims=True)
        lse = lse_ref[head : head + 1, :]
        for row in range(0, length, ROWS):
            at = slice(row, row + ROWS)
            block = jnp.exp(score[at, :] + bias_s[at, :] - lse)
            chance[at, :] = block.astype(LOW)
            grad[at, :] = (block * (pull[at, :] - delta)).astype(LOW)

    def combine(head, turned):
        part_v = nt(chance_s[head % 2], grad_ctx_s[lanes(head), :])
        part_k = nn(grad_s[head % 2], q_s[:, lanes(head)])
        part = turned[head % 2 * HEAD_DIM : (head % 2 + 1) * HEAD_DIM]
        return part_v, part_k, nn(part, grad_s[head % 2])

    def keep(head, one, two):
        first = lax.broadcasted_iota(jnp.int32, one[0].shape, 1) < HEAD_DIM
        dv_ref[:, lanes(head)] = jnp.where(first, one[0], two[0]).astype(LOW)
        dk_ref[:, lanes(head)] = jnp.where(first, one[1], two[1]).astype(LOW)
        dq_ref[:, lanes(head)] = jnp.concatenate([one[2], two[2]], axis=0).T.astype(LOW)

    for load in loads[:4]:
        load.wait()
    products(0)
    loads[4].wait()
    waiting = None
    found = []
    for head in range(heads):
        soften(head)
        if head % 2 == 0:
            turned = k_s[:, lanes(head)].T
        if len(found) == 2:
            keep(head - 2, *found)
            found = []
        if head + 1 < heads:
            products(head + 1)
        if waiting is not None:
            found.append(combine(*waiting))
        waiting = (head, turned)
    found.append(combine(*waiting))
    keep(heads - 1, *found)
    for load in loads[5:]:
        load.wait()
    piece = own_ref.shape[0]
    for rows, ref in ((pl.ds(0, piece), own_ref), (pl.ds(piece, length - piece), sent_ref)):
        grad = (
            grad_one_s[rows, :]
            + nt(dq_ref[rows, :], wq_s[...]) * SCORE_SCALE
            + nt(dk_ref[rows, :], wk_s[...])
            + nt(dv_ref[rows, :], wv_s[...])
        )
        ref[...] = grad.astype(ref.dtype)
    sums_ref[...] = jnp.concatenate(
        [
            row_total(dq_ref[...].astype(WIDE)) * SCORE_SCALE,
            row_total(dv_ref[...].astype(WIDE)),
            jnp.zeros((6, model), WIDE),
        ],
        axis=0,
    )


def attend_back(piece, place, q, k, v, ctx, grad_ctx, lse, segs, marks, grad_one, wq, wk, wv, *earlier):
    length, width = q.shape
    heads = width // HEAD_DIM
    shapes = (
        jax.ShapeDtypeStruct((length, width), LOW),
        jax.ShapeDtypeStruct((length, width), LOW),
        jax.ShapeDtypeStruct((length, width), LOW),
        jax.ShapeDtypeStruct((piece, width), WIDE),
        jax.ShapeDtypeStruct((length - piece, width), LOW),
        jax.ShapeDtypeStruct((8, width), WIDE),
    )
    tokens = pltpu.VMEM((length, width), LOW)
    turned = pltpu.VMEM((width, length), LOW)
    weight = pltpu.VMEM((width, width), LOW)
    return pl.pallas_call(
        ignoring(attend_back_kernel, 13, len(earlier)),
        out_shape=shapes,
        in_specs=[IN_SMEM] + [IN_VMEM] * 3 + [ANY] * (9 + len(earlier)),
        out_specs=(IN_VMEM,) * 6,
        scratch_shapes=[
            tokens, tokens, tokens, turned, turned, pltpu.VMEM((length, width), WIDE),
            weight, weight, weight,
            pltpu.VMEM((length, length), WIDE),
            pltpu.VMEM((2, length, length), WIDE),
            pltpu.VMEM((2, length, length), WIDE),
            pltpu.VMEM((2, length, length), LOW),
            pltpu.VMEM((2, length, length), LOW),
            pltpu.SemaphoreType.DMA((9,)),
        ],
        compiler_params=pltpu.CompilerParams(vmem_limit_bytes=VMEM_LIMIT),
        cost_estimate=cost(),
        name="attend_back",
    )(place, segs, marks, lse, q, k, v, ctx, grad_ctx, grad_one, wq, wk, wv, *earlier)


def square_kernel(
    place_ref, x0_ref, x1_ref, dq0_ref, dq1_ref, dk0_ref, dk1_ref, dv0_ref, dv1_ref, ctx0_ref,
    ctx1_ref, attn_ref, send0_ref, send1_ref, keep0_ref, keep1_ref, x_s, dq_s, dk_s, dv_s, ctx_s, attn_s, out_s, in_sems,
    out_sems,
):
    length, width = x0_ref.shape
    first, second = pl.ds(0, length), pl.ds(length, length)
    loads = []
    for a, b in (
        (x0_ref, x_s.at[first]), (x1_ref, x_s.at[second]), (dv0_ref, dv_s.at[first]),
        (dv1_ref, dv_s.at[second]), (dq0_ref, dq_s.at[first]), (dq1_ref, dq_s.at[second]),
        (ctx0_ref, ctx_s.at[:, first]), (ctx1_ref, ctx_s.at[:, second]), (attn_ref, attn_s),
        (dk0_ref, dk_s.at[first]), (dk1_ref, dk_s.at[second]),
    ):
        loads.append(pltpu.make_async_copy(a, b, in_sems.at[len(loads)]))
        loads[-1].start()
    mine = place_ref[0] == 0
    x = x_s[...]
    step = 256
    copies = []

    def place(part, columns, low, high):
        for n, kept in enumerate((False, True)):
            spot = pl.ds((n * 2 + part) * width, width)
            out_s[spot, columns] = jnp.where(mine == kept, low, high).astype(LOW)

    def flush(part):
        for n, ref in enumerate(((send0_ref, send1_ref)[part], (keep0_ref, keep1_ref)[part])):
            spot = pl.ds((n * 2 + part) * width, width)
            copies.append(
                pltpu.make_async_copy(out_s.at[spot, :], ref, out_sems.at[len(copies)])
            )
            copies[-1].start()

    for load in loads[:6]:
        load.wait()
    x = x_s[...]
    for start in range(0, width, step):
        columns = pl.ds(start, step)
        place(0, columns, tn(x, dq_s[:, columns]) * SCORE_SCALE, tn(x, dv_s[:, columns]))
    flush(0)
    for load in loads[6:]:
        load.wait()
    for start in range(0, width, step):
        columns = pl.ds(start, step)
        place(1, columns, tn(x, dk_s[:, columns]), nn(ctx_s[...], attn_s[:, columns]))
    flush(1)
    for copy in copies:
        copy.wait()


def square_grads(place, xs, dqs, dks, dvs, ctxs, attn, *earlier):
    length, width = xs[0].shape
    rows = length * len(xs)
    tokens = pltpu.VMEM((rows, width), LOW)
    out = jax.ShapeDtypeStruct((width, width), LOW)
    return pl.pallas_call(
        ignoring(square_kernel, 12, len(earlier)),
        out_shape=(out,) * 4,
        in_specs=[IN_SMEM] + [ANY] * (11 + len(earlier)),
        out_specs=(ANY,) * 4,
        scratch_shapes=[
            tokens, tokens, tokens, tokens, pltpu.VMEM((width, rows), LOW), tokens,
            pltpu.VMEM((4 * width, width), LOW),
            pltpu.SemaphoreType.DMA((11,)),
            pltpu.SemaphoreType.DMA((4,)),
        ],
        compiler_params=pltpu.CompilerParams(vmem_limit_bytes=VMEM_LIMIT),
        cost_estimate=cost(),
        name="square_grads",
    )(place, *xs, *dqs, *dks, *dvs, *ctxs, attn, *earlier)


def pick_kernel(place_ref, value_ref, out_ref):
    out_ref[...] = value_ref[...]


def pick(value, place, rows, *earlier):
    shape = (rows,) + value.shape[1:]
    return pl.pallas_call(
        ignoring(pick_kernel, 2, len(earlier)),
        out_shape=jax.ShapeDtypeStruct(shape, value.dtype),
        grid_spec=pltpu.PrefetchScalarGridSpec(
            num_scalar_prefetch=1,
            grid=(1,),
            in_specs=[pl.BlockSpec(shape, lambda i, p: (p[0], 0, 0))] + [ANY] * len(earlier),
            out_specs=pl.BlockSpec(shape, lambda i, p: (0, 0, 0)),
        ),
        cost_estimate=cost(),
        name="pick",
    )(place.astype(jnp.int32).reshape(1), value, *earlier)


def other_pieces(value, slot, slots, *earlier):
    count = lax.axis_size("seq")
    me = lax.axis_index("seq")
    found = []
    for shift in range(1, count):
        place = (me + shift) % count * slots + slot
        if value.ndim == 2:
            block = lax.dynamic_index_in_dim(value, place, 0, keepdims=False)
        else:
            block = pick(value, place, 1, *earlier)[0]
        pairs = [(source, (source + shift) % count) for source in range(count)]
        found.append(lax.ppermute(block, "seq", pairs))
    return found


def send_back(parts, shifts=None):
    count = lax.axis_size("seq")
    found = []
    for shift in range(1, count):
        pairs = [(source, (source + shift) % count) for source in range(count)]
        found.append(lax.ppermute(parts[shift - 1], "seq", pairs))
    return found


def join_kernel(me_ref, *refs, slots, count):
    out_ref = refs[-1]
    index = pl.program_id(0)
    shift = lax.rem(index // slots - me_ref[0] + count, count)
    for n in range(count):
        for slot in range(slots):

            @pl.when((shift == n) & (lax.rem(index, slots) == slot))
            def _(n=n, slot=slot):
                value = refs[n][slot] if len(refs) == count + 1 else refs[n * slots + slot][...]
                out_ref[0] = value.astype(out_ref.dtype)


def join(me, arrays, slots, count, *earlier):
    piece, width = arrays[0].shape[-2:]
    return pl.pallas_call(
        ignoring(
            functools.partial(join_kernel, slots=slots, count=count), 1 + len(arrays), len(earlier)
        ),
        out_shape=jax.ShapeDtypeStruct((slots * count, piece, width), arrays[0].dtype),
        grid_spec=pltpu.PrefetchScalarGridSpec(
            num_scalar_prefetch=1,
            grid=(slots * count,),
            in_specs=[whole(array.shape) for array in arrays] + [ANY] * len(earlier),
            out_specs=pl.BlockSpec((1, piece, width), lambda i, p: (i, 0, 0)),
        ),
        compiler_params=pltpu.CompilerParams(vmem_limit_bytes=SMALL_LIMIT),
        cost_estimate=cost(),
        name="join",
    )(me, *arrays, *earlier)


def collect_kernel(sums0_ref, sums1_ref, one_ref, two_ref, up_ref, *refs):
    stat_refs, mark_ref, out_ref = refs[:-2], refs[-2], refs[-1]
    width = out_ref.shape[1]
    out_ref[0:2, :] = sums0_ref[0:2, :] + sums1_ref[0:2, :]
    out_ref[2:5, :] = one_ref[0:3, :]
    out_ref[5:8, :] = two_ref[0:3, :]
    lane = lax.broadcasted_iota(jnp.int32, (1, width), 1)
    known = (mark_ref[...] >= 0).astype(WIDE)
    tokens = jnp.sum(jnp.sum(known, axis=1, keepdims=True), axis=0, keepdims=True)
    fed = stat_refs[2]
    stats = (
        stat_refs[0][0:1, 0:1] + stat_refs[1][0:1, 0:1],
        stat_refs[0][1:2, 0:1] + stat_refs[1][1:2, 0:1],
        fed[0:1, 0:1], fed[1:2, 0:1], tokens,
    )
    row = jnp.zeros((1, width), WIDE)
    for n, stat in enumerate(stats):
        row = jnp.where(lane == n, stat, row)
    out_ref[8:9, :] = row
    parts = up_ref.shape[1] // width
    for n in range(parts):
        out_ref[9 + n : 10 + n, :] = row_total(up_ref[:, n * width : (n + 1) * width])
    left = out_ref.shape[0] - 9 - parts
    out_ref[9 + parts :, :] = jnp.zeros((left, width), WIDE)


def collect(sums, sums_one, sums_two, up_sums, stats, marks, *earlier):
    width = sums_one.shape[1]
    rows = 9 + up_sums.shape[1] // width
    args = (*sums, sums_one, sums_two, up_sums, *stats, marks)
    return pl.pallas_call(
        ignoring(collect_kernel, len(args), len(earlier)),
        out_shape=jax.ShapeDtypeStruct((rows + (-rows) % 8, width), WIDE),
        in_specs=[IN_VMEM] * len(args) + [ANY] * len(earlier),
        out_specs=IN_VMEM,
        compiler_params=pltpu.CompilerParams(vmem_limit_bytes=VMEM_LIMIT),
        cost_estimate=cost(),
        name="collect",
    )(*args, *earlier)


def swap(value, axis, bit):
    count = lax.axis_size(axis)
    return lax.ppermute(value, axis, [(source, source ^ bit) for source in range(count)])


def bit_of(axis, bit):
    return (lax.axis_index(axis) // bit) % 2


CORE = ("dp", 1)
HALVINGS = 5
STEP_ROWS = 16


def chip_axes():
    dp, seq = lax.axis_size("dp"), lax.axis_size("seq")
    along_dp = [("dp", 2**i) for i in range(1, dp.bit_length() - 1)]
    along_seq = [("seq", 2**i) for i in range(seq.bit_length() - 1)]
    return along_dp[0], along_seq[0], along_dp[1], along_dp[2:] + along_seq[1:]


class Chain:
    def __init__(self, bits):
        self.last = ()
        self.bits = bits

    def run(self, function, *args):
        out = function(*args, *self.last)
        arrays = out if isinstance(out, (tuple, list)) else (out,)
        self.last = (min(arrays, key=lambda array: array.size),)
        return out

    def round(self, *tasks):
        outs = list(self.run(round_call, self.bits, [task[:-1] for task in tasks]))
        for task in tasks:
            count = 2 if task[0] == "halve" else 1
            task[-1](*[outs.pop(0) for _ in range(count)])


def add_rows(first, first_start, second, second_start, out, rows):
    def step(index, carried):
        spots = [
            pl.ds(pl.multiple_of(start + index * STEP_ROWS, STEP_ROWS), STEP_ROWS)
            for start in (first_start, second_start, 0)
        ]
        both = first[spots[0], :].astype(WIDE) + second[spots[1], :].astype(WIDE)
        out[spots[2], :] = both.astype(LOW)
        return carried

    lax.fori_loop(0, rows // STEP_ROWS, step, 0)


def round_kernel(bits_ref, *refs, plan, inputs):
    outs = list(refs[inputs:])
    for kind, places, meta in plan:
        first, second = refs[places[0]], refs[places[1]]
        if kind == "halve":
            rows, offset, which = meta
            mine = bits_ref[which]
            for bit in (1 - mine, mine):
                start = offset + bit * rows
                add_rows(first, start, second, start, outs.pop(0), rows)
        elif kind == "add":
            add_rows(first, meta, second, 0, outs.pop(0), second.shape[0])
        elif kind == "merge":
            rows = first.shape[0]
            out = outs.pop(0)
            out[:rows, :] = first[...]
            out[rows:, :] = second[...]
        else:
            outs.pop(0)[...] = first[...]


def round_call(bits, tasks, *earlier):
    arrays, plan, shapes = [], [], []
    for kind, pair, meta in tasks:
        places = []
        for array in pair:
            known = [n for n, other in enumerate(arrays) if other is array]
            if not known:
                arrays.append(array)
            places.append(known[0] if known else len(arrays) - 1)
        plan.append((kind, places, meta))
        rows, width = pair[0].shape
        if kind == "halve":
            shapes += [jax.ShapeDtypeStruct((meta[0], width), LOW)] * 2
        elif kind == "merge":
            shapes.append(jax.ShapeDtypeStruct((2 * rows, width), LOW))
        elif kind == "add":
            shapes.append(jax.ShapeDtypeStruct(pair[1].shape, LOW))
        else:
            shapes.append(jax.ShapeDtypeStruct((rows, width), pair[0].dtype))
    return pl.pallas_call(
        ignoring(
            functools.partial(round_kernel, plan=plan, inputs=len(arrays)),
            1 + len(arrays),
            len(earlier),
        ),
        out_shape=tuple(shapes),
        in_specs=[IN_SMEM] + [IN_VMEM] * len(arrays) + [ANY] * len(earlier),
        out_specs=(IN_VMEM,) * len(shapes),
        compiler_params=pltpu.CompilerParams(vmem_limit_bytes=SMALL_LIMIT),
        cost_estimate=cost(),
        name="round",
    )(bits, *arrays, *earlier)


class Reduction:
    def __init__(self, kept, got, order, names, back):
        self.order, self.names, self.back = order, names, back
        self.first, self.second = kept, got
        self.count, self.offset = kept.shape[0], 0
        self.step = 1

    def send(self):
        axis = self.order[self.step]
        rows, offset = self.count // 2, self.offset

        def found(sent, kept):
            self.first, self.second = kept, swap(sent, *axis)
            self.count, self.offset = rows, 0
            self.step += 1

        meta = (rows, offset, self.names.index(axis))
        return "halve", (self.first, self.second), meta, found

    def share(self):
        def found(share):
            self.have = share
            if self.step < len(self.order):
                self.first, self.second = share, swap(share, *self.order[self.step])
                self.step += 1
            else:
                self.step = len(self.back) - 1
                self.got = swap(share, *self.back[self.step])

        return "add", (self.first, self.second), 0, found

    def more_shares(self):
        return len(self.order) - HALVINGS

    def gather(self):
        def found(merged):
            self.step -= 1
            self.have, self.got = merged, swap(merged, *self.back[self.step])

        return "merge", (self.have, self.got), None, found

    def copy(self):
        def found(got):
            self.got = got

        return "copy", (self.got, self.got), None, found

    def halves(self):
        return [self.have, self.got, swap(self.have, *CORE), swap(self.got, *CORE)]

    def moves(self):
        chips = [axis for axis in self.order[:HALVINGS] if axis != CORE]
        return [len(chips) - 1 - chips.index(axis) for axis in self.back]

    def place(self):
        place = 0
        for axis in self.back:
            place = place * 2 + bit_of(*axis)
        return place.astype(jnp.int32)


def attach_kernel(small_ref, part_ref, out_ref):
    rows = small_ref.shape[0]
    out_ref[:rows, :] = small_ref[...].astype(LOW)
    out_ref[rows:, :] = part_ref[...]


def attach(small, part, *earlier):
    rows = small.shape[0] + part.shape[0]
    return pl.pallas_call(
        ignoring(attach_kernel, 2, len(earlier)),
        out_shape=jax.ShapeDtypeStruct((rows, part.shape[1]), LOW),
        in_specs=[IN_VMEM] * 2 + [ANY] * len(earlier),
        out_specs=IN_VMEM,
        compiler_params=pltpu.CompilerParams(vmem_limit_bytes=SMALL_LIMIT),
        cost_estimate=cost(),
        name="attach",
    )(small, part, *earlier)


def detach_kernel(value_ref, small_ref, out_ref):
    count, rows, _ = value_ref.shape
    few = small_ref.shape[0]
    each = rows - few
    total_here = jnp.zeros(small_ref.shape, WIDE)
    for n in range(count):
        total_here = total_here + value_ref[n, :few, :].astype(WIDE)
        out_ref[n * each : (n + 1) * each, :] = value_ref[n, few:, :].astype(WIDE)

    @pl.when(pl.program_id(0) == 0)
    def _():
        small_ref[...] = jnp.zeros_like(small_ref)

    small_ref[...] += total_here


def detach(value, few, *earlier):
    count, rows, width = value.shape
    steps = 8
    return pl.pallas_call(
        ignoring(detach_kernel, 1, len(earlier)),
        out_shape=(
            jax.ShapeDtypeStruct((few, width), WIDE),
            jax.ShapeDtypeStruct((count * (rows - few), width), WIDE),
        ),
        grid=(steps,),
        in_specs=[pl.BlockSpec((count // steps, rows, width), lambda t: (t, 0, 0))]
        + [ANY] * len(earlier),
        out_specs=(
            whole((few, width)),
            pl.BlockSpec((count // steps * (rows - few), width), lambda t: (t, 0)),
        ),
        compiler_params=pltpu.CompilerParams(
            vmem_limit_bytes=SMALL_LIMIT, dimension_semantics=("arbitrary",)
        ),
        cost_estimate=cost(),
        name="detach",
    )(value, *earlier)


def spot_of_block(index, moves):
    spot = 0
    for move in moves:
        spot = spot * 2 + ((index >> move) & 1)
    return spot


def turn_kernel(place_ref, own, other, *refs, moves):
    out_ref = refs[-1]
    blocks = 1 << (HALVINGS - 2)
    block = own.shape[0] // blocks
    count = out_ref.shape[1] // block
    step = pl.program_id(0)
    mine = place_ref[0] == step // 2
    start = (place_ref[2] * 2 + lax.rem(step, 2)) * count
    found = []
    for j in range(count):
        spot = spot_of_block(start + j, moves) ^ place_ref[1]
        at = pl.ds(pl.multiple_of(lax.rem(spot, blocks) * block, block), block)
        found.append(jnp.where(mine, own[at, :], other[at, :]).astype(WIDE))
    out_ref[...] = jnp.concatenate(found, axis=0).T


def turn(place, own, other, moves, into, *earlier):
    rows, width = own.shape
    into = () if into is None else (into,)
    return pl.pallas_call(
        ignoring(functools.partial(turn_kernel, moves=moves), 3 + len(into), len(earlier)),
        out_shape=jax.ShapeDtypeStruct((width, 4 * rows), WIDE),
        grid_spec=pltpu.PrefetchScalarGridSpec(
            num_scalar_prefetch=1,
            grid=(4,),
            in_specs=[whole(own.shape)] * 2 + [ANY] * (len(into) + len(earlier)),
            out_specs=pl.BlockSpec((width, rows // 2), lambda t, p: (0, t // 2 * 4 + p[2] * 2 + lax.rem(t, 2))),
        ),
        input_output_aliases={3: 0} if into else {},
        compiler_params=pltpu.CompilerParams(vmem_limit_bytes=SMALL_LIMIT),
        cost_estimate=cost(6 * 10**9),
        name="turn",
    )(place, own, other, *into, *earlier)


def gate_kernel(*refs):
    pass


def gate(values, *earlier):
    count = len(values)
    return pl.pallas_call(
        gate_kernel,
        out_shape=tuple(jax.ShapeDtypeStruct(value.shape, value.dtype) for value in values),
        in_specs=[ANY] * (count + len(earlier)),
        out_specs=(ANY,) * count,
        input_output_aliases={n: n for n in range(count)},
        compiler_params=pltpu.CompilerParams(vmem_limit_bytes=SMALL_LIMIT),
        cost_estimate=cost(),
        name="gate",
    )(*values, *earlier)


def finish_kernel(
    place_ref, near_own, far_own, near_other, far_other, low_ref, high_ref, *, moves
):
    blocks = 1 << (HALVINGS - 2)
    block = near_own.shape[0] // blocks
    step = pl.program_id(0)
    rows = low_ref.shape[0]
    first = place_ref[0] == 0
    for j in range(rows // block):
        spot = spot_of_block(step * (rows // block) + j, moves) ^ place_ref[1]
        at = pl.ds(pl.multiple_of(lax.rem(spot, blocks) * block, block), block)
        here = pl.ds(j * block, block)
        own = jnp.where(spot < blocks, near_own[at, :], far_own[at, :]).astype(WIDE)
        other = jnp.where(spot < blocks, near_other[at, :], far_other[at, :]).astype(WIDE)
        low_ref[here, :] = jnp.where(first, own, other)
        high_ref[here, :] = jnp.where(first, other, own)


def finish(place, arrays, moves, *earlier):
    rows, width = arrays[0].shape
    shape = jax.ShapeDtypeStruct((2 * rows, width), WIDE)
    tile = rows // 2
    return pl.pallas_call(
        ignoring(functools.partial(finish_kernel, moves=moves), 5, len(earlier)),
        out_shape=(shape, shape),
        grid_spec=pltpu.PrefetchScalarGridSpec(
            num_scalar_prefetch=1,
            grid=(4,),
            in_specs=[whole(array.shape) for array in arrays] + [ANY] * len(earlier),
            out_specs=(
                pl.BlockSpec((tile, width), lambda t, p: (t, 0)),
                pl.BlockSpec((tile, width), lambda t, p: (t, 0)),
            ),
        ),
        compiler_params=pltpu.CompilerParams(vmem_limit_bytes=SMALL_LIMIT),
        cost_estimate=cost(6 * 10**9),
        name="finish",
    )(place, *arrays, *earlier)


def on_device(
    inputs, cotangent, w_query, b_query, w_key, w_value, b_value, w_out, b_out, gain_one,
    shift_one, w_up, b_up, w_down, b_down, gain_two, shift_two, live_counts, valid_mask, segments,
):
    seqs, piece, width = inputs.shape
    count = lax.axis_size("seq")
    me = lax.axis_index("seq").astype(jnp.int32)
    slots = seqs // count
    length = piece * count
    x, y, z, rest = chip_axes()
    names = [CORE, x, y, z] + rest
    bits = jnp.stack([bit_of(*axis).astype(jnp.int32) for axis in names])
    core = bits[0]
    chain = Chain(bits)
    chain.last = (segments,)
    base = (me * slots).reshape(1)

    x_got = []
    for slot in range(slots):
        x_got.append(other_pieces(inputs, slot, slots, *(x_got[-1][-1:] if x_got else ())))
    vectors = jnp.concatenate(
        [v.reshape(1, -1) for v in (
            b_query, b_value, b_out, gain_one, shift_one, b_down, gain_two, shift_two
        )]
    ).astype(WIDE)
    bias_up = b_up.astype(WIDE).reshape(1, -1)
    live = (jnp.arange(seqs) < live_counts[0]).astype(jnp.int32)
    code = segments * 2 + valid_mask * live[:, None]
    codes = jnp.stack(
        [
            jnp.concatenate(
                [lax.dynamic_index_in_dim(code, base[0] + slot, 0, keepdims=False)]
                + other_pieces(code, slot, slots)
            )
            for slot in range(slots)
        ]
    )
    segs = codes // 2
    weight = codes % 2
    marks = jnp.where(weight > 0, segs, -1)

    forward = []
    for slot in range(slots):
        forward.append(
            chain.run(
                attend, jnp.stack([base[0], jnp.int32(slot)]), inputs, x_got[slot], segs, marks, vectors, w_query, w_key,
                w_value, w_out,
            )
        )
    cot_got = []
    for shift in range(1, count):
        block = pick(cotangent, (me + shift) % count, slots, x_got[-1][-1], forward[0][9])
        pairs = [(source, (source + shift) % count) for source in range(count)]
        cot_got.append(lax.ppermute(block, "seq", pairs))
    slope, mid_low, result_own, result_sent, grad_h2, grad_feed, down, sums_two, stat_two = (
        chain.run(
            feed_forward, base, [each[6] for each in forward], cotangent, cot_got, marks, w_up,
            bias_up, w_down, vectors,
        )
    )
    everywhere = ("dp", "seq")
    down = lax.psum_scatter(down, everywhere, scatter_dimension=0, tiled=True)
    result_got = send_back([result_sent[n] for n in range(count - 1)])
    grad_h1, grad_attn, grad_ctx, up_sent, up_kept, up_sums, sums_one = chain.run(
        feed_back, bits[0:1], grad_feed, grad_h2, slope,
        [each[7] for each in forward], [each[8] for each in forward], mid_low, w_up, w_down,
        w_out, vectors,
    )
    (up_sent,) = chain.run(gate, (up_sent,), *result_got)
    last = rest[0]
    up = Reduction(
        up_kept, swap(up_sent, *CORE), [CORE, y, z, x] + rest, names, [y, x, z, last]
    )
    backward, grad_got = [], []
    for slot in range(slots):
        if slot == 1:
            chain.round(up.send())
        q, k, v, _, ctx, lse = forward[slot][:6]
        backward.append(
            chain.run(
                attend_back, piece, jnp.full((1,), slot, jnp.int32), q, k, v, ctx, grad_ctx, lse,
                segs, marks, grad_h1, w_query, w_key, w_value,
            )
        )
        sent = backward[-1][4]
        grad_got.append(
            send_back([sent[n * piece : (n + 1) * piece] for n in range(count - 1)])
        )
    small = chain.run(
        collect, [each[5] for each in backward], sums_one, sums_two, up_sums,
        [each[9] for each in forward] + [stat_two], marks,
    )
    square_sent0, square_sent1, square_kept0, square_kept1 = chain.run(
        square_grads, bits[0:1], [each[3] for each in forward],
        *([each[i] for each in backward] for i in range(3)), [each[4] for each in forward],
        grad_attn,
    )
    squares = [
        Reduction(square_kept0, swap(square_sent0, *CORE), [CORE, x, y, z] + rest, names, [x, z, y, last]),
        Reduction(square_kept1, swap(square_sent1, *CORE), [CORE, y, z, x] + rest, names, [z, x, y, last]),
    ]

    def each_square(step):
        return [step(square) for square in squares]

    chain.round(up.send())
    chain.round(*each_square(Reduction.send))
    chain.round(*each_square(Reduction.send), up.send())
    few = small.shape[0]
    down = chain.run(attach, small, down)
    down = lax.all_gather(down, everywhere, axis=0, tiled=False)
    chain.round(*each_square(Reduction.send), up.send())
    for _ in range(up.more_shares()):
        chain.round(up.share())
    chain.round(*each_square(Reduction.send), up.share())
    result_out = chain.run(join, me.reshape(1), [result_own] + result_got, slots, count)
    for _ in range(up.more_shares()):
        chain.round(*each_square(Reduction.share))
    chain.round(*each_square(Reduction.share), up.gather())
    grad_arrays = [each[3] for each in backward]
    for n in range(count - 1):
        grad_arrays += [got[n] for got in grad_got]
    grad_out = chain.run(join, me.reshape(1), grad_arrays, slots, count)
    chain.round(*each_square(Reduction.gather), up.gather())
    chain.round(*each_square(Reduction.gather))
    chain.round(*each_square(Reduction.gather), up.gather())
    small, grad_w_down = chain.run(detach, down, few)
    finished = [
        chain.run(finish, jnp.stack([core, square.place()]), square.halves(), square.moves())
        for square in squares
    ]
    up_place = [core, up.place()]
    up_near = up.have, swap(up.have, *CORE)
    grad_w_up = chain.run(
        turn, jnp.stack(up_place + [bits[2]]), *up_near, up.moves(), None
    )
    far = up.got
    grad_w_up = turn(
        jnp.stack(up_place + [1 - bits[2]]), far, swap(far, *CORE), up.moves(), grad_w_up
    )
    rms_values = jnp.sqrt(small[8, :4] / (width * small[8, 4]))
    hidden = w_up.shape[1]
    return (
        result_out,
        grad_out,
        finished[0][0],
        small[0],
        finished[1][0],
        finished[0][1],
        small[1],
        finished[1][1],
        small[4],
        small[2],
        small[3],
        grad_w_up,
        small[9 : 9 + hidden // width].reshape(-1),
        grad_w_down,
        small[7],
        small[5],
        small[6],
        rms_values,
    )


def solution(mesh):
    split = P("dp", "seq", None)
    pair = P("dp", "seq")
    return jax.shard_map(
        on_device,
        mesh=mesh,
        in_specs=(split, split) + (P(),) * 15 + (P("dp"), pair, pair),
        out_specs=(split, split) + (P(),) * 16,
        check_vma=False,
    )
```

```python
import functools

import jax
import jax.numpy as jnp
from jax import lax
from jax.experimental import pallas as pl
from jax.experimental.pallas import tpu as pltpu
from jax.sharding import PartitionSpec as P

HEAD_DIM = 64
EPSILON = 1e-05
NEGATIVE = -1e30
SCORE_SCALE = 0.125
LOW = jnp.bfloat16
WIDE = jnp.float32
VMEM_LIMIT = 63 * 1024 * 1024
SMALL_LIMIT = 20 * 1024 * 1024
HIDDEN_STEP = 768
TILE = 512
ROWS = 32
ROWS_NORM = 16
ANY = pl.BlockSpec(memory_space=pltpu.HBM)
IN_VMEM = pl.BlockSpec(memory_space=pltpu.VMEM)
IN_SMEM = pl.BlockSpec(memory_space=pltpu.SMEM)

ERF_P = 0.3275911
ERF_C = (0.254829592, -0.284496736, 1.421413741, -1.453152027, 1.061405429)
ROOT_HALF = 0.7071067811865476
DENSITY = 0.3989422804014327
EXP2_SCALE = -0.7213475204444817


def nn(left, right):
    return jnp.dot(left, right, preferred_element_type=WIDE)


def nt(left, right):
    return lax.dot_general(
        left, right, (((1,), (1,)), ((), ())), preferred_element_type=WIDE
    )


def tn(left, right):
    return lax.dot_general(
        left, right, (((0,), (0,)), ((), ())), preferred_element_type=WIDE
    )


def gelu_pair(hidden):
    size = jnp.abs(hidden)
    falling = jnp.exp2(hidden * hidden * EXP2_SCALE)
    t = pl.reciprocal(1.0 + (ERF_P * ROOT_HALF) * size, approx=True)
    c1, c2, c3, c4, c5 = (0.5 * c for c in ERF_C)
    shape = ((((c5 * t + c4) * t + c3) * t + c2) * t + c1) * t
    gone = falling * (shape - DENSITY * size)
    slope = jnp.where(hidden >= 0.0, 1.0 - gone, gone)
    return jnp.maximum(hidden, 0.0) - size * (shape * falling), slope


def lane_half(half):
    lane = lax.broadcasted_iota(jnp.int32, (1, 2 * HEAD_DIM), 1)
    inside = (lane < HEAD_DIM) if half == 0 else (lane >= HEAD_DIM)
    return inside.astype(WIDE).astype(LOW)


def fill_bias(bias_ref, seg_row, mark_col):
    length = bias_ref.shape[0]
    key_place = lax.broadcasted_iota(jnp.int32, (length, length), 0)
    query_place = lax.broadcasted_iota(jnp.int32, (length, length), 1)
    visible = (mark_col == seg_row) | (key_place == query_place)
    bias_ref[...] = jnp.where(visible, 0.0, NEGATIVE)


def total(rows_weight, values):
    per_row = jnp.sum(values * values, axis=1, keepdims=True) * rows_weight
    return jnp.sum(per_row, axis=0, keepdims=True)


def column(row):
    return jnp.broadcast_to(row.astype(WIDE), (8, row.shape[1])).T[:, 0:1]


VECTORS = ("b_query", "b_value", "b_out", "gain_one", "shift_one", "b_down", "gain_two", "shift_two")


def vector(ref, name):
    place = VECTORS.index(name)
    return ref[place : place + 1, :]


def attend_kernel(
    place_ref, seg_ref, mark_ref, vectors_ref, wq_ref, wk_ref, wv_ref, wo_ref, inputs_ref, *refs,
    pieces,
):
    (
        q_ref, k_ref, v_ref, x_ref, ctx_ref, lse_ref, mid_ref, norm_ref, rstd_ref, stat_ref,
        wq_s, wk_s, wv_s, wo_s, q_s, k_s, v_s, x_s, bias_s, score_s, chance_s, weight_s, in_sems,
        out_sems,
    ) = refs[pieces - 1 :]
    length, model = x_s.shape
    piece = length // pieces
    loads = [
        pltpu.make_async_copy(a, b, in_sems.at[n])
        for n, (a, b) in enumerate(
            ((wk_ref, wk_s), (wq_ref, wq_s), (wv_ref, wv_s), (wo_ref, wo_s))
        )
    ]
    tokens_in = [
        pltpu.make_async_copy(a, x_s.at[pl.ds(n * piece, piece), :], in_sems.at[4 + n])
        for n, a in enumerate((inputs_ref.at[place_ref[0] + place_ref[1]],) + refs[: pieces - 1])
    ]
    for load in tokens_in + loads:
        load.start()
    stores = [
        pltpu.make_async_copy(a, b, out_sems.at[n])
        for n, (a, b) in enumerate(((k_s, k_ref), (q_s, q_ref), (v_s, v_ref), (x_s, x_ref)))
    ]
    own = pl.ds(place_ref[1], 1)
    mark_col = column(mark_ref[own, :])
    weight_s[...] = (mark_col >= 0).astype(WIDE)
    fill_bias(bias_s, seg_ref[own, :].astype(WIDE), mark_col)
    heads = model // HEAD_DIM
    width = 2 * HEAD_DIM
    for load in tokens_in:
        load.wait()
    stores[3].start()
    loads[0].wait()
    k_s[...] = nn(x_s[...], wk_s[...]).astype(LOW)
    stores[0].start()
    loads[1].wait()
    q_s[...] = ((nn(x_s[...], wq_s[...]) + vector(vectors_ref, "b_query")) * SCORE_SCALE).astype(LOW)
    stores[1].start()
    loads[2].wait()
    v_s[...] = (nn(x_s[...], wv_s[...]) + vector(vectors_ref, "b_value")).astype(LOW)
    stores[2].start()

    def lanes(head):
        return pl.ds(head // 2 * width, width)

    def scores(head):
        keys = k_s[:, lanes(head)] * lane_half(head % 2)
        score_s[head % 2] = nt(keys, q_s[:, lanes(head)])

    def soften(head):
        here, chance = score_s.at[head % 2], chance_s.at[head % 2]
        top = jnp.full((8, length), NEGATIVE, WIDE)
        for row in range(0, length, ROWS):
            block = here[row : row + ROWS, :] + bias_s[row : row + ROWS, :]
            here[row : row + ROWS, :] = block
            top = jnp.maximum(top, jnp.max(block.reshape(-1, 8, length), axis=0))
        top = jnp.max(top, axis=0, keepdims=True)
        amount = jnp.zeros((8, length), WIDE)
        for row in range(0, length, ROWS):
            block = jnp.exp(here[row : row + ROWS, :] - top)
            chance[row : row + ROWS, :] = block.astype(LOW)
            amount = amount + jnp.sum(block.reshape(-1, 8, length), axis=0)
        amount = jnp.sum(amount, axis=0, keepdims=True)
        lse_ref[head : head + 1, :] = top + jnp.log(amount)
        return 1.0 / amount

    def combine(head, share, turned):
        part = turned[head % 2 * HEAD_DIM : (head % 2 + 1) * HEAD_DIM]
        summed = nn(part, chance_s[head % 2]) * share
        ctx_ref[head * HEAD_DIM : (head + 1) * HEAD_DIM, :] = summed.astype(LOW)

    scores(0)
    waiting = None
    for head in range(heads):
        share = soften(head)
        if head % 2 == 0:
            turned = v_s[:, lanes(head)].T
        if head + 1 < heads:
            scores(head + 1)
        if waiting is not None:
            combine(*waiting)
        waiting = (head, share, turned)
    combine(*waiting)
    loads[3].wait()
    attention_all = tn(ctx_ref[...], wo_s[...])
    bias, gain, shift = (vector(vectors_ref, n) for n in ("b_out", "gain_one", "shift_one"))
    stats = [jnp.zeros((1, 1), WIDE) for _ in range(2)]
    for row in range(0, length, ROWS_NORM):
        at = pl.ds(row, ROWS_NORM)
        attention = attention_all[row : row + ROWS_NORM] + bias
        rows = x_s[at, :].astype(WIDE)
        total_in = rows + attention
        center = total_in - jnp.mean(total_in, axis=1, keepdims=True)
        rstd = lax.rsqrt(jnp.mean(center * center, axis=1, keepdims=True) + EPSILON)
        normal = center * rstd
        mid_ref[at, :] = normal * gain + shift
        norm_ref[at, :] = normal.astype(LOW)
        rstd_ref[at, :] = rstd
        row_weight = weight_s[at, :]
        stats[0] = stats[0] + total(row_weight, rows)
        stats[1] = stats[1] + total(row_weight, attention)
    stat_ref[...] = jnp.concatenate(
        [jnp.broadcast_to(stat, (1, 128)) for stat in stats] + [jnp.zeros((6, 128), WIDE)], axis=0
    )
    for store in stores:
        store.wait()


def cost(flops=10**8):
    return pl.CostEstimate(flops=flops, transcendentals=0, bytes_accessed=0)


def ignoring(kernel, inputs, extra):
    def wrapped(*refs):
        return kernel(*refs[:inputs], *refs[inputs + extra :])

    return wrapped


def whole(shape):
    return pl.BlockSpec(shape, lambda *_: (0,) * len(shape), pipeline_mode=pl.Buffered(1))


def attend(place, inputs, got, segs, marks, vectors, wq, wk, wv, wo, *earlier):
    pieces = len(got) + 1
    length, width = inputs.shape[1] * pieces, inputs.shape[2]
    heads = width // HEAD_DIM
    lse_rows = heads + (-heads) % 8
    tokens_out = jax.ShapeDtypeStruct((length, width), LOW)
    shapes = (
        tokens_out, tokens_out, tokens_out, tokens_out,
        jax.ShapeDtypeStruct((width, length), LOW),
        jax.ShapeDtypeStruct((lse_rows, length), WIDE),
        jax.ShapeDtypeStruct((length, width), WIDE),
        tokens_out,
        jax.ShapeDtypeStruct((length, 1), WIDE),
        jax.ShapeDtypeStruct((8, 128), WIDE),
    )
    args = (place, segs, marks, vectors, wq, wk, wv, wo, inputs, *got)
    weight = pltpu.VMEM((width, width), LOW)
    tokens = pltpu.VMEM((length, width), LOW)
    return pl.pallas_call(
        ignoring(
            functools.partial(attend_kernel, pieces=pieces), len(args), len(earlier)
        ),
        out_shape=shapes,
        in_specs=[IN_SMEM] + [IN_VMEM] * 3 + [ANY] * (4 + pieces + len(earlier)),
        out_specs=(ANY,) * 4 + (IN_VMEM,) * 6,
        scratch_shapes=[weight] * 4 + [tokens] * 4 + [
            pltpu.VMEM((length, length), WIDE),
            pltpu.VMEM((2, length, length), WIDE),
            pltpu.VMEM((2, length, length), LOW),
            pltpu.VMEM((length, 1), WIDE),
            pltpu.SemaphoreType.DMA((4 + pieces,)),
            pltpu.SemaphoreType.DMA((4,)),
        ],
        compiler_params=pltpu.CompilerParams(vmem_limit_bytes=VMEM_LIMIT),
        cost_estimate=cost(),
        name="attend",
    )(*args, *earlier)


def norm_back(grad, normal, rstd, gain):
    pulled = grad * gain
    return rstd * (
        pulled
        - jnp.mean(pulled, axis=1, keepdims=True)
        - normal * jnp.mean(pulled * normal, axis=1, keepdims=True)
    )


def row_total(values):
    return jnp.sum(values, axis=0, keepdims=True)


def feed_kernel(
    place_ref, mid0_ref, mid1_ref, cot_ref, mark_ref, bu_ref, vectors_ref, wu_ref, wd_ref, *refs,
    pieces,
):
    (
    slope_ref, low_ref, own_ref, sent_ref, grad_ref, grad_low_ref, down_ref, sums_ref, stat_ref,
    mid_s, cot_s, wu_s, wd_s, act_s, slope_s, low_s, result_s, grad_s, grad_low_s, out_s,
    feed_s, weight_s, sum_s, in_sems, up_sems, down_sems, tile_sems, out_sems,
    ) = refs[pieces - 1 :]
    length, width = mid0_ref.shape
    rows = cot_s.shape[0]
    piece = length // pieces
    hidden = wu_ref.shape[1]
    half = hidden // 2
    chunks = hidden // HIDDEN_STEP
    tile = TILE
    def own(chunk):
        return pl.ds(chunk * HIDDEN_STEP, HIDDEN_STEP)

    first_in = pltpu.make_async_copy(mid0_ref, mid_s.at[pl.ds(0, length)], in_sems.at[0])
    second_in = pltpu.make_async_copy(mid1_ref, mid_s.at[pl.ds(length, length)], in_sems.at[1])
    cot_in = []
    for slot in range(rows // length):
        own_piece = cot_ref.at[place_ref[0] + slot]
        for part, ref in enumerate([own_piece] + [ref.at[slot] for ref in refs[: pieces - 1]]):
            spot = pl.ds(slot * length + part * piece, piece)
            sem = in_sems.at[2 + len(cot_in)]
            cot_in.append(pltpu.make_async_copy(ref, cot_s.at[spot, :], sem))
    ups = [
        pltpu.make_async_copy(wu_ref.at[:, own(c)], wu_s.at[:, own(c)], up_sems.at[c])
        for c in range(chunks)
    ]
    downs = [
        pltpu.make_async_copy(wd_ref.at[own(c), :], wd_s.at[own(c), :], down_sems.at[c])
        for c in range(chunks)
    ]
    first_in.start()
    for chunk in range(chunks):
        ups[chunk].start()
        downs[chunk].start()
    second_in.start()
    for copy in cot_in:
        copy.start()
    sums_ref[...] = jnp.zeros_like(sums_ref)
    stat_ref[...] = jnp.zeros_like(stat_ref)
    sum_s[...] = jnp.zeros_like(sum_s)
    for slot in range(mark_ref.shape[0]):
        mark_col = column(mark_ref[slot : slot + 1, :])
        weight_s[pl.ds(slot * length, length), :] = (mark_col >= 0).astype(WIDE)

    def tile_copies(index):
        spot = pl.ds(pl.multiple_of(index * tile, tile), tile)
        pairs = (
            (low_s, low_ref), (grad_s, grad_ref), (grad_low_s, grad_low_ref), (slope_s, slope_ref),
        )
        return [
            pltpu.make_async_copy(a.at[spot, :], b.at[spot, :], tile_sems.at[n, index])
            for n, (a, b) in enumerate(pairs)
        ]

    def inside(index, row, count=ROWS):
        return pl.ds(pl.multiple_of(index * tile + row, count), count)

    def work(index, opening):
        spot = pl.ds(pl.multiple_of(index * tile, tile), tile)
        for row in range(0, tile, ROWS):
            low_s[inside(index, row), :] = mid_s[inside(index, row), :].astype(LOW)
        middle_low = low_s[spot, :]

        def up(chunk):
            if opening:
                ups[chunk].wait()
            return nn(middle_low, wu_s[:, own(chunk)])

        def down(chunk, feed):
            if opening:
                downs[chunk].wait()
            more = nn(act_s[spot, own(chunk)], wd_s[own(chunk), :])
            return more if feed is None else feed + more

        before = pl.ds(pl.multiple_of((index - 1) * tile, tile), tile)
        feed = None
        ahead = up(0)
        for chunk in range(chunks):
            bias = bu_ref[:, own(chunk)]
            for row in range(0, tile, ROWS):
                active, slope = gelu_pair(ahead[row : row + ROWS] + bias)
                act_s[inside(index, row), own(chunk)] = active.astype(LOW)
                slope_s[inside(index, row), own(chunk)] = slope.astype(LOW)
            if chunk + 1 < chunks:
                ahead = up(chunk + 1)
            if chunk > 0:
                feed = down(chunk - 1, feed)
            if not opening:
                gather_outer(sum_s, act_s, grad_low_s, before, own(chunk))
        feed_s[...] = down(chunks - 1, feed)

    def norm(index):
        gain, shift, bias = (vector(vectors_ref, n) for n in ("gain_two", "shift_two", "b_down"))
        sums = [jnp.zeros((1, width), WIDE) for _ in range(3)]
        stats = [jnp.zeros((1, 1), WIDE) for _ in range(2)]
        for row in range(0, tile, ROWS_NORM):
            here = inside(index, row, ROWS_NORM)
            feed_here = feed_s[row : row + ROWS_NORM, :] + bias
            total_in = mid_s[here, :] + feed_here
            center = total_in - jnp.mean(total_in, axis=1, keepdims=True)
            rstd = lax.rsqrt(jnp.mean(center * center, axis=1, keepdims=True) + EPSILON)
            normal = center * rstd
            result = normal * gain + shift
            result_s[here, :] = result.astype(LOW)
            weight = weight_s[here, :]
            grad_result = cot_s[here, :].astype(WIDE) * weight
            grad = norm_back(grad_result, normal, rstd, gain)
            grad_s[here, :] = grad
            grad_low = grad.astype(LOW)
            grad_low_s[here, :] = grad_low
            sums[0] = sums[0] + row_total(grad_result * normal)
            sums[1] = sums[1] + row_total(grad_result)
            sums[2] = sums[2] + row_total(grad_low.astype(WIDE))
            stats[0] = stats[0] + total(weight, feed_here)
            stats[1] = stats[1] + total(weight, result)
        for n in range(3):
            sums_ref[n : n + 1, :] += sums[n]
        for n in range(2):
            stat_ref[n : n + 1, :] += jnp.broadcast_to(stats[n], (1, 128))

    first_in.wait()
    work(0, True)
    second_in.wait()
    for copy in cot_in:
        copy.wait()

    def turn(index, carried):
        norm(index - 1)
        work(index, False)
        for copy in tile_copies(index - 1):
            copy.start()
        return carried

    lax.fori_loop(1, rows // tile, turn, 0)
    norm(rows // tile - 1)
    for copy in tile_copies(rows // tile - 1):
        copy.start()
    results = []
    for slot in range(rows // length):
        for part in range(pieces):
            spot = pl.ds(slot * length + part * piece, piece)
            target = sent_ref.at[part - 1, slot] if part else own_ref.at[slot]
            sem = in_sems.at[2 + len(results)]
            results.append(pltpu.make_async_copy(result_s.at[spot, :], target, sem))
            results[-1].start()
    outer(act_s, grad_low_s, out_s, (down_ref,), out_sems, sum_s, pl.ds(rows - tile, tile))
    for copy in results:
        copy.wait()
    for index in range(rows // tile):
        for copy in tile_copies(index):
            copy.wait()


def gather_outer(sum_s, left_s, right_s, rows, columns):
    sum_s[columns, :] += tn(left_s[rows, columns], right_s[rows, :])


def outer(left_s, right_s, out_s, targets, sems, sum_s, rows):
    places = [
        ref.at[pl.ds(row, HIDDEN_STEP), :]
        for ref in targets
        for row in range(0, ref.shape[0], HIDDEN_STEP)
    ]
    copies = []
    for step, target in enumerate(places):
        spot = pl.ds(step * HIDDEN_STEP, HIDDEN_STEP)
        out_s[spot, :] = (sum_s[spot, :] + tn(left_s[rows, spot], right_s[rows, :])).astype(LOW)
        copies.append(pltpu.make_async_copy(out_s.at[spot, :], target, sems.at[step]))
        copies[-1].start()
    for copy in copies:
        copy.wait()


def feed_forward(place, mids, cot, got, marks, wu, bu, wd, vectors, *earlier):
    length, width = mids[0].shape
    rows = length * len(mids)
    pieces = len(got) + 1
    hidden = wu.shape[1]
    chunks = hidden // HIDDEN_STEP
    shapes = (
        jax.ShapeDtypeStruct((rows, hidden), LOW),
        jax.ShapeDtypeStruct((rows, width), LOW),
        jax.ShapeDtypeStruct((len(mids), length // pieces, width), LOW),
        jax.ShapeDtypeStruct((pieces - 1, len(mids), length // pieces, width), LOW),
        jax.ShapeDtypeStruct((rows, width), WIDE),
        jax.ShapeDtypeStruct((rows, width), LOW),
        jax.ShapeDtypeStruct((hidden, width), LOW),
        jax.ShapeDtypeStruct((8, width), WIDE),
        jax.ShapeDtypeStruct((8, 128), WIDE),
    )
    return pl.pallas_call(
        ignoring(functools.partial(feed_kernel, pieces=pieces), 8 + pieces, len(earlier)),
        out_shape=shapes,
        in_specs=[IN_SMEM] + [ANY] * 3 + [IN_VMEM] * 3 + [ANY] * (1 + pieces + len(earlier)),
        out_specs=(ANY,) * 7 + (IN_VMEM,) * 2,
        scratch_shapes=[
            pltpu.VMEM((rows, width), WIDE),
            pltpu.VMEM((rows, width), LOW),
            pltpu.VMEM((width, hidden), LOW),
            pltpu.VMEM((hidden, width), LOW),
            pltpu.VMEM((rows, hidden), LOW),
            pltpu.VMEM((rows, hidden), LOW),
            pltpu.VMEM((rows, width), LOW),
            pltpu.VMEM((rows, width), LOW),
            pltpu.VMEM((rows, width), WIDE),
            pltpu.VMEM((rows, width), LOW),
            pltpu.VMEM((hidden, width), LOW),
            pltpu.VMEM((TILE, width), WIDE),
            pltpu.VMEM((rows, 1), WIDE),
            pltpu.VMEM((hidden, width), WIDE),
            pltpu.SemaphoreType.DMA((2 + pieces * len(mids),)),
            pltpu.SemaphoreType.DMA((chunks,)),
            pltpu.SemaphoreType.DMA((chunks,)),
            pltpu.SemaphoreType.DMA((4, rows // TILE)),
            pltpu.SemaphoreType.DMA((chunks,)),
        ],
        compiler_params=pltpu.CompilerParams(vmem_limit_bytes=VMEM_LIMIT),
        cost_estimate=cost(),
        name="feed_forward",
    )(place, mids[0], mids[1], cot, marks, bu, vectors, wu, wd, *got, *earlier)


def feed_back_kernel(
    place_ref, grad_low_ref, grad_ref, slope_ref, norm0_ref, norm1_ref, low_ref, wu_ref, wd_ref,
    wo_ref, rstd0_ref, rstd1_ref, vectors_ref,
    grad_one_ref, attn_ref, ctx_ref, send_ref, keep_ref, up_sums_ref, sums_ref,
    grad_low_s, grad_s, slope_s, norm_s, low_s, wu_s, wd_s, wo_s, rstd_s, grad_one_s, attn_s,
    ctx_s, middle_s, sum_s, out_s,
    in_sems, slope_sems, up_sems, down_sems, tile_sems, ctx_sems, out_sems,
):
    length = norm0_ref.shape[0]
    rows, width = grad_low_ref.shape
    hidden = wu_ref.shape[1]
    half = hidden // 2
    chunks = hidden // HIDDEN_STEP
    tile = TILE
    mine = place_ref[0]

    def place_of(chunk):
        part, inside = divmod(chunk * HIDDEN_STEP, half)
        start = (mine if part else 1 - mine) * half + inside
        return pl.ds(pl.multiple_of(start, HIDDEN_STEP), HIDDEN_STEP)

    def own(chunk):
        return pl.ds(chunk * HIDDEN_STEP, HIDDEN_STEP)

    def spot_of(index):
        return pl.ds(pl.multiple_of(index * tile, tile), tile)

    slopes = [
        pltpu.make_async_copy(
            slope_ref.at[spot_of(i), place_of(c)],
            slope_s.at[spot_of(i), own(c)],
            slope_sems.at[chunks * i + c],
        )
        for i in range(rows // tile)
        for c in range(chunks)
    ]
    ups = [
        pltpu.make_async_copy(wu_ref.at[:, place_of(c)], wu_s.at[:, own(c)], up_sems.at[c])
        for c in range(chunks)
    ]
    downs = [
        pltpu.make_async_copy(wd_ref.at[place_of(c), :], wd_s.at[own(c), :], down_sems.at[c])
        for c in range(chunks)
    ]
    others = [
        pltpu.make_async_copy(a, b, in_sems.at[n])
        for n, (a, b) in enumerate(
            (
                (grad_low_ref, grad_low_s),
                (grad_ref, grad_s),
                (norm0_ref, norm_s.at[pl.ds(0, length)]),
                (norm1_ref, norm_s.at[pl.ds(length, length)]),
                (wo_ref, wo_s),
                (low_ref, low_s),
            )
        )
    ]
    others[0].start()
    downs[0].start()
    slopes[0].start()
    ups[0].start()
    for chunk in range(1, chunks):
        downs[chunk].start()
        slopes[chunk].start()
        ups[chunk].start()
    for copy in others[1:] + slopes[chunks:]:
        copy.start()
    rstd_s[pl.ds(0, length), :] = rstd0_ref[...]
    rstd_s[pl.ds(length, length), :] = rstd1_ref[...]
    sums_ref[...] = jnp.zeros_like(sums_ref)
    up_sums_ref[...] = jnp.zeros_like(up_sums_ref)
    sum_s[...] = jnp.zeros_like(sum_s)

    def tile_copies(index):
        spot = spot_of(index)
        pairs = ((grad_one_s, grad_one_ref), (attn_s, attn_ref))
        return [
            pltpu.make_async_copy(a.at[spot, :], b.at[spot, :], tile_sems.at[n, index])
            for n, (a, b) in enumerate(pairs)
        ]

    def inside(index, row, count=ROWS):
        return pl.ds(pl.multiple_of(index * tile + row, count), count)

    def work(index, opening):
        spot = spot_of(index)
        grad_low = grad_low_s[spot, :]

        def back(chunk):
            if opening:
                downs[chunk].wait()
            return nt(grad_low, wd_s[own(chunk), :])

        def forth(chunk, grad):
            if opening:
                ups[chunk].wait()
            more = nt(slope_s[spot, own(chunk)], wu_s[:, own(chunk)])
            return more if grad is None else grad + more

        before = pl.ds(pl.multiple_of((index - 1) * tile, tile), tile)
        ahead = back(0)
        grad_middle = None
        for chunk in range(chunks):
            if opening:
                slopes[chunk].wait()
            sums = jnp.zeros((8, HIDDEN_STEP), WIDE)
            for row in range(0, tile, ROWS):
                at = inside(index, row)
                slope = slope_s[at, own(chunk)].astype(WIDE)
                grad_hidden = (ahead[row : row + ROWS] * slope).astype(LOW)
                slope_s[at, own(chunk)] = grad_hidden
                sums = sums + jnp.sum(
                    grad_hidden.astype(WIDE).reshape(-1, 8, HIDDEN_STEP), axis=0
                )
            up_sums_ref[:, place_of(chunk)] += sums
            if chunk + 1 < chunks:
                ahead = back(chunk + 1)
            if chunk > 0:
                grad_middle = forth(chunk - 1, grad_middle)
            if not opening:
                gather_outer(sum_s, slope_s, low_s, before, own(chunk))
        middle_s[...] = forth(chunks - 1, grad_middle)

    def norm(index):
        gain = vector(vectors_ref, "gain_one")
        sums = [jnp.zeros((1, width), WIDE) for _ in range(3)]
        for row in range(0, tile, ROWS_NORM):
            at = inside(index, row, ROWS_NORM)
            grad = middle_s[row : row + ROWS_NORM, :] + grad_s[at, :]
            normal = norm_s[at, :].astype(WIDE)
            grad_one = norm_back(grad, normal, rstd_s[at, :], gain)
            grad_one_s[at, :] = grad_one
            attn = grad_one.astype(LOW)
            attn_s[at, :] = attn
            sums[0] = sums[0] + row_total(grad * normal)
            sums[1] = sums[1] + row_total(grad)
            sums[2] = sums[2] + row_total(attn.astype(WIDE))
        for n in range(3):
            sums_ref[n : n + 1, :] += sums[n]

    def project(index):
        spot = spot_of(index)
        turned = nt(wo_s[...], attn_s[spot, :]).astype(LOW)
        slot, inner = divmod(index * tile, length)
        ctx_s[slot, :, inner : inner + tile] = turned
        copy = pltpu.make_async_copy(
            ctx_s.at[slot, :, pl.ds(inner, tile)], ctx_ref.at[slot, :, pl.ds(inner, tile)],
            ctx_sems.at[index],
        )
        copy.start()
        return copy

    others[0].wait()
    work(0, True)
    for copy in slopes[chunks:] + others[1:]:
        copy.wait()

    def turn(index, carried):
        norm(index - 1)
        work(index, False)
        for copy in tile_copies(index - 1):
            copy.start()
        return carried

    lax.fori_loop(1, rows // tile, turn, 0)
    norm(rows // tile - 1)
    for copy in tile_copies(rows // tile - 1):
        copy.start()
    copies = [project(index) for index in range(rows // tile)]
    outer(
        slope_s, low_s, out_s, (send_ref, keep_ref), out_sems, sum_s,
        pl.ds(rows - tile, tile),
    )
    for copy in copies:
        copy.wait()
    for index in range(rows // tile):
        for copy in tile_copies(index):
            copy.wait()


def feed_back(place, grad_low, grad, slope, norms, rstds, mid_low, wu, wd, wo, vectors, *earlier):
    rows, width = grad.shape
    length = norms[0].shape[0]
    hidden = wu.shape[1]
    chunks = hidden // HIDDEN_STEP
    part = jax.ShapeDtypeStruct((hidden // 2, width), LOW)
    shapes = (
        jax.ShapeDtypeStruct((rows, width), WIDE),
        jax.ShapeDtypeStruct((rows, width), LOW),
        jax.ShapeDtypeStruct((rows // length, width, length), LOW),
        part, part,
        jax.ShapeDtypeStruct((8, hidden), WIDE),
        jax.ShapeDtypeStruct((8, width), WIDE),
    )
    return pl.pallas_call(
        ignoring(feed_back_kernel, 13, len(earlier)),
        out_shape=shapes,
        in_specs=[IN_SMEM] + [ANY] * 9 + [IN_VMEM] * 3 + [ANY] * len(earlier),
        out_specs=(ANY,) * 5 + (IN_VMEM,) * 2,
        scratch_shapes=[
            pltpu.VMEM((rows, width), LOW),
            pltpu.VMEM((rows, width), WIDE),
            pltpu.VMEM((rows, hidden), LOW),
            pltpu.VMEM((rows, width), LOW),
            pltpu.VMEM((rows, width), LOW),
            pltpu.VMEM((width, hidden), LOW),
            pltpu.VMEM((hidden, width), LOW),
            pltpu.VMEM((width, width), LOW),
            pltpu.VMEM((rows, 1), WIDE),
            pltpu.VMEM((rows, width), WIDE),
            pltpu.VMEM((rows, width), LOW),
            pltpu.VMEM((rows // length, width, length), LOW),
            pltpu.VMEM((TILE, width), WIDE),
            pltpu.VMEM((hidden, width), WIDE),
            pltpu.VMEM((hidden, width), LOW),
            pltpu.SemaphoreType.DMA((6,)),
            pltpu.SemaphoreType.DMA((chunks * rows // TILE,)),
            pltpu.SemaphoreType.DMA((chunks,)),
            pltpu.SemaphoreType.DMA((chunks,)),
            pltpu.SemaphoreType.DMA((2, rows // TILE)),
            pltpu.SemaphoreType.DMA((rows // TILE,)),
            pltpu.SemaphoreType.DMA((chunks,)),
        ],
        compiler_params=pltpu.CompilerParams(vmem_limit_bytes=VMEM_LIMIT),
        cost_estimate=cost(),
        name="feed_back",
    )(
        place, grad_low, grad, slope, norms[0], norms[1], mid_low, wu, wd, wo, rstds[0], rstds[1],
        vectors, *earlier,
    )


def attend_back_kernel(
    place_ref, seg_ref, mark_ref, lse_ref, q_ref, k_ref, v_ref, ctx_ref, grad_ctx_ref, grad_one_ref, wq_ref,
    wk_ref, wv_ref,
    dq_ref, dk_ref, dv_ref, own_ref, sent_ref, sums_ref,
    q_s, k_s, v_s, ctx_s, grad_ctx_s, grad_one_s, wq_s, wk_s, wv_s, bias_s, score_s, pull_s,
    chance_s, grad_s, in_sems,
):
    length, model = q_ref.shape
    slot = place_ref[0]
    heads = model // HEAD_DIM
    width = 2 * HEAD_DIM
    loads = [
        pltpu.make_async_copy(a, b, in_sems.at[n])
        for n, (a, b) in enumerate(
            (
                (k_ref, k_s), (q_ref, q_s), (v_ref, v_s), (grad_ctx_ref.at[slot], grad_ctx_s),
                (ctx_ref, ctx_s), (wq_ref, wq_s), (wk_ref, wk_s), (wv_ref, wv_s),
                (grad_one_ref.at[pl.ds(pl.multiple_of(slot * length, length), length), :], grad_one_s),
            )
        )
    ]
    for load in loads:
        load.start()
    mark_col = column(mark_ref[pl.ds(slot, 1), :])
    fill_bias(bias_s, seg_ref[pl.ds(slot, 1), :].astype(WIDE), mark_col)

    def lanes(head):
        return pl.ds(head // 2 * width, width)

    def rows_of(head):
        return pl.ds(head * HEAD_DIM, HEAD_DIM)

    def products(head):
        score_s[head % 2] = nt(k_s[:, lanes(head)] * lane_half(head % 2), q_s[:, lanes(head)])
        values = v_s[:, lanes(head)] * lane_half(head % 2)
        pull_s[head % 2] = nn(values, grad_ctx_s[lanes(head), :])

    def soften(head):
        score, pull = score_s.at[head % 2], pull_s.at[head % 2]
        chance, grad = chance_s.at[head % 2], grad_s.at[head % 2]
        shared = grad_ctx_s[rows_of(head), :].astype(WIDE) * ctx_s[rows_of(head), :].astype(WIDE)
        delta = jnp.sum(shared, axis=0, keepdims=True)
        lse = lse_ref[head : head + 1, :]
        for row in range(0, length, ROWS):
            at = slice(row, row + ROWS)
            block = jnp.exp(score[at, :] + bias_s[at, :] - lse)
            chance[at, :] = block.astype(LOW)
            grad[at, :] = (block * (pull[at, :] - delta)).astype(LOW)

    def combine(head, turned):
        part_v = nt(chance_s[head % 2], grad_ctx_s[lanes(head), :])
        part_k = nn(grad_s[head % 2], q_s[:, lanes(head)])
        part = turned[head % 2 * HEAD_DIM : (head % 2 + 1) * HEAD_DIM]
        return part_v, part_k, nn(part, grad_s[head % 2])

    def keep(head, one, two):
        first = lax.broadcasted_iota(jnp.int32, one[0].shape, 1) < HEAD_DIM
        dv_ref[:, lanes(head)] = jnp.where(first, one[0], two[0]).astype(LOW)
        dk_ref[:, lanes(head)] = jnp.where(first, one[1], two[1]).astype(LOW)
        dq_ref[:, lanes(head)] = jnp.concatenate([one[2], two[2]], axis=0).T.astype(LOW)

    for load in loads[:4]:
        load.wait()
    products(0)
    loads[4].wait()
    waiting = None
    found = []
    for head in range(heads):
        soften(head)
        if head % 2 == 0:
            turned = k_s[:, lanes(head)].T
        if len(found) == 2:
            keep(head - 2, *found)
            found = []
        if head + 1 < heads:
            products(head + 1)
        if waiting is not None:
            found.append(combine(*waiting))
        waiting = (head, turned)
    found.append(combine(*waiting))
    keep(heads - 1, *found)
    for load in loads[5:]:
        load.wait()
    piece = own_ref.shape[0]
    for rows, ref in ((pl.ds(0, piece), own_ref), (pl.ds(piece, length - piece), sent_ref)):
        grad = (
            grad_one_s[rows, :]
            + nt(dq_ref[rows, :], wq_s[...]) * SCORE_SCALE
            + nt(dk_ref[rows, :], wk_s[...])
            + nt(dv_ref[rows, :], wv_s[...])
        )
        ref[...] = grad.astype(ref.dtype)
    sums_ref[...] = jnp.concatenate(
        [
            row_total(dq_ref[...].astype(WIDE)) * SCORE_SCALE,
            row_total(dv_ref[...].astype(WIDE)),
            jnp.zeros((6, model), WIDE),
        ],
        axis=0,
    )


def attend_back(piece, place, q, k, v, ctx, grad_ctx, lse, segs, marks, grad_one, wq, wk, wv, *earlier):
    length, width = q.shape
    heads = width // HEAD_DIM
    shapes = (
        jax.ShapeDtypeStruct((length, width), LOW),
        jax.ShapeDtypeStruct((length, width), LOW),
        jax.ShapeDtypeStruct((length, width), LOW),
        jax.ShapeDtypeStruct((piece, width), WIDE),
        jax.ShapeDtypeStruct((length - piece, width), LOW),
        jax.ShapeDtypeStruct((8, width), WIDE),
    )
    tokens = pltpu.VMEM((length, width), LOW)
    turned = pltpu.VMEM((width, length), LOW)
    weight = pltpu.VMEM((width, width), LOW)
    return pl.pallas_call(
        ignoring(attend_back_kernel, 13, len(earlier)),
        out_shape=shapes,
        in_specs=[IN_SMEM] + [IN_VMEM] * 3 + [ANY] * (9 + len(earlier)),
        out_specs=(IN_VMEM,) * 6,
        scratch_shapes=[
            tokens, tokens, tokens, turned, turned, pltpu.VMEM((length, width), WIDE),
            weight, weight, weight,
            pltpu.VMEM((length, length), WIDE),
            pltpu.VMEM((2, length, length), WIDE),
            pltpu.VMEM((2, length, length), WIDE),
            pltpu.VMEM((2, length, length), LOW),
            pltpu.VMEM((2, length, length), LOW),
            pltpu.SemaphoreType.DMA((9,)),
        ],
        compiler_params=pltpu.CompilerParams(vmem_limit_bytes=VMEM_LIMIT),
        cost_estimate=cost(),
        name="attend_back",
    )(place, segs, marks, lse, q, k, v, ctx, grad_ctx, grad_one, wq, wk, wv, *earlier)


def square_kernel(
    place_ref, x0_ref, x1_ref, dq0_ref, dq1_ref, dk0_ref, dk1_ref, dv0_ref, dv1_ref, ctx0_ref,
    ctx1_ref, attn_ref, send0_ref, send1_ref, keep0_ref, keep1_ref, x_s, dq_s, dk_s, dv_s, ctx_s, attn_s, out_s, in_sems,
    out_sems,
):
    length, width = x0_ref.shape
    first, second = pl.ds(0, length), pl.ds(length, length)
    loads = []
    for a, b in (
        (x0_ref, x_s.at[first]), (x1_ref, x_s.at[second]), (dv0_ref, dv_s.at[first]),
        (dv1_ref, dv_s.at[second]), (dq0_ref, dq_s.at[first]), (dq1_ref, dq_s.at[second]),
        (ctx0_ref, ctx_s.at[:, first]), (ctx1_ref, ctx_s.at[:, second]), (attn_ref, attn_s),
        (dk0_ref, dk_s.at[first]), (dk1_ref, dk_s.at[second]),
    ):
        loads.append(pltpu.make_async_copy(a, b, in_sems.at[len(loads)]))
        loads[-1].start()
    mine = place_ref[0] == 0
    x = x_s[...]
    step = 256
    copies = []

    def place(part, columns, low, high):
        for n, kept in enumerate((False, True)):
            spot = pl.ds((n * 2 + part) * width, width)
            out_s[spot, columns] = jnp.where(mine == kept, low, high).astype(LOW)

    def flush(part):
        for n, ref in enumerate(((send0_ref, send1_ref)[part], (keep0_ref, keep1_ref)[part])):
            spot = pl.ds((n * 2 + part) * width, width)
            copies.append(
                pltpu.make_async_copy(out_s.at[spot, :], ref, out_sems.at[len(copies)])
            )
            copies[-1].start()

    for load in loads[:6]:
        load.wait()
    x = x_s[...]
    for start in range(0, width, step):
        columns = pl.ds(start, step)
        place(0, columns, tn(x, dq_s[:, columns]) * SCORE_SCALE, tn(x, dv_s[:, columns]))
    flush(0)
    for load in loads[6:]:
        load.wait()
    for start in range(0, width, step):
        columns = pl.ds(start, step)
        place(1, columns, tn(x, dk_s[:, columns]), nn(ctx_s[...], attn_s[:, columns]))
    flush(1)
    for copy in copies:
        copy.wait()


def square_grads(place, xs, dqs, dks, dvs, ctxs, attn, *earlier):
    length, width = xs[0].shape
    rows = length * len(xs)
    tokens = pltpu.VMEM((rows, width), LOW)
    out = jax.ShapeDtypeStruct((width, width), LOW)
    return pl.pallas_call(
        ignoring(square_kernel, 12, len(earlier)),
        out_shape=(out,) * 4,
        in_specs=[IN_SMEM] + [ANY] * (11 + len(earlier)),
        out_specs=(ANY,) * 4,
        scratch_shapes=[
            tokens, tokens, tokens, tokens, pltpu.VMEM((width, rows), LOW), tokens,
            pltpu.VMEM((4 * width, width), LOW),
            pltpu.SemaphoreType.DMA((11,)),
            pltpu.SemaphoreType.DMA((4,)),
        ],
        compiler_params=pltpu.CompilerParams(vmem_limit_bytes=VMEM_LIMIT),
        cost_estimate=cost(),
        name="square_grads",
    )(place, *xs, *dqs, *dks, *dvs, *ctxs, attn, *earlier)


def pick_kernel(place_ref, value_ref, out_ref):
    out_ref[...] = value_ref[...]


def pick(value, place, rows, *earlier):
    shape = (rows,) + value.shape[1:]
    return pl.pallas_call(
        ignoring(pick_kernel, 2, len(earlier)),
        out_shape=jax.ShapeDtypeStruct(shape, value.dtype),
        grid_spec=pltpu.PrefetchScalarGridSpec(
            num_scalar_prefetch=1,
            grid=(1,),
            in_specs=[pl.BlockSpec(shape, lambda i, p: (p[0], 0, 0))] + [ANY] * len(earlier),
            out_specs=pl.BlockSpec(shape, lambda i, p: (0, 0, 0)),
        ),
        cost_estimate=cost(),
        name="pick",
    )(place.astype(jnp.int32).reshape(1), value, *earlier)


def other_pieces(value, slot, slots, *earlier):
    count = lax.axis_size("seq")
    me = lax.axis_index("seq")
    found = []
    for shift in range(1, count):
        place = (me + shift) % count * slots + slot
        if value.ndim == 2:
            block = lax.dynamic_index_in_dim(value, place, 0, keepdims=False)
        else:
            block = pick(value, place, 1, *earlier)[0]
        pairs = [(source, (source + shift) % count) for source in range(count)]
        found.append(lax.ppermute(block, "seq", pairs))
    return found


def send_back(parts, shifts=None):
    count = lax.axis_size("seq")
    found = []
    for shift in range(1, count):
        pairs = [(source, (source + shift) % count) for source in range(count)]
        found.append(lax.ppermute(parts[shift - 1], "seq", pairs))
    return found


def join_kernel(me_ref, *refs, slots, count):
    out_ref = refs[-1]
    index = pl.program_id(0)
    shift = lax.rem(index // slots - me_ref[0] + count, count)
    for n in range(count):
        for slot in range(slots):

            @pl.when((shift == n) & (lax.rem(index, slots) == slot))
            def _(n=n, slot=slot):
                value = refs[n][slot] if len(refs) == count + 1 else refs[n * slots + slot][...]
                out_ref[0] = value.astype(out_ref.dtype)


def join(me, arrays, slots, count, *earlier):
    piece, width = arrays[0].shape[-2:]
    return pl.pallas_call(
        ignoring(
            functools.partial(join_kernel, slots=slots, count=count), 1 + len(arrays), len(earlier)
        ),
        out_shape=jax.ShapeDtypeStruct((slots * count, piece, width), arrays[0].dtype),
        grid_spec=pltpu.PrefetchScalarGridSpec(
            num_scalar_prefetch=1,
            grid=(slots * count,),
            in_specs=[whole(array.shape) for array in arrays] + [ANY] * len(earlier),
            out_specs=pl.BlockSpec((1, piece, width), lambda i, p: (i, 0, 0)),
        ),
        compiler_params=pltpu.CompilerParams(vmem_limit_bytes=SMALL_LIMIT),
        cost_estimate=cost(),
        name="join",
    )(me, *arrays, *earlier)


def collect_kernel(sums0_ref, sums1_ref, one_ref, two_ref, up_ref, *refs):
    stat_refs, mark_ref, out_ref = refs[:-2], refs[-2], refs[-1]
    width = out_ref.shape[1]
    out_ref[0:2, :] = sums0_ref[0:2, :] + sums1_ref[0:2, :]
    out_ref[2:5, :] = one_ref[0:3, :]
    out_ref[5:8, :] = two_ref[0:3, :]
    lane = lax.broadcasted_iota(jnp.int32, (1, width), 1)
    known = (mark_ref[...] >= 0).astype(WIDE)
    tokens = jnp.sum(jnp.sum(known, axis=1, keepdims=True), axis=0, keepdims=True)
    fed = stat_refs[2]
    stats = (
        stat_refs[0][0:1, 0:1] + stat_refs[1][0:1, 0:1],
        stat_refs[0][1:2, 0:1] + stat_refs[1][1:2, 0:1],
        fed[0:1, 0:1], fed[1:2, 0:1], tokens,
    )
    row = jnp.zeros((1, width), WIDE)
    for n, stat in enumerate(stats):
        row = jnp.where(lane == n, stat, row)
    out_ref[8:9, :] = row
    parts = up_ref.shape[1] // width
    for n in range(parts):
        out_ref[9 + n : 10 + n, :] = row_total(up_ref[:, n * width : (n + 1) * width])
    left = out_ref.shape[0] - 9 - parts
    out_ref[9 + parts :, :] = jnp.zeros((left, width), WIDE)


def collect(sums, sums_one, sums_two, up_sums, stats, marks, *earlier):
    width = sums_one.shape[1]
    rows = 9 + up_sums.shape[1] // width
    args = (*sums, sums_one, sums_two, up_sums, *stats, marks)
    return pl.pallas_call(
        ignoring(collect_kernel, len(args), len(earlier)),
        out_shape=jax.ShapeDtypeStruct((rows + (-rows) % 8, width), WIDE),
        in_specs=[IN_VMEM] * len(args) + [ANY] * len(earlier),
        out_specs=IN_VMEM,
        compiler_params=pltpu.CompilerParams(vmem_limit_bytes=VMEM_LIMIT),
        cost_estimate=cost(),
        name="collect",
    )(*args, *earlier)


def swap(value, axis, bit):
    count = lax.axis_size(axis)
    return lax.ppermute(value, axis, [(source, source ^ bit) for source in range(count)])


def bit_of(axis, bit):
    return (lax.axis_index(axis) // bit) % 2


CORE = ("dp", 1)
HALVINGS = 5
STEP_ROWS = 16


def chip_axes():
    dp, seq = lax.axis_size("dp"), lax.axis_size("seq")
    along_dp = [("dp", 2**i) for i in range(1, dp.bit_length() - 1)]
    along_seq = [("seq", 2**i) for i in range(seq.bit_length() - 1)]
    return along_dp[0], along_seq[0], along_dp[1], along_dp[2:] + along_seq[1:]


class Chain:
    def __init__(self, bits):
        self.last = ()
        self.bits = bits

    def run(self, function, *args):
        out = function(*args, *self.last)
        arrays = out if isinstance(out, (tuple, list)) else (out,)
        self.last = (min(arrays, key=lambda array: array.size),)
        return out

    def round(self, *tasks):
        outs = list(self.run(round_call, self.bits, [task[:-1] for task in tasks]))
        for task in tasks:
            count = 2 if task[0] == "halve" else 1
            task[-1](*[outs.pop(0) for _ in range(count)])


def add_rows(first, first_start, second, second_start, out, rows):
    def step(index, carried):
        spots = [
            pl.ds(pl.multiple_of(start + index * STEP_ROWS, STEP_ROWS), STEP_ROWS)
            for start in (first_start, second_start, 0)
        ]
        both = first[spots[0], :].astype(WIDE) + second[spots[1], :].astype(WIDE)
        out[spots[2], :] = both.astype(LOW)
        return carried

    lax.fori_loop(0, rows // STEP_ROWS, step, 0)


def round_kernel(bits_ref, *refs, plan, inputs):
    outs = list(refs[inputs:])
    for kind, places, meta in plan:
        first, second = refs[places[0]], refs[places[1]]
        if kind == "halve":
            rows, offset, which = meta
            mine = bits_ref[which]
            for bit in (1 - mine, mine):
                start = offset + bit * rows
                add_rows(first, start, second, start, outs.pop(0), rows)
        elif kind == "add":
            add_rows(first, meta, second, 0, outs.pop(0), second.shape[0])
        elif kind == "merge":
            rows = first.shape[0]
            out = outs.pop(0)
            out[:rows, :] = first[...]
            out[rows:, :] = second[...]
        else:
            outs.pop(0)[...] = first[...]


def round_call(bits, tasks, *earlier):
    arrays, plan, shapes = [], [], []
    for kind, pair, meta in tasks:
        places = []
        for array in pair:
            known = [n for n, other in enumerate(arrays) if other is array]
            if not known:
                arrays.append(array)
            places.append(known[0] if known else len(arrays) - 1)
        plan.append((kind, places, meta))
        rows, width = pair[0].shape
        if kind == "halve":
            shapes += [jax.ShapeDtypeStruct((meta[0], width), LOW)] * 2
        elif kind == "merge":
            shapes.append(jax.ShapeDtypeStruct((2 * rows, width), LOW))
        elif kind == "add":
            shapes.append(jax.ShapeDtypeStruct(pair[1].shape, LOW))
        else:
            shapes.append(jax.ShapeDtypeStruct((rows, width), pair[0].dtype))
    return pl.pallas_call(
        ignoring(
            functools.partial(round_kernel, plan=plan, inputs=len(arrays)),
            1 + len(arrays),
            len(earlier),
        ),
        out_shape=tuple(shapes),
        in_specs=[IN_SMEM] + [IN_VMEM] * len(arrays) + [ANY] * len(earlier),
        out_specs=(IN_VMEM,) * len(shapes),
        compiler_params=pltpu.CompilerParams(vmem_limit_bytes=SMALL_LIMIT),
        cost_estimate=cost(),
        name="round",
    )(bits, *arrays, *earlier)


class Reduction:
    def __init__(self, kept, got, order, names, back):
        self.order, self.names, self.back = order, names, back
        self.first, self.second = kept, got
        self.count, self.offset = kept.shape[0], 0
        self.step = 1

    def send(self):
        axis = self.order[self.step]
        rows, offset = self.count // 2, self.offset

        def found(sent, kept):
            self.first, self.second = kept, swap(sent, *axis)
            self.count, self.offset = rows, 0
            self.step += 1

        meta = (rows, offset, self.names.index(axis))
        return "halve", (self.first, self.second), meta, found

    def share(self):
        def found(share):
            self.have = share
            if self.step < len(self.order):
                self.first, self.second = share, swap(share, *self.order[self.step])
                self.step += 1
            else:
                self.step = len(self.back) - 1
                self.got = swap(share, *self.back[self.step])

        return "add", (self.first, self.second), 0, found

    def more_shares(self):
        return len(self.order) - HALVINGS

    def gather(self):
        def found(merged):
            self.step -= 1
            self.have, self.got = merged, swap(merged, *self.back[self.step])

        return "merge", (self.have, self.got), None, found

    def copy(self):
        def found(got):
            self.got = got

        return "copy", (self.got, self.got), None, found

    def hold(self, nothing):
        self.got = self.got + nothing

    def halves(self):
        return [self.have, self.got, swap(self.have, *CORE), swap(self.got, *CORE)]

    def moves(self):
        chips = [axis for axis in self.order[:HALVINGS] if axis != CORE]
        return [len(chips) - 1 - chips.index(axis) for axis in self.back]

    def place(self):
        place = 0
        for axis in self.back:
            place = place * 2 + bit_of(*axis)
        return place.astype(jnp.int32)


def attach_kernel(small_ref, part_ref, out_ref):
    rows = small_ref.shape[0]
    out_ref[:rows, :] = small_ref[...].astype(LOW)
    out_ref[rows:, :] = part_ref[...]


def attach(small, part, *earlier):
    rows = small.shape[0] + part.shape[0]
    return pl.pallas_call(
        ignoring(attach_kernel, 2, len(earlier)),
        out_shape=jax.ShapeDtypeStruct((rows, part.shape[1]), LOW),
        in_specs=[IN_VMEM] * 2 + [ANY] * len(earlier),
        out_specs=IN_VMEM,
        compiler_params=pltpu.CompilerParams(vmem_limit_bytes=SMALL_LIMIT),
        cost_estimate=cost(),
        name="attach",
    )(small, part, *earlier)


def detach_kernel(value_ref, small_ref, out_ref):
    count, rows, _ = value_ref.shape
    few = small_ref.shape[0]
    each = rows - few
    total_here = jnp.zeros(small_ref.shape, WIDE)
    for n in range(count):
        total_here = total_here + value_ref[n, :few, :].astype(WIDE)
        out_ref[n * each : (n + 1) * each, :] = value_ref[n, few:, :].astype(WIDE)

    @pl.when(pl.program_id(0) == 0)
    def _():
        small_ref[...] = jnp.zeros_like(small_ref)

    small_ref[...] += total_here


def detach(value, few, *earlier):
    count, rows, width = value.shape
    steps = 8
    return pl.pallas_call(
        ignoring(detach_kernel, 1, len(earlier)),
        out_shape=(
            jax.ShapeDtypeStruct((few, width), WIDE),
            jax.ShapeDtypeStruct((count * (rows - few), width), WIDE),
        ),
        grid=(steps,),
        in_specs=[pl.BlockSpec((count // steps, rows, width), lambda t: (t, 0, 0))]
        + [ANY] * len(earlier),
        out_specs=(
            whole((few, width)),
            pl.BlockSpec((count // steps * (rows - few), width), lambda t: (t, 0)),
        ),
        compiler_params=pltpu.CompilerParams(
            vmem_limit_bytes=SMALL_LIMIT, dimension_semantics=("arbitrary",)
        ),
        cost_estimate=cost(),
        name="detach",
    )(value, *earlier)


def spot_of_block(index, moves):
    spot = 0
    for move in moves:
        spot = spot * 2 + ((index >> move) & 1)
    return spot


def turn_kernel(place_ref, own, other, *refs, moves):
    out_ref = refs[-1]
    blocks = 1 << (HALVINGS - 2)
    block = own.shape[0] // blocks
    count = out_ref.shape[1] // block
    step = pl.program_id(0)
    mine = place_ref[0] == step // 2
    start = (place_ref[2] * 2 + lax.rem(step, 2)) * count
    found = []
    for j in range(count):
        spot = spot_of_block(start + j, moves) ^ place_ref[1]
        at = pl.ds(pl.multiple_of(lax.rem(spot, blocks) * block, block), block)
        found.append(jnp.where(mine, own[at, :], other[at, :]).astype(WIDE))
    out_ref[...] = jnp.concatenate(found, axis=0).T


def turn(place, own, other, moves, into, *earlier):
    rows, width = own.shape
    into = () if into is None else (into,)
    return pl.pallas_call(
        ignoring(functools.partial(turn_kernel, moves=moves), 3 + len(into), len(earlier)),
        out_shape=jax.ShapeDtypeStruct((width, 4 * rows), WIDE),
        grid_spec=pltpu.PrefetchScalarGridSpec(
            num_scalar_prefetch=1,
            grid=(4,),
            in_specs=[whole(own.shape)] * 2 + [ANY] * (len(into) + len(earlier)),
            out_specs=pl.BlockSpec((width, rows // 2), lambda t, p: (0, t // 2 * 4 + p[2] * 2 + lax.rem(t, 2))),
        ),
        input_output_aliases={3: 0} if into else {},
        compiler_params=pltpu.CompilerParams(vmem_limit_bytes=SMALL_LIMIT),
        cost_estimate=cost(3 * 10**10),
        name="turn",
    )(place, own, other, *into, *earlier)


def gate_kernel(*refs):
    pass


def gate(values, *earlier):
    count = len(values)
    return pl.pallas_call(
        gate_kernel,
        out_shape=tuple(jax.ShapeDtypeStruct(value.shape, value.dtype) for value in values),
        in_specs=[ANY] * (count + len(earlier)),
        out_specs=(ANY,) * count,
        input_output_aliases={n: n for n in range(count)},
        compiler_params=pltpu.CompilerParams(vmem_limit_bytes=SMALL_LIMIT),
        cost_estimate=cost(),
        name="gate",
    )(*values, *earlier)


def finish_kernel(
    place_ref, near_own, far_own, near_other, far_other, low_ref, high_ref, *, moves
):
    blocks = 1 << (HALVINGS - 2)
    block = near_own.shape[0] // blocks
    step = pl.program_id(0)
    rows = low_ref.shape[0]
    first = place_ref[0] == 0
    for j in range(rows // block):
        spot = spot_of_block(step * (rows // block) + j, moves) ^ place_ref[1]
        at = pl.ds(pl.multiple_of(lax.rem(spot, blocks) * block, block), block)
        here = pl.ds(j * block, block)
        own = jnp.where(spot < blocks, near_own[at, :], far_own[at, :]).astype(WIDE)
        other = jnp.where(spot < blocks, near_other[at, :], far_other[at, :]).astype(WIDE)
        low_ref[here, :] = jnp.where(first, own, other)
        high_ref[here, :] = jnp.where(first, other, own)


def finish(place, arrays, moves, *earlier):
    rows, width = arrays[0].shape
    shape = jax.ShapeDtypeStruct((2 * rows, width), WIDE)
    tile = rows // 2
    return pl.pallas_call(
        ignoring(functools.partial(finish_kernel, moves=moves), 5, len(earlier)),
        out_shape=(shape, shape),
        grid_spec=pltpu.PrefetchScalarGridSpec(
            num_scalar_prefetch=1,
            grid=(4,),
            in_specs=[whole(array.shape) for array in arrays] + [ANY] * len(earlier),
            out_specs=(
                pl.BlockSpec((tile, width), lambda t, p: (t, 0)),
                pl.BlockSpec((tile, width), lambda t, p: (t, 0)),
            ),
        ),
        compiler_params=pltpu.CompilerParams(vmem_limit_bytes=SMALL_LIMIT),
        cost_estimate=cost(3 * 10**10),
        name="finish",
    )(place, *arrays, *earlier)


def on_device(
    inputs, cotangent, w_query, b_query, w_key, w_value, b_value, w_out, b_out, gain_one,
    shift_one, w_up, b_up, w_down, b_down, gain_two, shift_two, live_counts, valid_mask, segments,
):
    seqs, piece, width = inputs.shape
    count = lax.axis_size("seq")
    me = lax.axis_index("seq").astype(jnp.int32)
    slots = seqs // count
    length = piece * count
    x, y, z, rest = chip_axes()
    names = [CORE, x, y, z] + rest
    bits = jnp.stack([bit_of(*axis).astype(jnp.int32) for axis in names])
    core = bits[0]
    chain = Chain(bits)
    chain.last = (segments,)
    base = (me * slots).reshape(1)

    x_got = []
    for slot in range(slots):
        x_got.append(other_pieces(inputs, slot, slots, *(x_got[-1][-1:] if x_got else ())))
    vectors = jnp.concatenate(
        [v.reshape(1, -1) for v in (
            b_query, b_value, b_out, gain_one, shift_one, b_down, gain_two, shift_two
        )]
    ).astype(WIDE)
    bias_up = b_up.astype(WIDE).reshape(1, -1)
    live = (jnp.arange(seqs) < live_counts[0]).astype(jnp.int32)
    code = segments * 2 + valid_mask * live[:, None]
    codes = jnp.stack(
        [
            jnp.concatenate(
                [lax.dynamic_index_in_dim(code, base[0] + slot, 0, keepdims=False)]
                + other_pieces(code, slot, slots)
            )
            for slot in range(slots)
        ]
    )
    segs = codes // 2
    weight = codes % 2
    marks = jnp.where(weight > 0, segs, -1)

    forward = []
    for slot in range(slots):
        forward.append(
            chain.run(
                attend, jnp.stack([base[0], jnp.int32(slot)]), inputs, x_got[slot], segs, marks, vectors, w_query, w_key,
                w_value, w_out,
            )
        )
    cot_got = []
    for shift in range(1, count):
        block = pick(cotangent, (me + shift) % count, slots, x_got[-1][-1], forward[0][9])
        pairs = [(source, (source + shift) % count) for source in range(count)]
        cot_got.append(lax.ppermute(block, "seq", pairs))
    slope, mid_low, result_own, result_sent, grad_h2, grad_feed, down, sums_two, stat_two = (
        chain.run(
            feed_forward, base, [each[6] for each in forward], cotangent, cot_got, marks, w_up,
            bias_up, w_down, vectors,
        )
    )
    everywhere = ("dp", "seq")
    down = lax.psum_scatter(down, everywhere, scatter_dimension=0, tiled=True)
    result_got = send_back([result_sent[n] for n in range(count - 1)])
    grad_h1, grad_attn, grad_ctx, up_sent, up_kept, up_sums, sums_one = chain.run(
        feed_back, bits[0:1], grad_feed, grad_h2, slope,
        [each[7] for each in forward], [each[8] for each in forward], mid_low, w_up, w_down,
        w_out, vectors,
    )
    (up_sent,) = chain.run(gate, (up_sent,), *result_got)
    last = rest[0]
    up = Reduction(
        up_kept, swap(up_sent, *CORE), [CORE, y, z, x] + rest, names, [y, x, z, last]
    )
    backward, grad_got = [], []
    for slot in range(slots):
        if slot == 1:
            chain.round(up.send())
        q, k, v, _, ctx, lse = forward[slot][:6]
        backward.append(
            chain.run(
                attend_back, piece, jnp.full((1,), slot, jnp.int32), q, k, v, ctx, grad_ctx, lse,
                segs, marks, grad_h1, w_query, w_key, w_value,
            )
        )
        sent = backward[-1][4]
        grad_got.append(
            send_back([sent[n * piece : (n + 1) * piece] for n in range(count - 1)])
        )
    small = chain.run(
        collect, [each[5] for each in backward], sums_one, sums_two, up_sums,
        [each[9] for each in forward] + [stat_two], marks,
    )
    square_sent0, square_sent1, square_kept0, square_kept1 = chain.run(
        square_grads, bits[0:1], [each[3] for each in forward],
        *([each[i] for each in backward] for i in range(3)), [each[4] for each in forward],
        grad_attn,
    )
    squares = [
        Reduction(square_kept0, swap(square_sent0, *CORE), [CORE, x, y, z] + rest, names, [x, z, y, last]),
        Reduction(square_kept1, swap(square_sent1, *CORE), [CORE, y, z, x] + rest, names, [z, x, y, last]),
    ]

    def each_square(step):
        return [step(square) for square in squares]

    chain.round(up.send())
    chain.round(*each_square(Reduction.send))
    chain.round(*each_square(Reduction.send), up.send())
    few = small.shape[0]
    down = chain.run(attach, small, down)
    down = lax.all_gather(down, everywhere, axis=0, tiled=False)
    chain.round(*each_square(Reduction.send), up.send())
    for _ in range(up.more_shares()):
        chain.round(up.share())
    chain.round(*each_square(Reduction.send), up.share())
    result_out = chain.run(join, me.reshape(1), [result_own] + result_got, slots, count)
    for _ in range(up.more_shares()):
        chain.round(*each_square(Reduction.share))
    chain.round(*each_square(Reduction.share), up.gather())
    grad_arrays = [each[3] for each in backward]
    for n in range(count - 1):
        grad_arrays += [got[n] for got in grad_got]
    grad_out = chain.run(join, me.reshape(1), grad_arrays, slots, count)
    chain.round(*each_square(Reduction.gather), up.gather())
    chain.round(*each_square(Reduction.gather))
    chain.round(*each_square(Reduction.gather), up.gather())
    small, grad_w_down = chain.run(detach, down, few)
    for square in squares:
        square.hold(small[few - 1, 0].astype(LOW))
    finished = [
        chain.run(finish, jnp.stack([core, square.place()]), square.halves(), square.moves())
        for square in squares
    ]
    up_place = [core, up.place()]
    up_near = up.have, swap(up.have, *CORE)
    grad_w_up = chain.run(
        turn, jnp.stack(up_place + [bits[2]]), *up_near, up.moves(), None
    )
    far = up.got
    grad_w_up = turn(
        jnp.stack(up_place + [1 - bits[2]]), far, swap(far, *CORE), up.moves(), grad_w_up
    )
    rms_values = jnp.sqrt(small[8, :4] / (width * small[8, 4]))
    hidden = w_up.shape[1]
    return (
        result_out,
        grad_out,
        finished[0][0],
        small[0],
        finished[1][0],
        finished[0][1],
        small[1],
        finished[1][1],
        small[4],
        small[2],
        small[3],
        grad_w_up,
        small[9 : 9 + hidden // width].reshape(-1),
        grad_w_down,
        small[7],
        small[5],
        small[6],
        rms_values,
    )


def solution(mesh):
    split = P("dp", "seq", None)
    pair = P("dp", "seq")
    return jax.shard_map(
        on_device,
        mesh=mesh,
        in_specs=(split, split) + (P(),) * 15 + (P("dp"), pair, pair),
        out_specs=(split, split) + (P(),) * 16,
        check_vma=False,
    )
```
